128 devices in a mesh: coarse: 8 (over z, y_hi), fine: 8 (over y_lo, x), lev: 2 (over core).
Axes of the slice: x: 4, y: 4 (y_hi: 2, y_lo: 2; y = y_hi * 2 + y_lo), z: 4, core: 2. Of those that a mesh axis runs over, the one named last changes fastest.
Arguments:
- ens_pert: bfloat16 [80, 48, 768, 128], P(('fine', 'lev'), None, 'coarse'), may hold values from -6 to 6
- ens_control: float32 [80, 32, 768, 128], P(('fine', 'lev'), None, 'coarse'), may hold values from -6 to 6
- eigen_modes: float32 [48, 32], replicated, may hold values from -1 to 1
- mode_count: int32 [768, 128], P('coarse'), may hold values from 16 to 32
- row_index: int32 [1536], P(('coarse', 'fine')), may hold values from 0 to 766, as said below
- row_weight: float32 [1536], P(('coarse', 'fine')), may hold values from 0 to 1
- col_index: int32 [256], replicated, may hold values from 0 to 126, as said below
- col_weight: float32 [256], replicated, may hold values from 0 to 1
- static_control: float32 [48, 1536, 256], P('lev', ('coarse', 'fine')), may hold values from -6 to 6
- static_std: float32 [48], P('lev'), may hold values from 0.5 to 2
- diffusivity: float32 [1536, 256], P(('coarse', 'fine')), may hold values from 0.12 to 0.24
- land_mask: int32 [1536, 256], P(('coarse', 'fine')), may hold values 0 or 1
- innovation: float32 [48, 1536, 256], P('lev', ('coarse', 'fine')), may hold values from -6 to 6
Outputs:
- increment: float32 [48, 1536, 256], P('lev', ('coarse', 'fine'))
- grad_static: float32 [48, 1536, 256], P('lev', ('coarse', 'fine'))
- grad_ens: float32 [80, 32, 768, 128], P(('fine', 'lev'), None, 'coarse')
The draws below stay inside these ranges and needn't reach their ends.
Inputs may be any that keep to these rules, and one draw needn't show every extreme that they name: `row_index`: for control row i the value is i // 2 or i // 2 - 1, kept within the range. `col_index`: for control column j the value is j // 2 or j // 2 - 1, kept within the range.
All inputs are finite; a program needn't handle non-finite values. No bound on the sum of `land_mask` on one device may be relied on, other than what follows from the above.
Results may differ from the reference program's by a relative error of at most 0.0003.
Values sent between devices are 32-bit elements; how exact they have to be, the bound alone decides.
A program may use at most 128 MiB of HBM per device.

```python
import math
import jax
import jax.numpy as jnp
from jax import lax

MEMBERS = 80
LEV = 48
MODES = 32
NSWEEP = 3
NXF = 256
NXC = 128
NYF = 1536
NYC = 768


def draw_row_index(key, part):
    key = jax.random.fold_in(key, 11)
    rows_all = jnp.arange(NYF, dtype=jnp.int32)
    offset = jax.random.randint(key, (NYF,), 0, 2, dtype=jnp.int32)
    return jnp.clip(rows_all // 2 - offset, 0, NYC - 2).astype(jnp.int32)


def draw_col_index(key, part):
    key = jax.random.fold_in(key, 23)
    cols_all = jnp.arange(NXF, dtype=jnp.int32)
    offset = jax.random.randint(key, (NXF,), 0, 2, dtype=jnp.int32)
    return jnp.clip(cols_all // 2 - offset, 0, NXC - 2).astype(jnp.int32)


def plant(entries, stream_key, smallest, largest):
    shape = entries.shape
    index_at = [jax.random.randint(jax.random.fold_in(stream_key, axis), (), 0, shape[axis]) for axis in range(len(shape))]
    entries = entries.at[tuple(index_at)].set(smallest)
    longest = shape.index(max(shape))
    index_at[longest] = (index_at[longest] + 1) % shape[longest]
    return entries.at[tuple(index_at)].set(largest)


def block_scale(key, shape, shards, smallest, high):
    loudness = 1.0
    for axis_at, shards_of in shards:
        draws = jax.random.uniform(jax.random.fold_in(jax.random.fold_in(key, 6), axis_at), (shards_of,), jnp.float32, smallest / len(shards), high / len(shards))
        loudness = loudness * jnp.repeat(jnp.exp(draws), shape[axis_at] // shards_of).reshape((-1,) + (1,) * (len(shape) - 1 - axis_at))
    return loudness


def noise(rng, shape, deviation, limit, split=(), kind=jnp.bfloat16):
    level = block_scale(rng, shape, split, -0.22, 0.18) if split else 1.0
    values = jax.random.normal(rng, shape, jnp.float32) * deviation * level
    return jnp.minimum(jnp.maximum(values, -limit), limit).astype(kind)


def setup_inputs(seed: int = 0) -> dict:
    key_list = jax.random.split(jax.random.key(seed), 14)
    return {
        "ens_pert": noise(key_list[0], (MEMBERS, LEV, NYC, NXC), 1.0, 6.0, ((0, 16), (2, 8))),
        "ens_control": noise(key_list[1], (MEMBERS, MODES, NYC, NXC), 1.0, 6.0, ((0, 16), (2, 8)), jnp.float32),
        "eigen_modes": noise(key_list[2], (LEV, MODES), MODES ** -0.5, 1.0, (), jnp.float32),
        "mode_count": plant(jax.random.randint(key_list[3], (NYC, NXC), MODES // 2, MODES + 1), jax.random.fold_in(key_list[3], 1), MODES // 2, MODES).astype(jnp.int32),
        "row_index": draw_row_index(jax.random.fold_in(key_list[13], 71), 0),
        "row_weight": jnp.clip(1.0 * jax.random.uniform(key_list[5], (NYF,), jnp.float32) ** block_scale(key_list[5], (NYF,), ((0, 64),), -0.2, 0.2), 0.0, 1.0),
        "col_index": draw_col_index(jax.random.fold_in(key_list[13], 71), 0),
        "col_weight": jnp.clip(jax.random.uniform(key_list[7], (NXF,), jnp.float32, 0.0, 1.0), 0.0, 1.0),
        "static_control": noise(key_list[8], (LEV, NYF, NXF), 1.0, 6.0, ((0, 2), (1, 64)), jnp.float32),
        "static_std": jnp.clip(jnp.exp(math.log(2.0) - 1.3862944 * jax.random.uniform(key_list[9], (LEV,), jnp.float32) ** block_scale(key_list[9], (LEV,), ((0, 2),), -0.2, 0.2)), 0.5, 2.0),
        "diffusivity": jnp.clip(0.12 + 0.12 * jax.random.uniform(key_list[10], (NYF, NXF), jnp.float32) ** block_scale(key_list[10], (NYF, NXF), ((0, 64),), -0.2, 0.2), 0.12, 0.24),
        "land_mask": plant((jax.random.randint(key_list[11], (NYF, NXF), 0, 2) < 1).astype(jnp.int32), jax.random.fold_in(key_list[11], 1), 0, 1),
        "innovation": noise(key_list[12], (LEV, NYF, NXF), 1.0, 6.0, ((0, 2), (1, 64)), jnp.float32),
    }


def stencil_matrix(offsets, fractions, extent):
    positions = jnp.arange(extent).astype(jnp.int32)[None, :]
    lower = offsets.astype(jnp.int32)[:, None]
    share = fractions[:, None]
    return (1.0 - share) * (positions == lower).astype(share.dtype) + share * (positions == lower + 1).astype(share.dtype)

def face_coefficients(spread_ext, coast_ext):
    row_faces = jnp.sqrt(spread_ext[:-1] * spread_ext[1:]) * (1.0 - 0.5 * jnp.abs(coast_ext[:-1] - coast_ext[1:]))
    next_spread = jnp.roll(spread_ext, -1, -1)
    next_coast = jnp.roll(coast_ext, -1, -1)
    interior = (jnp.arange(spread_ext.shape[-1]) < spread_ext.shape[-1] - 1).astype(spread_ext.dtype)
    col_faces = jnp.sqrt(spread_ext * next_spread) * (1.0 - 0.5 * jnp.abs(coast_ext - next_coast)) * interior
    return (row_faces, col_faces)

def diffuse_once(field, row_faces, col_faces):
    row_flux = row_faces[None] * (field[:, 1:] - field[:, :-1])
    change_rows = jnp.pad(row_flux, ((0, 0), (0, 1), (0, 0))) - jnp.pad(row_flux, ((0, 0), (1, 0), (0, 0)))
    col_flux = col_faces[None] * (jnp.roll(field, -1, -1) - field)
    change_cols = col_flux - jnp.roll(col_flux, 1, -1)
    return field + change_rows + change_cols

def reference(ens_pert, ens_control, eigen_modes, mode_count, row_index, row_weight, col_index, col_weight, static_control, static_std, diffusivity, land_mask, innovation):
    highest = lax.Precision.HIGHEST
    member_scale = 1.0 / math.sqrt(MEMBERS - 1)
    mode_keep = (jnp.arange(MODES).astype(jnp.int32)[:, None, None] < mode_count[None]).astype(ens_control.dtype)

    def add_member(running, member_pair):
        member_pert, member_amp = member_pair
        level_amp = jnp.einsum('lm,mrc->lrc', eigen_modes, member_amp * mode_keep, precision=highest)
        return (running + member_pert.astype(level_amp.dtype) * level_amp, None)
    coarse_inc, _ = lax.scan(add_member, jnp.zeros((LEV, NYC, NXC), ens_control.dtype), (ens_pert, ens_control))
    coarse_inc = coarse_inc * member_scale
    row_mat = stencil_matrix(row_index, row_weight, NYC)
    col_mat = stencil_matrix(col_index, col_weight, NXC)
    partial_rows = jnp.einsum('ir,lrc->lic', row_mat, coarse_inc, precision=highest)
    ens_fine = jnp.einsum('lic,jc->lij', partial_rows, col_mat, precision=highest)
    row_faces, col_faces = face_coefficients(diffusivity, land_mask.astype(diffusivity.dtype))

    def smooth(field):
        for sweep_step in range(NSWEEP):
            field = diffuse_once(field, row_faces, col_faces)
        return field
    static_sigma = static_std[:, None, None]
    increment = ens_fine + static_sigma * smooth(static_control)
    misfit = increment - innovation
    grad_static = static_control + smooth(static_sigma * misfit)
    back_cols = jnp.einsum('lij,jc->lic', misfit, col_mat, precision=highest)
    coarse_grad = jnp.einsum('ir,lic->lrc', row_mat, back_cols, precision=highest)

    def member_grad(member_pair):
        member_pert, member_amp = member_pair
        projected = jnp.einsum('lm,lrc->mrc', eigen_modes, member_pert.astype(coarse_grad.dtype) * coarse_grad, precision=highest)
        return member_amp + mode_keep * projected * member_scale
    grad_ens = lax.map(member_grad, (ens_pert, ens_control))
    return (increment, grad_static, grad_ens)
```

```python
import functools
import math

import jax
import jax.numpy as jnp
from jax import lax
from jax.experimental import pallas as pl
from jax.experimental.pallas import tpu as pltpu
from jax.sharding import PartitionSpec as P

MEMBERS = 80
NSWEEP = 3
HALO = 3
EDGE = 4
GROWN = 32
ROWS = 12
XROWS = 7
YROWS = ROWS - XROWS
YA = YROWS // 2
BLOCK = 16
F32 = jnp.float32
BF16 = jnp.bfloat16


def halves(value):
    hi = value.astype(BF16)
    return hi, (value - hi.astype(F32)).astype(BF16)


def stacked(value):
    hi, lo = halves(value)
    return jnp.concatenate([hi, hi, lo], axis=0)


def split_modes(matrix):
    hi = lax.reduce_precision(matrix, 8, 7)
    return jnp.concatenate([hi, matrix - hi, hi], axis=1).astype(BF16)


def forward_kernel(lhs_ref, count_ref, amp_ref, pert_ref, out_ref, wide_ref):
    members, modes = amp_ref.shape[:2]
    levels = pert_ref.shape[1]
    wide_ref[...] = pert_ref[...].reshape(wide_ref.shape).astype(F32)
    amps = amp_ref.reshape(members * modes * BLOCK, 128)
    lhs = lhs_ref[...]
    mode = lax.broadcasted_iota(jnp.int32, (modes, 128), 0)

    def row_pair(step, carry):
        first = step * 2
        keep = [mode < count_ref[pl.ds(first + h, 1), :] for h in range(2)]
        total = [jnp.zeros((levels, 128), F32) for _ in range(2)]
        for k in range(members):
            rhs = []
            for h in range(2):
                amp = amps[pl.ds(k * modes * BLOCK + first + h, modes, stride=BLOCK), :]
                rhs.append(stacked(jnp.where(keep[h], amp, 0.0)))
            level_amp = jnp.dot(lhs, jnp.concatenate(rhs, axis=1), preferred_element_type=F32)
            for h in range(2):
                pert = wide_ref[pl.ds(k * levels * BLOCK + first + h, levels, stride=BLOCK), :]
                total[h] = total[h] + pert * level_amp[:, h * 128 : (h + 1) * 128]
        for h in range(2):
            out_ref[0, first + h] = total[h][: levels // 2]
            out_ref[1, first + h] = total[h][levels // 2 :]
        return carry

    lax.fori_loop(0, BLOCK // 2, row_pair, 0, unroll=4)


def backward_kernel(lhs_ref, count_ref, amp_ref, pert_ref, grad_ref, out_ref, wide_ref):
    members, modes = amp_ref.shape[:2]
    levels = pert_ref.shape[1]
    wide_ref[...] = pert_ref[...].reshape(wide_ref.shape).astype(F32)
    amps = amp_ref.reshape(members * modes * BLOCK, 128)
    outs = out_ref.reshape(members * modes * BLOCK, 128)
    lhs = lhs_ref[...]
    mode = lax.broadcasted_iota(jnp.int32, (modes, 128), 0)

    def row_pair(step, carry):
        first = step * 2
        keep = [mode < count_ref[pl.ds(first + h, 1), :] for h in range(2)]
        grad = [
            jnp.concatenate([grad_ref[0, first + h], grad_ref[1, first + h]], axis=0)
            for h in range(2)
        ]
        for k in range(members):
            rhs = []
            for h in range(2):
                pert = wide_ref[pl.ds(k * levels * BLOCK + first + h, levels, stride=BLOCK), :]
                rhs.append(stacked(pert * grad[h]))
            proj = jnp.dot(lhs, jnp.concatenate(rhs, axis=1), preferred_element_type=F32)
            for h in range(2):
                at = pl.ds(k * modes * BLOCK + first + h, modes, stride=BLOCK)
                outs[at, :] = amps[at, :] + jnp.where(
                    keep[h], proj[:, h * 128 : (h + 1) * 128], 0.0
                )
        return carry

    lax.fori_loop(0, BLOCK // 2, row_pair, 0, unroll=4)


def forward(lhs, count, amp, pert):
    members, modes, rows, cols = amp.shape
    levels = pert.shape[1]
    return pl.pallas_call(
        forward_kernel,
        grid=(rows // BLOCK,),
        in_specs=[
            pl.BlockSpec(lhs.shape, lambda i: (0, 0)),
            pl.BlockSpec((BLOCK, cols), lambda i: (i, 0)),
            pl.BlockSpec((members, modes, BLOCK, cols), lambda i: (0, 0, i, 0)),
            pl.BlockSpec((members, levels, BLOCK, cols), lambda i: (0, 0, i, 0)),
        ],
        out_specs=pl.BlockSpec((2, BLOCK, levels // 2, cols), lambda i: (0, i, 0, 0)),
        out_shape=jax.ShapeDtypeStruct((2, rows, levels // 2, cols), F32),
        scratch_shapes=[pltpu.VMEM((members * levels * BLOCK, cols), F32)],
        compiler_params=pltpu.CompilerParams(vmem_limit_bytes=50 << 20),
        name="forward_modes",
    )(lhs, count, amp, pert)


def backward(lhs, count, amp, pert, grad):
    members, modes, rows, cols = amp.shape
    levels = pert.shape[1]
    return pl.pallas_call(
        backward_kernel,
        grid=(rows // BLOCK,),
        in_specs=[
            pl.BlockSpec(lhs.shape, lambda i: (0, 0)),
            pl.BlockSpec((BLOCK, cols), lambda i: (i, 0)),
            pl.BlockSpec((members, modes, BLOCK, cols), lambda i: (0, 0, i, 0)),
            pl.BlockSpec((members, levels, BLOCK, cols), lambda i: (0, 0, i, 0)),
            pl.BlockSpec((2, BLOCK, levels // 2, cols), lambda i: (0, i, 0, 0)),
        ],
        out_specs=pl.BlockSpec((members, modes, BLOCK, cols), lambda i: (0, 0, i, 0)),
        out_shape=jax.ShapeDtypeStruct(amp.shape, F32),
        scratch_shapes=[pltpu.VMEM((members * levels * BLOCK, cols), F32)],
        compiler_params=pltpu.CompilerParams(vmem_limit_bytes=50 << 20),
        name="backward_modes",
    )(lhs, count, amp, pert, grad)


def exchange_kernel(
    sizes,
    tile_ref,
    control_ref,
    innov_ref,
    std_ref,
    spread_ref,
    land_ref,
    row_index_ref,
    row_weight_ref,
    col_index_ref,
    col_weight_ref,
    inc_ref,
    grad_ref,
    coarse_ref,
    sums,
    core_in,
    x1_in,
    x2_in,
    x3_in,
    x4_in,
    yq_in,
    y1_in,
    y2_in,
    y3_in,
    window,
    field_a,
    field_b,
    misfit,
    cells,
    row_faces,
    col_faces,
    weights,
    sigma,
    col_mat,
    back,
    shares,
    planes_in,
    planes_out,
    send_sem,
    recv_sem,
    copy_sem,
    plane_sem,
):
    coarse_count, fine_count, rows_all = sizes
    xs = fine_count // 2
    coarse = lax.axis_index("coarse")
    fine = lax.axis_index("fine")
    lev = lax.axis_index("lev")
    x = lax.rem(fine, xs)
    y = fine // xs
    right, left, across = lax.rem(x + 1, xs), lax.rem(x + xs - 1, xs), lax.rem(x + 2, xs)
    other_y = 1 - y
    serial = coarse * fine_count + fine
    count = coarse_count * fine_count
    after, before = lax.rem(serial + 1, count), lax.rem(serial + count - 1, count)
    first_row = serial * 2 * ROWS

    to_core = (coarse, fine, 1 - lev)
    to_right = (coarse, y * xs + right, lev)
    to_left = (coarse, y * xs + left, lev)
    to_y = (coarse, other_y * xs + x, lev)
    to_after = (after // fine_count, lax.rem(after, fine_count), lev)
    to_before = (before // fine_count, lax.rem(before, fine_count), lev)

    barrier = pltpu.get_barrier_semaphore()
    for device in (to_core, to_right, to_left, to_y, to_after, to_before):
        pl.semaphore_signal(barrier, inc=1, device_id=device, device_id_type=pl.DeviceIdType.MESH)

    numbers = iter(range(100))
    sent = []

    def remote(src, dst, device):
        number = next(numbers)
        copy = pltpu.make_async_remote_copy(
            src_ref=src,
            dst_ref=dst,
            send_sem=send_sem.at[number],
            recv_sem=recv_sem.at[number],
            device_id=device,
            device_id_type=pl.DeviceIdType.MESH,
        )
        copy.start()
        sent.append(copy)
        return copy

    def share(ry, rx):
        return (ry * xs + rx) * ROWS

    lev_dev = control_ref.shape[0]
    own = 2 * ROWS
    lanes = [pl.ds(0, 128), pl.ds(128, 128)]
    plane_in = [
        [
            pltpu.make_async_copy(
                ref.at[:, :, lanes[side]],
                planes_in.at[number, side],
                plane_sem.at[2 * number + side],
            )
            for side in range(2)
        ]
        for number, ref in enumerate((control_ref, innov_ref))
    ]
    for pair in plane_in:
        for copy in pair:
            copy.start()

    def planes(ref, number, side):
        return ref.at[number, side].reshape(lev_dev * own, 128)

    for copy in plane_in[0]:
        copy.wait()

    def load_rows(i, carry):
        for side in range(2):
            field_a[EDGE + i, :, lanes[side]] = planes(planes_in, 0, side)[
                pl.ds(i, lev_dev, stride=own), :
            ]
        sub = lax.broadcasted_iota(jnp.int32, (8, 256), 0)
        weight = jnp.full((8, 256), row_weight_ref[i], F32)
        index = jnp.full((8, 256), row_index_ref[i], jnp.int32)
        upper = (index == (first_row + i) // 2).astype(F32)
        spread = jnp.broadcast_to(spread_ref[pl.ds(i, 1), :], (8, 256))
        land = jnp.broadcast_to(land_ref[pl.ds(i, 1), :], (8, 256)).astype(F32)
        cells[EDGE + i] = jnp.where(
            sub == 0, spread, jnp.where(sub == 1, land, jnp.where(sub == 2, weight, upper))
        )
        return carry

    lax.fori_loop(0, own, load_rows, 0, unroll=4)
    for ref in (cells, misfit):
        ref[0] = jnp.zeros(ref.shape[1:], F32)
        ref[GROWN - 1] = jnp.zeros(ref.shape[1:], F32)
    for row in (1, GROWN - 2):
        field_b[row] = jnp.zeros(field_b.shape[1:], F32)
    for lev_at in range(lev_dev):
        sigma[lev_at : lev_at + 1, :] = jnp.full((1, 256), std_ref[lev_at], F32)

    pl.semaphore_wait(barrier, 6)

    orders = [across, right, left, x]
    keep_own = pltpu.make_async_copy(tile_ref.at[lev], sums, copy_sem)
    keep_own.start()
    core_sends = []
    for rx in orders:
        for ry in (0, 1):
            rows = pl.ds(share(ry, rx), ROWS)
            core_sends.append(
                remote(tile_ref.at[1 - lev, rows], core_in.at[rows], to_core)
            )
    top, bottom = pl.ds(EDGE, HALO), pl.ds(EDGE + own - HALO, HALO)
    low, high = pl.ds(EDGE - HALO, HALO), pl.ds(EDGE + own, HALO)
    halo_sends = [
        remote(ref.at[src], ref.at[dst], device)
        for ref in (cells, field_a)
        for src, dst, device in ((top, high, to_before), (bottom, low, to_after))
    ]
    keep_own.wait()

    def x_rows(ry, rx):
        return pl.ds(share(ry, rx), XROWS)

    def y_rows(rx, part, ry=None):
        start = share(y if ry is None else ry, rx) + XROWS
        return {
            "all": pl.ds(start, YROWS),
            "a": pl.ds(start, YA),
            "b": pl.ds(start + YA, YROWS - YA),
        }[part]

    def add(rows, *terms):
        total = sums[rows]
        for term in terms:
            total = total + term[...]
        sums[rows] = total

    quarter = {}
    for number, rx in enumerate(orders):
        for ry in (0, 1):
            core_sends[2 * number + ry].wait_recv()
            rows = pl.ds(share(ry, rx), ROWS)
            add(rows, core_in.at[rows])
        quarter[number] = remote(sums.at[y_rows(rx, "all", other_y)], yq_in.at[number], to_y)
        if number == 0:
            x1 = [
                remote(sums.at[x_rows(0, across)], x1_in.at[0], to_right),
                remote(sums.at[x_rows(1, across)], x1_in.at[1], to_left),
            ]
        if number == 1:
            x2_right = remote(sums.at[x_rows(1, right)], x2_in.at[0], to_right)
        if number == 2:
            x2_left = remote(sums.at[x_rows(0, left)], x2_in.at[1], to_left)

    for copy in halo_sends[:2]:
        copy.wait_recv()

    def coefficients(e, carry):
        here, there = cells[e], cells[e + 1]
        line = first_row - EDGE + e
        inside = (line >= 0) & (line < rows_all) & (e >= 1) & (e <= GROWN - 2)
        facing = (line >= 0) & (line + 1 < rows_all)
        inside = jnp.where(inside, 1.0, 0.0).astype(F32)
        facing = jnp.where(facing, 1.0, 0.0).astype(F32)
        lane = lax.broadcasted_iota(jnp.int32, (8, 256), 1)
        spread, land = (jnp.broadcast_to(here[j : j + 1], (8, 256)) for j in (0, 1))
        spread_next, land_next = (jnp.broadcast_to(there[j : j + 1], (8, 256)) for j in (0, 1))
        row_faces[e] = (
            jnp.sqrt(spread * spread_next) * (1.0 - 0.5 * jnp.abs(land - land_next)) * facing
        )
        spread_right, land_right = (pltpu.roll(v, 255, 1) for v in (spread, land))
        col_faces[e] = jnp.where(
            lane < 255,
            jnp.sqrt(spread * spread_right) * (1.0 - 0.5 * jnp.abs(land - land_right)),
            0.0,
        )
        weight, upper = (jnp.broadcast_to(here[j : j + 1, :128], (8, 128)) for j in (2, 3))
        upper_on = upper > 0.5
        weights[0, e] = jnp.where(upper_on, 0.0, 1.0 - weight) * inside
        weights[1, e] = jnp.where(upper_on, 1.0 - weight, weight) * inside
        weights[2, e] = jnp.where(upper_on, weight, 0.0) * inside
        return carry

    lax.fori_loop(0, GROWN - 1, coefficients, 0, unroll=4)
    for j in range(3):
        weights[j, GROWN - 1] = jnp.zeros((8, 128), F32)
    col = lax.broadcasted_iota(jnp.int32, (128, 256), 0)
    col_at, col_w = col_index_ref[...], col_weight_ref[...]
    matrix = jnp.where(col == col_at, 1.0 - col_w, jnp.where(col == col_at + 1, col_w, 0.0))
    hi, lo = halves(matrix)
    col_mat[0], col_mat[1] = hi, lo

    for rx_copy, rows, slot, device, x3_slot in (
        (x1[0], x_rows(0, right), 0, to_right, 0),
        (x1[1], x_rows(1, left), 1, to_left, 1),
    ):
        rx_copy.wait_recv()
        add(rows, x1_in.at[slot])
        if slot == 0:
            x3_right = remote(sums.at[rows], x3_in.at[0], device)
        else:
            x3_left = remote(sums.at[rows], x3_in.at[1], device)

    for number, rx in enumerate(orders):
        quarter[number].wait_recv()
        add(y_rows(rx, "all"), yq_in.at[number])
        if number == 0:
            y1 = [
                remote(sums.at[y_rows(rx, "a")], y1_in.at[0, pl.ds(0, YA)], to_right),
                remote(sums.at[y_rows(rx, "b")], y1_in.at[1], to_left),
            ]
        if number == 1:
            y2_right = remote(sums.at[y_rows(rx, "b")], y2_in.at[0], to_right)
        if number == 2:
            y2_left = remote(sums.at[y_rows(rx, "a")], y2_in.at[1, pl.ds(0, YA)], to_left)

    def sweep(src, dst):
        def rows_of_four(step, carry):
            e = EDGE - 2 + 4 * step
            down = row_faces[pl.ds(e - 1, 5)]
            side = col_faces[pl.ds(e, 4)]
            for tile in range(lev_dev // 8):
                at = pl.ds(8 * tile, 8)
                v = src[pl.ds(e - 1, 6), at, :]
                mid = v[1:5]
                flux = down * (v[1:] - v[:-1])
                cross = side * (pltpu.roll(mid, 255, 2) - mid)
                dst[pl.ds(e, 4), at, :] = (
                    mid + (flux[1:] - flux[:-1]) + (cross - pltpu.roll(cross, 1, 2))
                )
            return carry

        lax.fori_loop(0, 7, rows_of_four, 0)

    for copy in halo_sends[2:]:
        copy.wait_recv()
        copy.wait_send()
    sweep(field_a, field_b)

    for copy, slot in ((y1[0], 0), (y1[1], 1)):
        copy.wait_recv()
    a_rows, b_rows = y_rows(right, "a"), y_rows(left, "b")
    add(a_rows, y1_in.at[0, pl.ds(0, YA)])
    y3_right = remote(sums.at[a_rows], y3_in.at[0, pl.ds(0, YA)], to_right)
    add(b_rows, y1_in.at[1])
    y3_left = remote(sums.at[b_rows], y3_in.at[1], to_left)

    sweep(field_b, field_a)
    sweep(field_a, field_b)

    def static_part(i, carry):
        for side in range(2):
            cols = lanes[side]
            misfit[EDGE + i, :, cols] = (
                sigma[:, cols] * field_b[EDGE + i, :, cols]
                - planes(planes_in, 1, side)[pl.ds(i, lev_dev, stride=own), :]
            )
        return carry

    for copy in plane_in[1]:
        copy.wait()

    lax.fori_loop(0, own, static_part, 0, unroll=4)
    misfit_sends = [
        remote(misfit.at[top], misfit.at[high], to_before),
        remote(misfit.at[bottom], misfit.at[low], to_after),
    ]

    for copy in (x2_right, x2_left, x3_right, x3_left):
        copy.wait_recv()
    rows = x_rows(other_y, x)
    add(rows, x3_in.at[other_y], x2_in.at[y])
    x4 = remote(sums.at[rows], x4_in, to_y)
    add(x_rows(y, x), x3_in.at[y], x2_in.at[other_y])
    for copy in (y2_right, y2_left, y3_right, y3_left):
        copy.wait_recv()
    mine = share(y, x)
    window[pl.ds(HALO + XROWS, YA)] = (
        sums[y_rows(x, "a")] + y3_in[0, :YA] + y2_in[1, :YA]
    )
    window[pl.ds(HALO + XROWS + YA, YROWS - YA)] = sums[y_rows(x, "b")] + y3_in[1] + y2_in[0]
    window_after = remote(
        window.at[pl.ds(ROWS, HALO)], window.at[pl.ds(0, HALO)], to_after
    )
    x4.wait_recv()
    window[pl.ds(HALO, XROWS)] = sums[pl.ds(mine, XROWS)] + x4_in[...]
    window_before = remote(
        window.at[pl.ds(HALO, HALO)], window.at[pl.ds(HALO + ROWS, HALO)], to_before
    )
    for copy in misfit_sends + [window_after, window_before]:
        copy.wait_recv()
    for copy in misfit_sends:
        copy.wait_send()

    def dot_split(lhs, which):
        hi, lo = halves(lhs)
        c_hi, c_lo = col_mat[0], col_mat[1]
        dims = (((1,), (which,)), ((), ()))
        dot = functools.partial(lax.dot_general, dimension_numbers=dims, preferred_element_type=F32)
        return dot(hi, c_hi) + (dot(lo, c_hi) + dot(hi, c_lo))

    span = 8

    def interpolate(step, carry):
        e0 = step * span
        lines = []
        for pair in range(span // 2):
            t = step * (span // 2) + pair + 1
            w = [window[t + d].reshape(lev_dev // 8, 8, 128) for d in (-1, 0, 1)]
            for h in range(2):
                e = e0 + 2 * pair + h
                line = weights[0, e] * w[0] + weights[1, e] * w[1] + weights[2, e] * w[2]
                lines.append(line.reshape(lev_dev, 128))
        fine_part = dot_split(jnp.concatenate(lines, axis=0), 0)
        at = pl.ds(e0, span)
        total = misfit[at] + fine_part.reshape(span, lev_dev, 256)
        misfit[at] = total
        back[at] = dot_split(total.reshape(span * lev_dev, 256), 1).reshape(span, lev_dev, 128)
        return carry

    lax.fori_loop(0, GROWN // span, interpolate, 0)

    def adjoint(r, carry):
        e = 2 * r + 2
        total = jnp.zeros((lev_dev // 8, 8, 128), F32)
        for j in range(6):
            total = total + weights[2 - j // 2, e + j] * back[e + j].reshape(lev_dev // 8, 8, 128)
        shares[lev, mine + r] = total.reshape(lev_dev, 128)
        return carry

    lax.fori_loop(0, ROWS, adjoint, 0, unroll=4)

    def to_all(rows, device):
        return remote(shares.at[lev, rows], shares.at[lev, rows], device)

    def x_part(ry, rx):
        return pl.ds(share(ry, rx), XROWS)

    pair_first = to_all(x_part(y, x), to_y)
    ring_y = [to_all(y_rows(x, "all"), to_right), to_all(y_rows(x, "all"), to_left)]
    ring_own = [to_all(x_part(y, x), to_right), to_all(x_part(y, x), to_left)]
    core = [to_all(pl.ds(mine, ROWS), to_core)]
    pair_y = [to_all(y_rows(x, "all"), to_y)]

    def scaled(e, carry):
        at = pl.ds(e * 2 + 1, 2)
        field_a[at] = sigma[...] * misfit[at]
        return carry

    lax.fori_loop(0, (GROWN - 2) // 2, scaled, 0)

    pair_first.wait_recv()
    ring_other = [to_all(x_part(other_y, x), to_right), to_all(x_part(other_y, x), to_left)]
    core.append(to_all(x_part(other_y, x), to_core))
    for copy in ring_y:
        copy.wait_recv()
    on_y = [
        to_all(y_rows(left, "a"), to_right),
        to_all(y_rows(right, "b"), to_left),
    ]
    for rx in (left, right):
        pair_y.append(to_all(y_rows(rx, "all"), to_y))
        core.append(to_all(y_rows(rx, "all"), to_core))

    sweep(field_a, field_b)

    for copy in ring_own + ring_other:
        copy.wait_recv()
    on_x = [to_all(x_part(0, left), to_right), to_all(x_part(1, right), to_left)]
    for rx in (left, right):
        for ry in (0, 1):
            core.append(to_all(x_part(ry, rx), to_core))
    for copy in on_y:
        copy.wait_recv()
    pair_y.append(to_all(y_rows(across, "all"), to_y))
    core.append(to_all(y_rows(across, "all"), to_core))

    sweep(field_b, field_a)
    sweep(field_a, field_b)

    def finish(i, carry):
        at = pl.ds(i, lev_dev, stride=own)
        for side in range(2):
            for number, value in ((0, field_b), (1, misfit)):
                planes(planes_out, number, side)[at, :] = (
                    planes(planes_in, number, side)[at, :] + value[EDGE + i, :, lanes[side]]
                )
        return carry

    lax.fori_loop(0, own, finish, 0, unroll=4)
    plane_out = [
        pltpu.make_async_copy(
            planes_out.at[number, side],
            ref.at[:, :, lanes[side]],
            plane_sem.at[2 * number + side],
        )
        for number, ref in enumerate((grad_ref, inc_ref))
        for side in range(2)
    ]
    for copy in plane_out:
        copy.start()

    for copy in on_x:
        copy.wait_recv()
    for ry in (0, 1):
        core.append(to_all(x_part(ry, across), to_core))
    for rx, copy in zip((x, left, right, across), pair_y):
        copy.wait_recv()
        core.append(to_all(y_rows(rx, "all", other_y), to_core))
    for copy in core:
        copy.wait_recv()
    out = pltpu.make_async_copy(shares, coarse_ref, copy_sem)
    out.start()
    waited = halo_sends[2:] + misfit_sends
    for copy in sent:
        if not any(copy is done for done in waited):
            copy.wait_send()
    out.wait()
    for copy in plane_out:
        copy.wait()


def exchange(sizes, tile, control, innov, std, spread, land, row_index, row_weight, col_index, col_weight):
    lev_dev, own, cols_fine = control.shape
    vmem = pl.BlockSpec(memory_space=pltpu.VMEM)
    smem = pl.BlockSpec(memory_space=pltpu.SMEM)
    anywhere = pl.BlockSpec(memory_space=pl.ANY)
    cell = (lev_dev, 128)
    row = (lev_dev, cols_fine)
    return pl.pallas_call(
        functools.partial(exchange_kernel, sizes),
        in_specs=[anywhere, anywhere, anywhere, smem, vmem, vmem, smem, smem, vmem, vmem],
        out_specs=[anywhere, anywhere, anywhere],
        out_shape=[
            jax.ShapeDtypeStruct(control.shape, F32),
            jax.ShapeDtypeStruct(control.shape, F32),
            jax.ShapeDtypeStruct(tile.shape, F32),
        ],
        scratch_shapes=[
            pltpu.VMEM(tile.shape[1:], F32),
            pltpu.VMEM(tile.shape[1:], F32),
            pltpu.VMEM((2, XROWS) + cell, F32),
            pltpu.VMEM((2, XROWS) + cell, F32),
            pltpu.VMEM((2, XROWS) + cell, F32),
            pltpu.VMEM((XROWS,) + cell, F32),
            pltpu.VMEM((4, YROWS) + cell, F32),
            pltpu.VMEM((2, YROWS - YA) + cell, F32),
            pltpu.VMEM((2, YROWS - YA) + cell, F32),
            pltpu.VMEM((2, YROWS - YA) + cell, F32),
            pltpu.VMEM((ROWS + 2 * HALO,) + cell, F32),
            pltpu.VMEM((GROWN,) + row, F32),
            pltpu.VMEM((GROWN,) + row, F32),
            pltpu.VMEM((GROWN,) + row, F32),
            pltpu.VMEM((GROWN, 8, cols_fine), F32),
            pltpu.VMEM((GROWN, 8, cols_fine), F32),
            pltpu.VMEM((GROWN, 8, cols_fine), F32),
            pltpu.VMEM((3, GROWN, 8, 128), F32),
            pltpu.VMEM(row, F32),
            pltpu.VMEM((2, 128, cols_fine), BF16),
            pltpu.VMEM((GROWN,) + cell, F32),
            pltpu.VMEM(tile.shape, F32),
            pltpu.VMEM((2, 2, lev_dev, own, 128), F32),
            pltpu.VMEM((2, 2, lev_dev, own, 128), F32),
            pltpu.SemaphoreType.DMA((80,)),
            pltpu.SemaphoreType.DMA((80,)),
            pltpu.SemaphoreType.DMA,
            pltpu.SemaphoreType.DMA((4,)),
        ],
        compiler_params=pltpu.CompilerParams(
            collective_id=0, has_side_effects=True, vmem_limit_bytes=50 << 20
        ),
        name="exchange",
    )(
        tile,
        control,
        innov,
        std,
        spread,
        land,
        row_index,
        row_weight,
        col_index.reshape(1, cols_fine),
        col_weight.reshape(1, cols_fine),
    )


def local(
    ens_pert,
    ens_control,
    eigen_modes,
    mode_count,
    row_index,
    row_weight,
    col_index,
    col_weight,
    static_control,
    static_std,
    diffusivity,
    land_mask,
    innovation,
):
    sizes = (
        lax.axis_size("coarse"),
        lax.axis_size("fine"),
        lax.axis_size("coarse") * lax.axis_size("fine") * row_index.shape[0],
    )
    scaled = eigen_modes * (1.0 / math.sqrt(MEMBERS - 1))
    tile = forward(split_modes(scaled), mode_count, ens_control, ens_pert)
    increment, grad_static, coarse_grad = exchange(
        sizes,
        tile,
        static_control,
        innovation,
        static_std,
        diffusivity,
        land_mask,
        row_index,
        row_weight,
        col_index,
        col_weight,
    )
    grad_ens = backward(split_modes(scaled.T), mode_count, ens_control, ens_pert, coarse_grad)
    return increment, grad_static, grad_ens


def solution(mesh):
    in_specs = (
        P(("fine", "lev"), None, "coarse", None),
        P(("fine", "lev"), None, "coarse", None),
        P(),
        P("coarse", None),
        P(("coarse", "fine")),
        P(("coarse", "fine")),
        P(),
        P(),
        P("lev", ("coarse", "fine"), None),
        P("lev"),
        P(("coarse", "fine"), None),
        P(("coarse", "fine"), None),
        P("lev", ("coarse", "fine"), None),
    )
    out_specs = (
        P("lev", ("coarse", "fine"), None),
        P("lev", ("coarse", "fine"), None),
        P(("fine", "lev"), None, "coarse", None),
    )
    return jax.shard_map(local, mesh=mesh, in_specs=in_specs, out_specs=out_specs, check_vma=False)
```

```python
import functools
import math

import jax
import jax.numpy as jnp
from jax import lax
from jax.experimental import pallas as pl
from jax.experimental.pallas import tpu as pltpu
from jax.sharding import PartitionSpec as P

MEMBERS = 80
NSWEEP = 3
HALO = 3
EDGE = 4
GROWN = 32
ROWS = 12
XROWS = 6
YROWS = ROWS - XROWS
YA = YROWS // 2
PITCH = 104
PIECE = 24
F32 = jnp.float32
BF16 = jnp.bfloat16


def halves(value):
    hi = value.astype(BF16)
    return hi, (value - hi.astype(F32)).astype(BF16)


def stacked(value):
    hi, lo = halves(value)
    return jnp.concatenate([hi, hi, lo], axis=0)


def split_modes(matrix):
    hi = lax.reduce_precision(matrix, 8, 7)
    return jnp.concatenate([hi, matrix - hi, hi], axis=1).astype(BF16)


def backward_kernel(
    lhs_ref,
    count_ref,
    amp_ref,
    wide_ref,
    grad_ref,
    planes_ref,
    out_ref,
    grad_static_ref,
    inc_ref,
    result,
    out_sem,
    plane_sem,
):
    members, modes = amp_ref.shape[:2]
    levels = wide_ref.shape[1]
    rows = out_ref.shape[2]
    plane_out = [
        pltpu.make_async_copy(
            planes_ref.at[number, side],
            ref.at[:, :, pl.ds(128 * side, 128)],
            plane_sem.at[2 * number + side],
        )
        for number, ref in enumerate((grad_static_ref, inc_ref))
        for side in range(2)
    ]
    for copy in plane_out:
        copy.start()
    amps = amp_ref.reshape(members * modes * PITCH, 128)
    perts = wide_ref.reshape(members * levels * PITCH, 128)
    outs = result.reshape(members * modes * PITCH, 128)
    lhs = lhs_ref[...]
    mode = lax.broadcasted_iota(jnp.int32, (modes, 128), 0)
    pieces = []
    for piece in range(rows // PIECE):

        def row_pair(step, carry):
            first = piece * PIECE + step * 2
            keep = [mode < count_ref[pl.ds(first + h, 1), :] for h in range(2)]
            grad = [
                jnp.concatenate([grad_ref[0, first + h], grad_ref[1, first + h]], axis=0)
                for h in range(2)
            ]
            for k in range(members):
                rhs = []
                for h in range(2):
                    pert = perts[pl.ds(k * levels * PITCH + first + h, levels, stride=PITCH), :]
                    rhs.append(stacked(pert * grad[h]))
                proj = jnp.dot(lhs, jnp.concatenate(rhs, axis=1), preferred_element_type=F32)
                for h in range(2):
                    at = pl.ds(k * modes * PITCH + first + h, modes, stride=PITCH)
                    outs[at, :] = amps[at, :] + jnp.where(
                        keep[h], proj[:, h * 128 : (h + 1) * 128], 0.0
                    )
            return carry

        lax.fori_loop(0, PIECE // 2, row_pair, 0, unroll=4)
        at = pl.ds(piece * PIECE, PIECE)
        copy = pltpu.make_async_copy(
            result.at[:, :, at, :], out_ref.at[:, :, at, :], out_sem.at[piece]
        )
        copy.start()
        pieces.append(copy)
    for copy in plane_out + pieces:
        copy.wait()


def backward(lhs, count, amp, wide, grad, planes, rows):
    members, modes, _, cols = amp.shape
    lev_dev, own = planes.shape[2:4]
    vmem = pl.BlockSpec(memory_space=pltpu.VMEM)
    anywhere = pl.BlockSpec(memory_space=pl.ANY)
    field = jax.ShapeDtypeStruct((lev_dev, own, 2 * cols), F32)
    return pl.pallas_call(
        backward_kernel,
        in_specs=[vmem] * 6,
        out_specs=[anywhere] * 3,
        out_shape=[jax.ShapeDtypeStruct((members, modes, rows, cols), F32), field, field],
        scratch_shapes=[
            pltpu.VMEM(amp.shape, F32),
            pltpu.SemaphoreType.DMA((rows // PIECE,)),
            pltpu.SemaphoreType.DMA((4,)),
        ],
        compiler_params=pltpu.CompilerParams(vmem_limit_bytes=12 << 20),
        name="backward_modes",
    )(lhs, count, amp, wide, grad, planes)


def exchange_kernel(
    sizes,
    lhs_ref,
    count_ref,
    amp_ref,
    pert_ref,
    control_ref,
    innov_ref,
    std_ref,
    spread_ref,
    land_ref,
    row_index_ref,
    row_weight_ref,
    col_index_ref,
    col_weight_ref,
    amp_out,
    wide,
    shares,
    planes_out,
    tile,
    narrow,
    core_in,
    x1_in,
    x2_in,
    x3_in,
    x4_in,
    yq_in,
    y1_in,
    y2_in,
    y3_in,
    window,
    field_a,
    field_b,
    misfit,
    cells,
    row_faces,
    col_faces,
    weights,
    sigma,
    col_mat,
    back,
    planes_in,
    send_sem,
    recv_sem,
    load_sem,
    plane_sem,
):
    coarse_count, fine_count, rows_all = sizes
    xs = fine_count // 2
    coarse = lax.axis_index("coarse")
    fine = lax.axis_index("fine")
    lev = lax.axis_index("lev")
    x = lax.rem(fine, xs)
    y = fine // xs
    right, left, across = lax.rem(x + 1, xs), lax.rem(x + xs - 1, xs), lax.rem(x + 2, xs)
    other_y = 1 - y
    serial = coarse * fine_count + fine
    count = coarse_count * fine_count
    after, before = lax.rem(serial + 1, count), lax.rem(serial + count - 1, count)
    first_row = serial * 2 * ROWS
    members, modes = amp_ref.shape[:2]
    levels = pert_ref.shape[1]
    sums = tile.at[lev]

    to_core = (coarse, fine, 1 - lev)
    to_right = (coarse, y * xs + right, lev)
    to_left = (coarse, y * xs + left, lev)
    to_y = (coarse, other_y * xs + x, lev)
    to_after = (after // fine_count, lax.rem(after, fine_count), lev)
    to_before = (before // fine_count, lax.rem(before, fine_count), lev)

    barrier = pltpu.get_barrier_semaphore()
    for device in (to_core, to_right, to_left, to_y, to_after, to_before):
        pl.semaphore_signal(barrier, inc=1, device_id=device, device_id_type=pl.DeviceIdType.MESH)

    numbers = iter(range(100))
    sent = []

    def remote(src, dst, device):
        number = next(numbers)
        copy = pltpu.make_async_remote_copy(
            src_ref=src,
            dst_ref=dst,
            send_sem=send_sem.at[number],
            recv_sem=recv_sem.at[number],
            device_id=device,
            device_id_type=pl.DeviceIdType.MESH,
        )
        copy.start()
        sent.append(copy)
        return copy

    def share(ry, rx):
        return (ry * xs + rx) * ROWS

    lev_dev = control_ref.shape[0]
    own = 2 * ROWS
    lanes = [pl.ds(0, 128), pl.ds(128, 128)]
    plane_in = [
        [
            pltpu.make_async_copy(
                ref.at[:, :, lanes[side]],
                planes_in.at[number, side],
                plane_sem.at[2 * number + side],
            )
            for side in range(2)
        ]
        for number, ref in enumerate((control_ref, innov_ref))
    ]
    for copy in plane_in[0]:
        copy.start()
    pert_in = []
    for k in range(members):
        copy = pltpu.make_async_copy(pert_ref.at[k], narrow.at[k], load_sem.at[k])
        copy.start()
        pert_in.append(copy)
    amp_in = []
    for number, (part, ry) in enumerate(
        ((across // 2, 0), (across // 2, 1), (1 - across // 2, 0), (1 - across // 2, 1))
    ):
        at = pl.ds(pl.multiple_of(ry * xs * ROWS + part * PIECE, PIECE), PIECE)
        copy = pltpu.make_async_copy(
            amp_ref.at[:, :, at, :], amp_out.at[:, :, at, :], load_sem.at[members + number]
        )
        copy.start()
        amp_in.append(copy)
    for copy in plane_in[1]:
        copy.start()

    def planes(ref, number, side):
        return ref.at[number, side].reshape(lev_dev * own, 128)

    for copy in plane_in[0]:
        copy.wait()

    def load_rows(i, carry):
        for side in range(2):
            field_a[EDGE + i, :, lanes[side]] = planes(planes_in, 0, side)[
                pl.ds(i, lev_dev, stride=own), :
            ]
        sub = lax.broadcasted_iota(jnp.int32, (8, 256), 0)
        weight = jnp.full((8, 256), row_weight_ref[i], F32)
        index = jnp.full((8, 256), row_index_ref[i], jnp.int32)
        upper = (index == (first_row + i) // 2).astype(F32)
        spread = jnp.broadcast_to(spread_ref[pl.ds(i, 1), :], (8, 256))
        land = jnp.broadcast_to(land_ref[pl.ds(i, 1), :], (8, 256)).astype(F32)
        cells[EDGE + i] = jnp.where(
            sub == 0, spread, jnp.where(sub == 1, land, jnp.where(sub == 2, weight, upper))
        )
        return carry

    lax.fori_loop(0, own, load_rows, 0, unroll=4)
    for ref in (cells, misfit):
        ref[0] = jnp.zeros(ref.shape[1:], F32)
        ref[GROWN - 1] = jnp.zeros(ref.shape[1:], F32)
    for row in (1, GROWN - 2):
        field_b[row] = jnp.zeros(field_b.shape[1:], F32)
    for lev_at in range(lev_dev):
        sigma[lev_at : lev_at + 1, :] = jnp.full((1, 256), std_ref[lev_at], F32)

    pl.semaphore_wait(barrier, 6)

    top, bottom = pl.ds(EDGE, HALO), pl.ds(EDGE + own - HALO, HALO)
    low, high = pl.ds(EDGE - HALO, HALO), pl.ds(EDGE + own, HALO)
    halo_sends = [
        remote(ref.at[src], ref.at[dst], device)
        for ref in (cells, field_a)
        for src, dst, device in ((top, high, to_before), (bottom, low, to_after))
    ]

    def x_rows(ry, rx):
        return pl.ds(share(ry, rx), XROWS)

    def y_rows(rx, part, ry=None):
        start = share(y if ry is None else ry, rx) + XROWS
        return {
            "all": pl.ds(start, YROWS),
            "a": pl.ds(start, YA),
            "b": pl.ds(start + YA, YROWS - YA),
        }[part]

    def add(rows, *terms):
        total = sums[rows]
        for term in terms:
            total = total + term[...]
        sums[rows] = total

    for k in range(members):
        pert_in[k].wait()

        def widen(level, carry):
            wide[k, level, pl.ds(0, pert_ref.shape[2])] = narrow[k, level].astype(F32)
            return carry

        lax.fori_loop(0, levels, widen, 0, unroll=4)

    for copy in halo_sends[:2]:
        copy.wait_recv()

    def coefficients(e, carry):
        here, there = cells[e], cells[e + 1]
        line = first_row - EDGE + e
        inside = (line >= 0) & (line < rows_all) & (e >= 1) & (e <= GROWN - 2)
        facing = (line >= 0) & (line + 1 < rows_all)
        inside = jnp.where(inside, 1.0, 0.0).astype(F32)
        facing = jnp.where(facing, 1.0, 0.0).astype(F32)
        lane = lax.broadcasted_iota(jnp.int32, (8, 256), 1)
        spread, land = (jnp.broadcast_to(here[j : j + 1], (8, 256)) for j in (0, 1))
        spread_next, land_next = (jnp.broadcast_to(there[j : j + 1], (8, 256)) for j in (0, 1))
        row_faces[e] = (
            jnp.sqrt(spread * spread_next) * (1.0 - 0.5 * jnp.abs(land - land_next)) * facing
        )
        spread_right, land_right = (pltpu.roll(v, 255, 1) for v in (spread, land))
        col_faces[e] = jnp.where(
            lane < 255,
            jnp.sqrt(spread * spread_right) * (1.0 - 0.5 * jnp.abs(land - land_right)),
            0.0,
        )
        weight, upper = (jnp.broadcast_to(here[j : j + 1, :128], (8, 128)) for j in (2, 3))
        upper_on = upper > 0.5
        weights[0, e] = jnp.where(upper_on, 0.0, 1.0 - weight) * inside
        weights[1, e] = jnp.where(upper_on, 1.0 - weight, weight) * inside
        weights[2, e] = jnp.where(upper_on, weight, 0.0) * inside
        return carry

    lax.fori_loop(0, GROWN - 1, coefficients, 0, unroll=4)
    for j in range(3):
        weights[j, GROWN - 1] = jnp.zeros((8, 128), F32)
    col = lax.broadcasted_iota(jnp.int32, (128, 256), 0)
    col_at, col_w = col_index_ref[...], col_weight_ref[...]
    matrix = jnp.where(col == col_at, 1.0 - col_w, jnp.where(col == col_at + 1, col_w, 0.0))
    hi, lo = halves(matrix)
    col_mat[0], col_mat[1] = hi, lo

    amps = amp_out.reshape(members * modes * PITCH, 128)
    perts = wide.reshape(members * levels * PITCH, 128)
    lhs = lhs_ref[...]
    mode = lax.broadcasted_iota(jnp.int32, (modes, 128), 0)

    def contract(start):
        def row_pair(step, carry):
            first = start + step * 2
            keep = [mode < count_ref[pl.ds(first + h, 1), :] for h in range(2)]
            total = [jnp.zeros((levels, 128), F32) for _ in range(2)]
            for k in range(members):
                rhs = []
                for h in range(2):
                    amp = amps[pl.ds(k * modes * PITCH + first + h, modes, stride=PITCH), :]
                    rhs.append(stacked(jnp.where(keep[h], amp, 0.0)))
                level_amp = jnp.dot(lhs, jnp.concatenate(rhs, axis=1), preferred_element_type=F32)
                for h in range(2):
                    pert = perts[pl.ds(k * levels * PITCH + first + h, levels, stride=PITCH), :]
                    total[h] = total[h] + pert * level_amp[:, h * 128 : (h + 1) * 128]
            for h in range(2):
                tile[0, first + h] = total[h][: levels // 2]
                tile[1, first + h] = total[h][levels // 2 :]
            return carry

        lax.fori_loop(0, ROWS // 2, row_pair, 0, unroll=3)

    order = [(0, across), (1, across), (0, right), (1, right), (1, left), (0, left), (other_y, x), (y, x)]
    core_sends = []

    def produce(number):
        start = share(*order[number])
        contract(start)
        rows = pl.ds(start, ROWS)
        core_sends.append(remote(tile.at[1 - lev, rows], core_in.at[rows], to_core))

    def settle(number):
        core_sends[number].wait_recv()
        rows = pl.ds(share(*order[number]), ROWS)
        add(rows, core_in.at[rows])

    def pass_y(rx, number):
        return remote(sums.at[y_rows(rx, "all", other_y)], yq_in.at[number], to_y)

    for copy in amp_in[:2]:
        copy.wait()
    produce(0)
    produce(1)
    for copy in amp_in[2:]:
        copy.wait()
    produce(2)
    settle(0)
    x1_right = remote(sums.at[x_rows(0, across)], x1_in.at[0], to_right)
    produce(3)
    settle(1)
    x1_left = remote(sums.at[x_rows(1, across)], x1_in.at[1], to_left)
    q_across = pass_y(across, 0)
    produce(4)
    settle(2)
    produce(5)
    settle(3)
    x2_right = remote(sums.at[x_rows(1, right)], x2_in.at[0], to_right)
    q_right = pass_y(right, 1)
    produce(6)
    settle(4)
    x1_right.wait_recv()
    add(x_rows(0, right), x1_in.at[0])
    x3_right = remote(sums.at[x_rows(0, right)], x3_in.at[0], to_right)
    x1_left.wait_recv()
    add(x_rows(1, left), x1_in.at[1])
    x3_left = remote(sums.at[x_rows(1, left)], x3_in.at[1], to_left)
    produce(7)
    settle(5)
    x2_left = remote(sums.at[x_rows(0, left)], x2_in.at[1], to_left)
    q_left = pass_y(left, 2)
    settle(6)
    q_own = pass_y(x, 3)
    q_across.wait_recv()
    add(y_rows(across, "all"), yq_in.at[0])
    y1_right = remote(sums.at[y_rows(across, "a")], y1_in.at[0, pl.ds(0, YA)], to_right)
    y1_left = remote(sums.at[y_rows(across, "b")], y1_in.at[1], to_left)
    q_right.wait_recv()
    add(y_rows(right, "all"), yq_in.at[1])
    y2_right = remote(sums.at[y_rows(right, "b")], y2_in.at[0], to_right)

    def sweep(src, dst):
        def rows_of_four(step, carry):
            e = EDGE - 2 + 4 * step
            down = row_faces[pl.ds(e - 1, 5)]
            side = col_faces[pl.ds(e, 4)]
            for tile in range(lev_dev // 8):
                at = pl.ds(8 * tile, 8)
                v = src[pl.ds(e - 1, 6), at, :]
                mid = v[1:5]
                flux = down * (v[1:] - v[:-1])
                cross = side * (pltpu.roll(mid, 255, 2) - mid)
                dst[pl.ds(e, 4), at, :] = (
                    mid + (flux[1:] - flux[:-1]) + (cross - pltpu.roll(cross, 1, 2))
                )
            return carry

        lax.fori_loop(0, 7, rows_of_four, 0)

    for copy in halo_sends[2:]:
        copy.wait_recv()
        copy.wait_send()
    sweep(field_a, field_b)

    settle(7)
    q_left.wait_recv()
    add(y_rows(left, "all"), yq_in.at[2])
    y2_left = remote(sums.at[y_rows(left, "a")], y2_in.at[1, pl.ds(0, YA)], to_left)
    y1_right.wait_recv()
    y1_left.wait_recv()
    a_rows, b_rows = y_rows(right, "a"), y_rows(left, "b")
    add(a_rows, y1_in.at[0, pl.ds(0, YA)])
    y3_right = remote(sums.at[a_rows], y3_in.at[0, pl.ds(0, YA)], to_right)
    add(b_rows, y1_in.at[1])
    y3_left = remote(sums.at[b_rows], y3_in.at[1], to_left)

    sweep(field_b, field_a)

    for copy in (x2_right, x2_left, x3_right, x3_left):
        copy.wait_recv()
    rows = x_rows(other_y, x)
    add(rows, x3_in.at[other_y], x2_in.at[y])
    x4 = remote(sums.at[rows], x4_in, to_y)
    add(x_rows(y, x), x3_in.at[y], x2_in.at[other_y])

    sweep(field_a, field_b)

    def static_part(i, carry):
        for side in range(2):
            cols = lanes[side]
            misfit[EDGE + i, :, cols] = (
                sigma[:, cols] * field_b[EDGE + i, :, cols]
                - planes(planes_in, 1, side)[pl.ds(i, lev_dev, stride=own), :]
            )
        return carry

    for copy in plane_in[1]:
        copy.wait()

    lax.fori_loop(0, own, static_part, 0, unroll=4)
    misfit_sends = [
        remote(misfit.at[top], misfit.at[high], to_before),
        remote(misfit.at[bottom], misfit.at[low], to_after),
    ]

    q_own.wait_recv()
    add(y_rows(x, "all"), yq_in.at[3])
    for copy in (y2_right, y2_left, y3_right, y3_left):
        copy.wait_recv()
    mine = share(y, x)
    window[pl.ds(HALO + XROWS, YA)] = (
        sums[y_rows(x, "a")] + y3_in[0, :YA] + y2_in[1, :YA]
    )
    window[pl.ds(HALO + XROWS + YA, YROWS - YA)] = sums[y_rows(x, "b")] + y3_in[1] + y2_in[0]
    window_after = remote(
        window.at[pl.ds(ROWS, HALO)], window.at[pl.ds(0, HALO)], to_after
    )
    x4.wait_recv()
    window[pl.ds(HALO, XROWS)] = sums[pl.ds(mine, XROWS)] + x4_in[...]
    window_before = remote(
        window.at[pl.ds(HALO, HALO)], window.at[pl.ds(HALO + ROWS, HALO)], to_before
    )
    for copy in misfit_sends + [window_after, window_before]:
        copy.wait_recv()
    for copy in misfit_sends:
        copy.wait_send()

    def dot_split(lhs, which):
        hi, lo = halves(lhs)
        c_hi, c_lo = col_mat[0], col_mat[1]
        dims = (((1,), (which,)), ((), ()))
        dot = functools.partial(lax.dot_general, dimension_numbers=dims, preferred_element_type=F32)
        return dot(hi, c_hi) + (dot(lo, c_hi) + dot(hi, c_lo))

    span = 8

    def interpolate(step, carry):
        e0 = step * span
        lines = []
        for pair in range(span // 2):
            t = step * (span // 2) + pair + 1
            w = [window[t + d].reshape(lev_dev // 8, 8, 128) for d in (-1, 0, 1)]
            for h in range(2):
                e = e0 + 2 * pair + h
                line = weights[0, e] * w[0] + weights[1, e] * w[1] + weights[2, e] * w[2]
                lines.append(line.reshape(lev_dev, 128))
        fine_part = dot_split(jnp.concatenate(lines, axis=0), 0)
        at = pl.ds(e0, span)
        total = misfit[at] + fine_part.reshape(span, lev_dev, 256)
        misfit[at] = total
        back[at] = dot_split(total.reshape(span * lev_dev, 256), 1).reshape(span, lev_dev, 128)
        return carry

    lax.fori_loop(0, GROWN // span, interpolate, 0)

    def adjoint(r, carry):
        e = 2 * r + 2
        total = jnp.zeros((lev_dev // 8, 8, 128), F32)
        for j in range(6):
            total = total + weights[2 - j // 2, e + j] * back[e + j].reshape(lev_dev // 8, 8, 128)
        shares[lev, mine + r] = total.reshape(lev_dev, 128)
        return carry

    lax.fori_loop(0, ROWS, adjoint, 0, unroll=4)

    def to_all(rows, device):
        return remote(shares.at[lev, rows], shares.at[lev, rows], device)

    def x_part(ry, rx):
        return pl.ds(share(ry, rx), XROWS)

    pair_first = to_all(x_part(y, x), to_y)
    ring_y = [to_all(y_rows(x, "all"), to_right), to_all(y_rows(x, "all"), to_left)]
    ring_own = [to_all(x_part(y, x), to_right), to_all(x_part(y, x), to_left)]
    core = [to_all(pl.ds(mine, ROWS), to_core)]
    pair_y = [to_all(y_rows(x, "all"), to_y)]

    def scaled(e, carry):
        at = pl.ds(e * 2 + 1, 2)
        field_a[at] = sigma[...] * misfit[at]
        return carry

    lax.fori_loop(0, (GROWN - 2) // 2, scaled, 0)

    pair_first.wait_recv()
    ring_other = [to_all(x_part(other_y, x), to_right), to_all(x_part(other_y, x), to_left)]
    core.append(to_all(x_part(other_y, x), to_core))
    for copy in ring_y:
        copy.wait_recv()
    on_y = [
        to_all(y_rows(left, "a"), to_right),
        to_all(y_rows(right, "b"), to_left),
    ]
    for rx in (left, right):
        pair_y.append(to_all(y_rows(rx, "all"), to_y))
        core.append(to_all(y_rows(rx, "all"), to_core))

    sweep(field_a, field_b)

    for copy in ring_own + ring_other:
        copy.wait_recv()
    on_x = [to_all(x_part(0, left), to_right), to_all(x_part(1, right), to_left)]
    for rx in (left, right):
        for ry in (0, 1):
            core.append(to_all(x_part(ry, rx), to_core))
    for copy in on_y:
        copy.wait_recv()
    pair_y.append(to_all(y_rows(across, "all"), to_y))
    core.append(to_all(y_rows(across, "all"), to_core))

    sweep(field_b, field_a)
    sweep(field_a, field_b)

    def finish(i, carry):
        at = pl.ds(i, lev_dev, stride=own)
        for side in range(2):
            for number, value in ((0, field_b), (1, misfit)):
                planes(planes_out, number, side)[at, :] = (
                    planes(planes_in, number, side)[at, :] + value[EDGE + i, :, lanes[side]]
                )
        return carry

    lax.fori_loop(0, own, finish, 0, unroll=4)
    for copy in on_x:
        copy.wait_recv()
    for ry in (0, 1):
        core.append(to_all(x_part(ry, across), to_core))
    for rx, copy in zip((x, left, right, across), pair_y):
        copy.wait_recv()
        core.append(to_all(y_rows(rx, "all", other_y), to_core))
    for copy in core:
        copy.wait_recv()
    waited = halo_sends[2:] + misfit_sends
    for copy in sent:
        if not any(copy is done for done in waited):
            copy.wait_send()


def exchange(sizes, lhs, count, amp, pert, control, innov, std, spread, land, row_index, row_weight, col_index, col_weight):
    members, modes, rows, cols = amp.shape
    levels = pert.shape[1]
    lev_dev, own, cols_fine = control.shape
    vmem = pl.BlockSpec(memory_space=pltpu.VMEM)
    smem = pl.BlockSpec(memory_space=pltpu.SMEM)
    anywhere = pl.BlockSpec(memory_space=pl.ANY)
    cell = (lev_dev, 128)
    row = (lev_dev, cols_fine)
    tile = (2, rows) + cell
    return pl.pallas_call(
        functools.partial(exchange_kernel, sizes),
        in_specs=[vmem, vmem, anywhere, anywhere, anywhere, anywhere, smem, vmem, vmem, smem, smem, vmem, vmem],
        out_specs=[vmem] * 4,
        out_shape=[
            pltpu.VMEM((members, modes, PITCH, cols), F32),
            pltpu.VMEM((members, levels, PITCH, cols), F32),
            pltpu.VMEM(tile, F32),
            pltpu.VMEM((2, 2, lev_dev, own, 128), F32),
        ],
        scratch_shapes=[
            pltpu.VMEM(tile, F32),
            pltpu.VMEM(pert.shape, BF16),
            pltpu.VMEM((rows,) + cell, F32),
            pltpu.VMEM((2, XROWS) + cell, F32),
            pltpu.VMEM((2, XROWS) + cell, F32),
            pltpu.VMEM((2, XROWS) + cell, F32),
            pltpu.VMEM((XROWS,) + cell, F32),
            pltpu.VMEM((4, YROWS) + cell, F32),
            pltpu.VMEM((2, YROWS - YA) + cell, F32),
            pltpu.VMEM((2, YROWS - YA) + cell, F32),
            pltpu.VMEM((2, YROWS - YA) + cell, F32),
            pltpu.VMEM((ROWS + 2 * HALO,) + cell, F32),
            pltpu.VMEM((GROWN,) + row, F32),
            pltpu.VMEM((GROWN,) + row, F32),
            pltpu.VMEM((GROWN,) + row, F32),
            pltpu.VMEM((GROWN, 8, cols_fine), F32),
            pltpu.VMEM((GROWN, 8, cols_fine), F32),
            pltpu.VMEM((GROWN, 8, cols_fine), F32),
            pltpu.VMEM((3, GROWN, 8, 128), F32),
            pltpu.VMEM(row, F32),
            pltpu.VMEM((2, 128, cols_fine), BF16),
            pltpu.VMEM((GROWN,) + cell, F32),
            pltpu.VMEM((2, 2, lev_dev, own, 128), F32),
            pltpu.SemaphoreType.DMA((80,)),
            pltpu.SemaphoreType.DMA((80,)),
            pltpu.SemaphoreType.DMA((members + 4,)),
            pltpu.SemaphoreType.DMA((4,)),
        ],
        compiler_params=pltpu.CompilerParams(
            collective_id=0, has_side_effects=True, vmem_limit_bytes=24 << 20
        ),
        name="exchange",
    )(
        lhs,
        count,
        amp,
        pert,
        control,
        innov,
        std,
        spread,
        land,
        row_index,
        row_weight,
        col_index.reshape(1, cols_fine),
        col_weight.reshape(1, cols_fine),
    )


def local(
    ens_pert,
    ens_control,
    eigen_modes,
    mode_count,
    row_index,
    row_weight,
    col_index,
    col_weight,
    static_control,
    static_std,
    diffusivity,
    land_mask,
    innovation,
):
    sizes = (
        lax.axis_size("coarse"),
        lax.axis_size("fine"),
        lax.axis_size("coarse") * lax.axis_size("fine") * row_index.shape[0],
    )
    scaled = eigen_modes * (1.0 / math.sqrt(MEMBERS - 1))
    amp, wide, coarse_grad, planes = exchange(
        sizes,
        split_modes(scaled),
        mode_count,
        ens_control,
        ens_pert,
        static_control,
        innovation,
        static_std,
        diffusivity,
        land_mask,
        row_index,
        row_weight,
        col_index,
        col_weight,
    )
    grad_ens, grad_static, increment = backward(
        split_modes(scaled.T), mode_count, amp, wide, coarse_grad, planes, mode_count.shape[0]
    )
    return increment, grad_static, grad_ens


def solution(mesh):
    in_specs = (
        P(("fine", "lev"), None, "coarse", None),
        P(("fine", "lev"), None, "coarse", None),
        P(),
        P("coarse", None),
        P(("coarse", "fine")),
        P(("coarse", "fine")),
        P(),
        P(),
        P("lev", ("coarse", "fine"), None),
        P("lev"),
        P(("coarse", "fine"), None),
        P(("coarse", "fine"), None),
        P("lev", ("coarse", "fine"), None),
    )
    out_specs = (
        P("lev", ("coarse", "fine"), None),
        P("lev", ("coarse", "fine"), None),
        P(("fine", "lev"), None, "coarse", None),
    )
    return jax.shard_map(local, mesh=mesh, in_specs=in_specs, out_specs=out_specs, check_vma=False)
```

```python
import functools
import math

import jax
import jax.numpy as jnp
from jax import lax
from jax.experimental import pallas as pl
from jax.experimental.pallas import tpu as pltpu
from jax.sharding import PartitionSpec as P

MEMBERS = 80
NSWEEP = 3
HALO = 3
EDGE = 4
GROWN = 32
ROWS = 12
XROWS = 6
YROWS = ROWS - XROWS
YA = YROWS // 2
PITCH = 104
PIECE = 24
F32 = jnp.float32
BF16 = jnp.bfloat16


def halves(value):
    hi = value.astype(BF16)
    return hi, (value - hi.astype(F32)).astype(BF16)


def stacked(value):
    hi, lo = halves(value)
    return jnp.concatenate([hi, hi, lo], axis=0)


def split_modes(matrix):
    hi = lax.reduce_precision(matrix, 8, 7)
    lo = matrix - hi
    wide = jnp.concatenate([hi, lo, hi], axis=1).astype(BF16)
    tall = jnp.concatenate([hi, lo, hi], axis=0).astype(BF16)
    return tall.T, wide


def backward_kernel(
    lhs_ref,
    count_ref,
    amp_ref,
    wide_ref,
    grad_ref,
    planes_ref,
    out_ref,
    grad_static_ref,
    inc_ref,
    result,
    out_sem,
    plane_sem,
):
    members, modes = amp_ref.shape[:2]
    levels = wide_ref.shape[1]
    rows = out_ref.shape[2]
    plane_out = [
        pltpu.make_async_copy(
            planes_ref.at[number, side],
            ref.at[:, :, pl.ds(128 * side, 128)],
            plane_sem.at[2 * number + side],
        )
        for number, ref in enumerate((grad_static_ref, inc_ref))
        for side in range(2)
    ]
    for copy in plane_out:
        copy.start()
    amps = amp_ref.reshape(members * modes * PITCH, 128)
    perts = wide_ref.reshape(members * levels * PITCH, 128)
    outs = result.reshape(members * modes * PITCH, 128)
    lhs = lhs_ref[...]
    mode = lax.broadcasted_iota(jnp.int32, (modes, 128), 0)
    pieces = []
    for piece in range(rows // PIECE):

        def row_pair(step, carry):
            first = piece * PIECE + step * 2
            keep = [mode < count_ref[pl.ds(first + h, 1), :] for h in range(2)]
            grad = [
                jnp.concatenate([grad_ref[0, first + h], grad_ref[1, first + h]], axis=0)
                for h in range(2)
            ]
            for k in range(members):
                rhs = []
                for h in range(2):
                    pert = perts[pl.ds(k * levels * PITCH + first + h, levels, stride=PITCH), :]
                    rhs.append(stacked(pert * grad[h]))
                proj = jnp.dot(lhs, jnp.concatenate(rhs, axis=1), preferred_element_type=F32)
                for h in range(2):
                    at = pl.ds(k * modes * PITCH + first + h, modes, stride=PITCH)
                    outs[at, :] = amps[at, :] + jnp.where(
                        keep[h], proj[:, h * 128 : (h + 1) * 128], 0.0
                    )
            return carry

        lax.fori_loop(0, PIECE // 2, row_pair, 0, unroll=4)
        at = pl.ds(piece * PIECE, PIECE)
        copy = pltpu.make_async_copy(
            result.at[:, :, at, :], out_ref.at[:, :, at, :], out_sem.at[piece]
        )
        copy.start()
        pieces.append(copy)
    for copy in plane_out + pieces:
        copy.wait()


def backward(lhs, count, amp, wide, grad, planes, rows):
    members, modes, _, cols = amp.shape
    lev_dev, own = planes.shape[2:4]
    vmem = pl.BlockSpec(memory_space=pltpu.VMEM)
    anywhere = pl.BlockSpec(memory_space=pl.ANY)
    field = jax.ShapeDtypeStruct((lev_dev, own, 2 * cols), F32)
    return pl.pallas_call(
        backward_kernel,
        in_specs=[vmem] * 6,
        out_specs=[anywhere] * 3,
        out_shape=[jax.ShapeDtypeStruct((members, modes, rows, cols), F32), field, field],
        scratch_shapes=[
            pltpu.VMEM(amp.shape, F32),
            pltpu.SemaphoreType.DMA((rows // PIECE,)),
            pltpu.SemaphoreType.DMA((4,)),
        ],
        compiler_params=pltpu.CompilerParams(vmem_limit_bytes=12 << 20),
        name="backward_modes",
    )(lhs, count, amp, wide, grad, planes)


def exchange_kernel(
    sizes,
    lhs_ref,
    count_in,
    amp_ref,
    pert_ref,
    control_ref,
    innov_ref,
    std_in,
    spread_in,
    land_in,
    row_index_in,
    row_weight_in,
    col_index_in,
    col_weight_in,
    amp_out,
    wide,
    shares,
    planes_out,
    count_ref,
    tile,
    narrow,
    core_in,
    x1_in,
    x2_in,
    x3_in,
    x4_in,
    yq_in,
    y1_in,
    y2_in,
    y3_in,
    window,
    field_a,
    field_b,
    misfit,
    cells,
    row_faces,
    col_faces,
    weights,
    sigma,
    col_mat,
    back,
    planes_in,
    std_ref,
    spread_ref,
    land_ref,
    row_index_ref,
    row_weight_ref,
    col_index_ref,
    col_weight_ref,
    send_sem,
    recv_sem,
    load_sem,
    plane_sem,
    small_sem,
):
    coarse_count, fine_count, rows_all = sizes
    xs = fine_count // 2
    coarse = lax.axis_index("coarse")
    fine = lax.axis_index("fine")
    lev = lax.axis_index("lev")
    x = lax.rem(fine, xs)
    y = fine // xs
    right, left, across = lax.rem(x + 1, xs), lax.rem(x + xs - 1, xs), lax.rem(x + 2, xs)
    other_y = 1 - y
    serial = coarse * fine_count + fine
    count = coarse_count * fine_count
    after, before = lax.rem(serial + 1, count), lax.rem(serial + count - 1, count)
    first_row = serial * 2 * ROWS
    members, modes = amp_ref.shape[:2]
    levels = pert_ref.shape[1]
    sums = tile.at[lev]

    to_core = (coarse, fine, 1 - lev)
    to_right = (coarse, y * xs + right, lev)
    to_left = (coarse, y * xs + left, lev)
    to_y = (coarse, other_y * xs + x, lev)
    to_after = (after // fine_count, lax.rem(after, fine_count), lev)
    to_before = (before // fine_count, lax.rem(before, fine_count), lev)

    barrier = pltpu.get_barrier_semaphore()
    for device in (to_core, to_right, to_left, to_y, to_after, to_before):
        pl.semaphore_signal(barrier, inc=1, device_id=device, device_id_type=pl.DeviceIdType.MESH)

    numbers = iter(range(100))
    sent = []

    def remote(src, dst, device):
        number = next(numbers)
        copy = pltpu.make_async_remote_copy(
            src_ref=src,
            dst_ref=dst,
            send_sem=send_sem.at[number],
            recv_sem=recv_sem.at[number],
            device_id=device,
            device_id_type=pl.DeviceIdType.MESH,
        )
        copy.start()
        sent.append(copy)
        return copy

    def share(ry, rx):
        return (ry * xs + rx) * ROWS

    lev_dev = control_ref.shape[0]
    own = 2 * ROWS
    lanes = [pl.ds(0, 128), pl.ds(128, 128)]
    plane_in = [
        [
            pltpu.make_async_copy(
                ref.at[:, :, lanes[side]],
                planes_in.at[number, side],
                plane_sem.at[2 * number + side],
            )
            for side in range(2)
        ]
        for number, ref in enumerate((control_ref, innov_ref))
    ]
    small_in = [
        pltpu.make_async_copy(src, dst, small_sem.at[number])
        for number, (src, dst) in enumerate(
            (
                (spread_in, spread_ref),
                (land_in, land_ref),
                (row_index_in, row_index_ref),
                (row_weight_in, row_weight_ref),
                (std_in, std_ref),
                (col_index_in, col_index_ref),
                (col_weight_in, col_weight_ref),
                (count_in, count_ref),
            )
        )
    ]
    for copy in small_in + plane_in[0]:
        copy.start()
    half_rows = xs * ROWS
    pert_in, amp_in = [], []
    for half, ry in enumerate((other_y, y)):
        at = pl.ds(pl.multiple_of(ry * half_rows, 16), half_rows)
        for k in range(members):
            copy = pltpu.make_async_copy(
                pert_ref.at[k, :, at, :], narrow.at[k, :, at, :], load_sem.at[half * members + k]
            )
            copy.start()
            pert_in.append(copy)
        for part in (0, 1):
            column = lax.rem(across // 2 + part, 2)
            at = pl.ds(pl.multiple_of(ry * half_rows + column * PIECE, PIECE), PIECE)
            copy = pltpu.make_async_copy(
                amp_ref.at[:, :, at, :],
                amp_out.at[:, :, at, :],
                load_sem.at[2 * members + 2 * half + part],
            )
            copy.start()
            amp_in.append(copy)
    for copy in plane_in[1]:
        copy.start()

    def planes(ref, number, side):
        return ref.at[number, side].reshape(lev_dev * own, 128)

    for copy in small_in + plane_in[0]:
        copy.wait()

    def load_rows(i, carry):
        for side in range(2):
            field_a[EDGE + i, :, lanes[side]] = planes(planes_in, 0, side)[
                pl.ds(i, lev_dev, stride=own), :
            ]
        sub = lax.broadcasted_iota(jnp.int32, (8, 256), 0)
        weight = jnp.full((8, 256), row_weight_ref[i], F32)
        index = jnp.full((8, 256), row_index_ref[i], jnp.int32)
        upper = (index == (first_row + i) // 2).astype(F32)
        spread = jnp.broadcast_to(spread_ref[pl.ds(i, 1), :], (8, 256))
        land = jnp.broadcast_to(land_ref[pl.ds(i, 1), :], (8, 256)).astype(F32)
        cells[EDGE + i] = jnp.where(
            sub == 0, spread, jnp.where(sub == 1, land, jnp.where(sub == 2, weight, upper))
        )
        return carry

    lax.fori_loop(0, own, load_rows, 0, unroll=4)
    for ref in (cells, misfit):
        ref[0] = jnp.zeros(ref.shape[1:], F32)
        ref[GROWN - 1] = jnp.zeros(ref.shape[1:], F32)
    for row in (1, GROWN - 2):
        field_b[row] = jnp.zeros(field_b.shape[1:], F32)
    for lev_at in range(lev_dev):
        sigma[lev_at : lev_at + 1, :] = jnp.full((1, 256), std_ref[lev_at], F32)

    pl.semaphore_wait(barrier, 6)

    top, bottom = pl.ds(EDGE, HALO), pl.ds(EDGE + own - HALO, HALO)
    low, high = pl.ds(EDGE - HALO, HALO), pl.ds(EDGE + own, HALO)
    halo_sends = [
        remote(ref.at[src], ref.at[dst], device)
        for ref in (cells, field_a)
        for src, dst, device in ((top, high, to_before), (bottom, low, to_after))
    ]

    def x_rows(ry, rx):
        return pl.ds(share(ry, rx), XROWS)

    def y_rows(rx, part, ry=None):
        start = share(y if ry is None else ry, rx) + XROWS
        return {
            "all": pl.ds(start, YROWS),
            "a": pl.ds(start, YA),
            "b": pl.ds(start + YA, YROWS - YA),
        }[part]

    def add(rows, *terms):
        total = sums[rows]
        for term in terms:
            total = total + term[...]
        sums[rows] = total

    def widen(half):
        at = pl.ds(pl.multiple_of((other_y, y)[half] * half_rows, 16), half_rows)
        for k in range(members):
            pert_in[half * members + k].wait()

            def widen_level(level, carry):
                wide[k, level, at] = narrow[k, level, at].astype(F32)
                return carry

            lax.fori_loop(0, levels, widen_level, 0, unroll=8)

    widen(0)

    for copy in halo_sends[:2]:
        copy.wait_recv()

    def coefficients(e, carry):
        here, there = cells[e], cells[e + 1]
        line = first_row - EDGE + e
        inside = (line >= 0) & (line < rows_all) & (e >= 1) & (e <= GROWN - 2)
        facing = (line >= 0) & (line + 1 < rows_all)
        inside = jnp.where(inside, 1.0, 0.0).astype(F32)
        facing = jnp.where(facing, 1.0, 0.0).astype(F32)
        lane = lax.broadcasted_iota(jnp.int32, (8, 256), 1)
        spread, land = (jnp.broadcast_to(here[j : j + 1], (8, 256)) for j in (0, 1))
        spread_next, land_next = (jnp.broadcast_to(there[j : j + 1], (8, 256)) for j in (0, 1))
        row_faces[e] = (
            jnp.sqrt(spread * spread_next) * (1.0 - 0.5 * jnp.abs(land - land_next)) * facing
        )
        spread_right, land_right = (pltpu.roll(v, 255, 1) for v in (spread, land))
        col_faces[e] = jnp.where(
            lane < 255,
            jnp.sqrt(spread * spread_right) * (1.0 - 0.5 * jnp.abs(land - land_right)),
            0.0,
        )
        weight, upper = (jnp.broadcast_to(here[j : j + 1, :128], (8, 128)) for j in (2, 3))
        upper_on = upper > 0.5
        weights[0, e] = jnp.where(upper_on, 0.0, 1.0 - weight) * inside
        weights[1, e] = jnp.where(upper_on, 1.0 - weight, weight) * inside
        weights[2, e] = jnp.where(upper_on, weight, 0.0) * inside
        return carry

    lax.fori_loop(0, GROWN - 1, coefficients, 0, unroll=4)
    for j in range(3):
        weights[j, GROWN - 1] = jnp.zeros((8, 128), F32)
    col = lax.broadcasted_iota(jnp.int32, (128, 256), 0)
    col_at, col_w = col_index_ref[...], col_weight_ref[...]
    matrix = jnp.where(col == col_at, 1.0 - col_w, jnp.where(col == col_at + 1, col_w, 0.0))
    hi, lo = halves(matrix)
    col_mat[0], col_mat[1] = hi, lo

    amps = amp_out.reshape(members * modes * PITCH, 128)
    perts = wide.reshape(members * levels * PITCH, 128)
    lhs = lhs_ref[...]
    mode = lax.broadcasted_iota(jnp.int32, (modes, 128), 0)

    def contract(start):
        def row_pair(step, carry):
            first = start + step * 2
            keep = [mode < count_ref[pl.ds(first + h, 1), :] for h in range(2)]
            total = [jnp.zeros((levels, 128), F32) for _ in range(2)]
            for k in range(members):
                rhs = []
                for h in range(2):
                    amp = amps[pl.ds(k * modes * PITCH + first + h, modes, stride=PITCH), :]
                    rhs.append(stacked(jnp.where(keep[h], amp, 0.0)))
                level_amp = jnp.dot(lhs, jnp.concatenate(rhs, axis=1), preferred_element_type=F32)
                for h in range(2):
                    pert = perts[pl.ds(k * levels * PITCH + first + h, levels, stride=PITCH), :]
                    total[h] = total[h] + pert * level_amp[:, h * 128 : (h + 1) * 128]
            for h in range(2):
                tile[0, first + h] = total[h][: levels // 2]
                tile[1, first + h] = total[h][levels // 2 :]
            return carry

        lax.fori_loop(0, ROWS // 2, row_pair, 0, unroll=3)

    order = [
        (other_y, across),
        (other_y, right),
        (other_y, left),
        (other_y, x),
        (y, across),
        (y, left),
        (y, right),
        (y, x),
    ]
    core_sends = []

    def produce(number):
        start = share(*order[number])
        contract(start)
        rows = pl.ds(start, ROWS)
        core_sends.append(remote(tile.at[1 - lev, rows], core_in.at[rows], to_core))

    def settle(number):
        core_sends[number].wait_recv()
        rows = pl.ds(share(*order[number]), ROWS)
        add(rows, core_in.at[rows])

    def pass_y(rx, number):
        return remote(sums.at[y_rows(rx, "all", other_y)], yq_in.at[number], to_y)

    amp_in[0].wait()
    produce(0)
    amp_in[1].wait()
    produce(1)
    produce(2)
    produce(3)
    settle(0)
    x1_right = remote(sums.at[x_rows(other_y, across)], x1_in.at[0], to_right)
    q_across = pass_y(across, 0)
    widen(1)
    settle(1)
    q_right = pass_y(right, 1)
    amp_in[2].wait()
    produce(4)
    settle(2)
    x2_left = remote(sums.at[x_rows(other_y, left)], x2_in.at[1], to_left)
    q_left = pass_y(left, 2)
    amp_in[3].wait()
    produce(5)
    settle(3)
    q_own = pass_y(x, 3)
    settle(4)
    x1_left = remote(sums.at[x_rows(y, across)], x1_in.at[1], to_left)
    produce(6)
    x1_right.wait_recv()
    add(x_rows(other_y, right), x1_in.at[0])
    x3_right = remote(sums.at[x_rows(other_y, right)], x3_in.at[0], to_right)
    q_across.wait_recv()
    add(y_rows(across, "all"), yq_in.at[0])
    y1_right = remote(sums.at[y_rows(across, "a")], y1_in.at[0, pl.ds(0, YA)], to_right)
    y1_left = remote(sums.at[y_rows(across, "b")], y1_in.at[1], to_left)
    settle(5)
    produce(7)
    settle(6)
    x2_right = remote(sums.at[x_rows(y, right)], x2_in.at[0], to_right)
    q_right.wait_recv()
    add(y_rows(right, "all"), yq_in.at[1])
    y2_right = remote(sums.at[y_rows(right, "b")], y2_in.at[0], to_right)
    q_left.wait_recv()
    add(y_rows(left, "all"), yq_in.at[2])
    y2_left = remote(sums.at[y_rows(left, "a")], y2_in.at[1, pl.ds(0, YA)], to_left)
    x1_left.wait_recv()
    add(x_rows(y, left), x1_in.at[1])
    x3_left = remote(sums.at[x_rows(y, left)], x3_in.at[1], to_left)
    settle(7)

    def sweep(src, dst, first=0, last=7):
        def rows_of_four(step, carry):
            e = EDGE - 2 + 4 * step
            down = row_faces[pl.ds(e - 1, 5)]
            side = col_faces[pl.ds(e, 4)]
            for tile in range(lev_dev // 8):
                at = pl.ds(8 * tile, 8)
                v = src[pl.ds(e - 1, 6), at, :]
                mid = v[1:5]
                flux = down * (v[1:] - v[:-1])
                cross = side * (pltpu.roll(mid, 255, 2) - mid)
                dst[pl.ds(e, 4), at, :] = (
                    mid + (flux[1:] - flux[:-1]) + (cross - pltpu.roll(cross, 1, 2))
                )
            return carry

        lax.fori_loop(first, last, rows_of_four, 0)

    for copy in halo_sends[2:]:
        copy.wait_recv()
        copy.wait_send()
    sweep(field_a, field_b)

    y1_right.wait_recv()
    y1_left.wait_recv()
    a_rows, b_rows = y_rows(right, "a"), y_rows(left, "b")
    add(a_rows, y1_in.at[0, pl.ds(0, YA)])
    y3_right = remote(sums.at[a_rows], y3_in.at[0, pl.ds(0, YA)], to_right)
    add(b_rows, y1_in.at[1])
    y3_left = remote(sums.at[b_rows], y3_in.at[1], to_left)

    x3_right.wait_recv()
    x2_left.wait_recv()
    rows = x_rows(other_y, x)
    add(rows, x3_in.at[0], x2_in.at[1])
    x4 = remote(sums.at[rows], x4_in, to_y)

    sweep(field_b, field_a)
    sweep(field_a, field_b)

    def static_part(i, carry):
        for side in range(2):
            cols = lanes[side]
            misfit[EDGE + i, :, cols] = (
                sigma[:, cols] * field_b[EDGE + i, :, cols]
                - planes(planes_in, 1, side)[pl.ds(i, lev_dev, stride=own), :]
            )
        return carry

    for copy in plane_in[1]:
        copy.wait()

    lax.fori_loop(0, own, static_part, 0, unroll=4)
    misfit_sends = [
        remote(misfit.at[top], misfit.at[high], to_before),
        remote(misfit.at[bottom], misfit.at[low], to_after),
    ]

    x3_left.wait_recv()
    x2_right.wait_recv()
    add(x_rows(y, x), x3_in.at[1], x2_in.at[0])
    q_own.wait_recv()
    add(y_rows(x, "all"), yq_in.at[3])
    for copy in (y2_right, y2_left, y3_right, y3_left):
        copy.wait_recv()
    mine = share(y, x)
    window[pl.ds(HALO + XROWS, YA)] = (
        sums[y_rows(x, "a")] + y3_in[0, :YA] + y2_in[1, :YA]
    )
    window[pl.ds(HALO + XROWS + YA, YROWS - YA)] = sums[y_rows(x, "b")] + y3_in[1] + y2_in[0]
    window_after = remote(
        window.at[pl.ds(ROWS, HALO)], window.at[pl.ds(0, HALO)], to_after
    )
    x4.wait_recv()
    window[pl.ds(HALO, XROWS)] = sums[pl.ds(mine, XROWS)] + x4_in[...]
    window_before = remote(
        window.at[pl.ds(HALO, HALO)], window.at[pl.ds(HALO + ROWS, HALO)], to_before
    )
    for copy in misfit_sends + [window_after, window_before]:
        copy.wait_recv()
    for copy in misfit_sends:
        copy.wait_send()

    def dot_split(lhs, which):
        hi, lo = halves(lhs)
        c_hi, c_lo = col_mat[0], col_mat[1]
        dims = (((1,), (which,)), ((), ()))
        dot = functools.partial(lax.dot_general, dimension_numbers=dims, preferred_element_type=F32)
        return dot(hi, c_hi) + (dot(lo, c_hi) + dot(hi, c_lo))

    span = 8

    def interpolate(step, carry):
        e0 = step * span
        lines = []
        for pair in range(span // 2):
            t = step * (span // 2) + pair + 1
            w = [window[t + d].reshape(lev_dev // 8, 8, 128) for d in (-1, 0, 1)]
            for h in range(2):
                e = e0 + 2 * pair + h
                line = weights[0, e] * w[0] + weights[1, e] * w[1] + weights[2, e] * w[2]
                lines.append(line.reshape(lev_dev, 128))
        fine_part = dot_split(jnp.concatenate(lines, axis=0), 0)
        at = pl.ds(e0, span)
        total = misfit[at] + fine_part.reshape(span, lev_dev, 256)
        misfit[at] = total
        field_a[at] = sigma[...] * total
        back[at] = dot_split(total.reshape(span * lev_dev, 256), 1).reshape(span, lev_dev, 128)
        return carry

    lax.fori_loop(0, GROWN // span, interpolate, 0)

    def adjoint(r, carry):
        e = 2 * r + 2
        total = jnp.zeros((lev_dev // 8, 8, 128), F32)
        for j in range(6):
            total = total + weights[2 - j // 2, e + j] * back[e + j].reshape(lev_dev // 8, 8, 128)
        shares[lev, mine + r] = total.reshape(lev_dev, 128)
        return carry

    lax.fori_loop(0, ROWS, adjoint, 0, unroll=4)

    def to_all(rows, device):
        return remote(shares.at[lev, rows], shares.at[lev, rows], device)

    def x_part(ry, rx):
        return pl.ds(share(ry, rx), XROWS)

    pair_first = to_all(x_part(y, x), to_y)
    ring_y = [to_all(y_rows(x, "all"), to_right), to_all(y_rows(x, "all"), to_left)]
    ring_own = [to_all(x_part(y, x), to_right), to_all(x_part(y, x), to_left)]
    core = [to_all(pl.ds(mine, ROWS), to_core)]
    pair_y = [to_all(y_rows(x, "all"), to_y)]

    sweep(field_a, field_b)
    sweep(field_b, field_a, 0, 3)
    pair_first.wait_recv()
    ring_other = [to_all(x_part(other_y, x), to_right), to_all(x_part(other_y, x), to_left)]
    core.append(to_all(x_part(other_y, x), to_core))
    for copy in ring_y:
        copy.wait_recv()
    on_y = [
        to_all(y_rows(left, "a"), to_right),
        to_all(y_rows(right, "b"), to_left),
    ]
    for rx in (left, right):
        pair_y.append(to_all(y_rows(rx, "all"), to_y))
        core.append(to_all(y_rows(rx, "all"), to_core))

    sweep(field_b, field_a, 3, 7)
    for copy in ring_own:
        copy.wait_recv()
    on_x = [to_all(x_part(y, right), to_left)]
    for rx in (left, right):
        core.append(to_all(x_part(y, rx), to_core))
    sweep(field_a, field_b, 0, 3)
    for copy in on_y:
        copy.wait_recv()
    pair_y.append(to_all(y_rows(across, "all"), to_y))
    core.append(to_all(y_rows(across, "all"), to_core))
    sweep(field_a, field_b, 3, 7)
    for copy in ring_other:
        copy.wait_recv()
    on_x.append(to_all(x_part(other_y, left), to_right))
    for rx in (left, right):
        core.append(to_all(x_part(other_y, rx), to_core))

    def finish(i, carry):
        at = pl.ds(i, lev_dev, stride=own)
        for side in range(2):
            for number, value in ((0, field_b), (1, misfit)):
                planes(planes_out, number, side)[at, :] = (
                    planes(planes_in, number, side)[at, :] + value[EDGE + i, :, lanes[side]]
                )
        return carry

    lax.fori_loop(0, own, finish, 0, unroll=4)
    for rx, copy in zip((x, left, right), pair_y):
        copy.wait_recv()
        core.append(to_all(y_rows(rx, "all", other_y), to_core))
    on_x[0].wait_recv()
    core.append(to_all(x_part(y, across), to_core))
    pair_y[3].wait_recv()
    core.append(to_all(y_rows(across, "all", other_y), to_core))
    on_x[1].wait_recv()
    core.append(to_all(x_part(other_y, across), to_core))
    for copy in core:
        copy.wait_recv()
    waited = halo_sends[2:] + misfit_sends
    for copy in sent:
        if not any(copy is done for done in waited):
            copy.wait_send()


def exchange(sizes, lhs, count, amp, pert, control, innov, std, spread, land, row_index, row_weight, col_index, col_weight):
    members, modes, rows, cols = amp.shape
    levels = pert.shape[1]
    lev_dev, own, cols_fine = control.shape
    vmem = pl.BlockSpec(memory_space=pltpu.VMEM)
    anywhere = pl.BlockSpec(memory_space=pl.ANY)
    cell = (lev_dev, 128)
    row = (lev_dev, cols_fine)
    tile = (2, rows) + cell
    return pl.pallas_call(
        functools.partial(exchange_kernel, sizes),
        in_specs=[vmem] + [anywhere] * 12,
        out_specs=[vmem] * 5,
        out_shape=[
            pltpu.VMEM((members, modes, PITCH, cols), F32),
            pltpu.VMEM((members, levels, PITCH, cols), F32),
            pltpu.VMEM(tile, F32),
            pltpu.VMEM((2, 2, lev_dev, own, 128), F32),
            pltpu.VMEM(count.shape, jnp.int32),
        ],
        scratch_shapes=[
            pltpu.VMEM(tile, F32),
            pltpu.VMEM(pert.shape, BF16),
            pltpu.VMEM((rows,) + cell, F32),
            pltpu.VMEM((2, XROWS) + cell, F32),
            pltpu.VMEM((2, XROWS) + cell, F32),
            pltpu.VMEM((2, XROWS) + cell, F32),
            pltpu.VMEM((XROWS,) + cell, F32),
            pltpu.VMEM((4, YROWS) + cell, F32),
            pltpu.VMEM((2, YROWS - YA) + cell, F32),
            pltpu.VMEM((2, YROWS - YA) + cell, F32),
            pltpu.VMEM((2, YROWS - YA) + cell, F32),
            pltpu.VMEM((ROWS + 2 * HALO,) + cell, F32),
            pltpu.VMEM((GROWN,) + row, F32),
            pltpu.VMEM((GROWN,) + row, F32),
            pltpu.VMEM((GROWN,) + row, F32),
            pltpu.VMEM((GROWN, 8, cols_fine), F32),
            pltpu.VMEM((GROWN, 8, cols_fine), F32),
            pltpu.VMEM((GROWN, 8, cols_fine), F32),
            pltpu.VMEM((3, GROWN, 8, 128), F32),
            pltpu.VMEM(row, F32),
            pltpu.VMEM((2, 128, cols_fine), BF16),
            pltpu.VMEM((GROWN,) + cell, F32),
            pltpu.VMEM((2, 2, lev_dev, own, 128), F32),
            pltpu.SMEM(std.shape, F32),
            pltpu.VMEM(spread.shape, F32),
            pltpu.VMEM(land.shape, jnp.int32),
            pltpu.SMEM(row_index.shape, jnp.int32),
            pltpu.SMEM(row_weight.shape, F32),
            pltpu.VMEM((1, cols_fine), jnp.int32),
            pltpu.VMEM((1, cols_fine), F32),
            pltpu.SemaphoreType.DMA((80,)),
            pltpu.SemaphoreType.DMA((80,)),
            pltpu.SemaphoreType.DMA((2 * members + 4,)),
            pltpu.SemaphoreType.DMA((4,)),
            pltpu.SemaphoreType.DMA((8,)),
        ],
        compiler_params=pltpu.CompilerParams(
            collective_id=0, has_side_effects=True, vmem_limit_bytes=24 << 20
        ),
        name="exchange",
    )(
        lhs,
        *(
            pltpu.with_memory_space_constraint(operand, pltpu.HBM)
            for operand in (
                count,
                amp,
                pert,
                control,
                innov,
                std,
                spread,
                land,
                row_index,
                row_weight,
                col_index.reshape(1, cols_fine),
                col_weight.reshape(1, cols_fine),
            )
        ),
    )


def local(
    ens_pert,
    ens_control,
    eigen_modes,
    mode_count,
    row_index,
    row_weight,
    col_index,
    col_weight,
    static_control,
    static_std,
    diffusivity,
    land_mask,
    innovation,
):
    sizes = (
        lax.axis_size("coarse"),
        lax.axis_size("fine"),
        lax.axis_size("coarse") * lax.axis_size("fine") * row_index.shape[0],
    )
    scaled = eigen_modes * (1.0 / math.sqrt(MEMBERS - 1))
    tall, across = split_modes(scaled.T)
    amp, wide, coarse_grad, planes, count = exchange(
        sizes,
        tall,
        mode_count,
        ens_control,
        ens_pert,
        static_control,
        innovation,
        static_std,
        diffusivity,
        land_mask,
        row_index,
        row_weight,
        col_index,
        col_weight,
    )
    grad_ens, grad_static, increment = backward(
        across, count, amp, wide, coarse_grad, planes, mode_count.shape[0]
    )
    return increment, grad_static, grad_ens


def solution(mesh):
    in_specs = (
        P(("fine", "lev"), None, "coarse", None),
        P(("fine", "lev"), None, "coarse", None),
        P(),
        P("coarse", None),
        P(("coarse", "fine")),
        P(("coarse", "fine")),
        P(),
        P(),
        P("lev", ("coarse", "fine"), None),
        P("lev"),
        P(("coarse", "fine"), None),
        P(("coarse", "fine"), None),
        P("lev", ("coarse", "fine"), None),
    )
    out_specs = (
        P("lev", ("coarse", "fine"), None),
        P("lev", ("coarse", "fine"), None),
        P(("fine", "lev"), None, "coarse", None),
    )
    return jax.shard_map(local, mesh=mesh, in_specs=in_specs, out_specs=out_specs, check_vma=False)
```

```python
import functools
import math

import jax
import jax.numpy as jnp
from jax import lax
from jax.experimental import pallas as pl
from jax.experimental.pallas import tpu as pltpu
from jax.sharding import PartitionSpec as P

MEMBERS = 80
NSWEEP = 3
HALO = 3
EDGE = 4
GROWN = 32
ROWS = 12
XROWS = 5
YROWS = ROWS - XROWS
PITCH = 104
PIECE = 24
F32 = jnp.float32
BF16 = jnp.bfloat16


def halves(value):
    hi = value.astype(BF16)
    return hi, (value - hi.astype(F32)).astype(BF16)


def stacked(value):
    hi, lo = halves(value)
    return jnp.concatenate([hi, hi, lo], axis=0)


def split_modes(matrix):
    hi = lax.reduce_precision(matrix, 8, 7)
    lo = matrix - hi
    wide = jnp.concatenate([hi, lo, hi], axis=1).astype(BF16)
    tall = jnp.concatenate([hi, lo, hi], axis=0).astype(BF16)
    return tall.T, wide


def backward_kernel(
    lhs_ref,
    count_ref,
    amp_ref,
    wide_ref,
    grad_ref,
    planes_ref,
    out_ref,
    grad_static_ref,
    inc_ref,
    result,
    out_sem,
    plane_sem,
):
    members, modes = amp_ref.shape[:2]
    levels = wide_ref.shape[1]
    rows = out_ref.shape[2]
    plane_out = [
        pltpu.make_async_copy(
            planes_ref.at[number, side],
            ref.at[:, :, pl.ds(128 * side, 128)],
            plane_sem.at[2 * number + side],
        )
        for number, ref in enumerate((grad_static_ref, inc_ref))
        for side in range(2)
    ]
    for copy in plane_out:
        copy.start()
    amps = amp_ref.reshape(members * modes * PITCH, 128)
    perts = wide_ref.reshape(members * levels * PITCH, 128)
    outs = result.reshape(members * modes * PITCH, 128)
    lhs = lhs_ref[...]
    mode = lax.broadcasted_iota(jnp.int32, (modes, 128), 0)
    pieces = []
    for piece in range(rows // PIECE):

        def row_pair(step, carry):
            first = piece * PIECE + step * 2
            keep = [mode < count_ref[pl.ds(first + h, 1), :] for h in range(2)]
            grad = [
                jnp.concatenate([grad_ref[0, first + h], grad_ref[1, first + h]], axis=0)
                for h in range(2)
            ]
            for k in range(members):
                rhs = []
                for h in range(2):
                    pert = perts[pl.ds(k * levels * PITCH + first + h, levels, stride=PITCH), :]
                    rhs.append(stacked(pert * grad[h]))
                proj = jnp.dot(lhs, jnp.concatenate(rhs, axis=1), preferred_element_type=F32)
                for h in range(2):
                    at = pl.ds(k * modes * PITCH + first + h, modes, stride=PITCH)
                    outs[at, :] = amps[at, :] + jnp.where(
                        keep[h], proj[:, h * 128 : (h + 1) * 128], 0.0
                    )
            return carry

        lax.fori_loop(0, PIECE // 2, row_pair, 0, unroll=4)
        at = pl.ds(piece * PIECE, PIECE)
        copy = pltpu.make_async_copy(
            result.at[:, :, at, :], out_ref.at[:, :, at, :], out_sem.at[piece]
        )
        copy.start()
        pieces.append(copy)
    for copy in plane_out + pieces:
        copy.wait()


def backward(lhs, count, amp, wide, grad, planes, rows):
    members, modes, _, cols = amp.shape
    lev_dev, own = planes.shape[2:4]
    vmem = pl.BlockSpec(memory_space=pltpu.VMEM)
    anywhere = pl.BlockSpec(memory_space=pl.ANY)
    field = jax.ShapeDtypeStruct((lev_dev, own, 2 * cols), F32)
    return pl.pallas_call(
        backward_kernel,
        in_specs=[vmem] * 6,
        out_specs=[anywhere] * 3,
        out_shape=[jax.ShapeDtypeStruct((members, modes, rows, cols), F32), field, field],
        scratch_shapes=[
            pltpu.VMEM(amp.shape, F32),
            pltpu.SemaphoreType.DMA((rows // PIECE,)),
            pltpu.SemaphoreType.DMA((4,)),
        ],
        compiler_params=pltpu.CompilerParams(vmem_limit_bytes=12 << 20),
        name="backward_modes",
    )(lhs, count, amp, wide, grad, planes)


def exchange_kernel(
    sizes,
    lhs_ref,
    count_in,
    amp_ref,
    pert_ref,
    control_ref,
    innov_ref,
    std_in,
    spread_in,
    land_in,
    row_index_in,
    row_weight_in,
    col_index_in,
    col_weight_in,
    amp_out,
    wide,
    shares,
    planes_out,
    count_ref,
    tile,
    narrow,
    core_in,
    x_in,
    pair_x_in,
    pair_y_in,
    y_in,
    window,
    field_a,
    field_b,
    misfit,
    cells,
    row_faces,
    col_faces,
    weights,
    sigma,
    col_mat,
    back,
    planes_in,
    std_ref,
    spread_ref,
    land_ref,
    row_index_ref,
    row_weight_ref,
    col_index_ref,
    col_weight_ref,
    send_sem,
    recv_sem,
    load_sem,
    plane_sem,
    small_sem,
):
    coarse_count, fine_count, rows_all = sizes
    xs = fine_count // 2
    coarse = lax.axis_index("coarse")
    fine = lax.axis_index("fine")
    lev = lax.axis_index("lev")
    x = lax.rem(fine, xs)
    y = fine // xs
    right, left, across = lax.rem(x + 1, xs), lax.rem(x + xs - 1, xs), lax.rem(x + 2, xs)
    other_y = 1 - y
    serial = coarse * fine_count + fine
    count = coarse_count * fine_count
    after, before = lax.rem(serial + 1, count), lax.rem(serial + count - 1, count)
    first_row = serial * 2 * ROWS
    members, modes = amp_ref.shape[:2]
    levels = pert_ref.shape[1]
    sums = tile.at[lev]

    to_core = (coarse, fine, 1 - lev)
    to_right = (coarse, y * xs + right, lev)
    to_left = (coarse, y * xs + left, lev)
    to_across = (coarse, y * xs + across, lev)
    to_y = (coarse, other_y * xs + x, lev)
    to_after = (after // fine_count, lax.rem(after, fine_count), lev)
    to_before = (before // fine_count, lax.rem(before, fine_count), lev)

    barrier = pltpu.get_barrier_semaphore()
    for device in (to_core, to_right, to_left, to_across, to_y, to_after, to_before):
        pl.semaphore_signal(barrier, inc=1, device_id=device, device_id_type=pl.DeviceIdType.MESH)

    numbers = iter(range(100))
    sent = []

    def remote(src, dst, device):
        number = next(numbers)
        copy = pltpu.make_async_remote_copy(
            src_ref=src,
            dst_ref=dst,
            send_sem=send_sem.at[number],
            recv_sem=recv_sem.at[number],
            device_id=device,
            device_id_type=pl.DeviceIdType.MESH,
        )
        copy.start()
        sent.append(copy)
        return copy

    def share(ry, rx):
        return (ry * xs + rx) * ROWS

    lev_dev = control_ref.shape[0]
    own = 2 * ROWS
    half_rows = xs * ROWS
    lanes = [pl.ds(0, 128), pl.ds(128, 128)]

    count_load = pltpu.make_async_copy(count_in, count_ref, small_sem.at[7])
    count_load.start()
    pert_in, amp_in = [], []

    def load_half(half):
        at = pl.ds(pl.multiple_of((other_y, y)[half] * half_rows, 16), half_rows)
        for k in range(members):
            copy = pltpu.make_async_copy(
                pert_ref.at[k, :, at, :], narrow.at[k, :, at, :], load_sem.at[half * members + k]
            )
            copy.start()
            pert_in.append(copy)
        for part in (0, 1):
            column = lax.rem(across // 2 + part, 2)
            start = (other_y, y)[half] * half_rows + column * PIECE
            at = pl.ds(pl.multiple_of(start, PIECE), PIECE)
            copy = pltpu.make_async_copy(
                amp_ref.at[:, :, at, :],
                amp_out.at[:, :, at, :],
                load_sem.at[2 * members + 2 * half + part],
            )
            copy.start()
            amp_in.append(copy)

    load_half(0)
    plane_in = [
        [
            pltpu.make_async_copy(
                ref.at[:, :, lanes[side]],
                planes_in.at[number, side],
                plane_sem.at[2 * number + side],
            )
            for side in range(2)
        ]
        for number, ref in enumerate((control_ref, innov_ref))
    ]
    small_in = [
        pltpu.make_async_copy(src, dst, small_sem.at[number])
        for number, (src, dst) in enumerate(
            (
                (spread_in, spread_ref),
                (land_in, land_ref),
                (row_index_in, row_index_ref),
                (row_weight_in, row_weight_ref),
                (std_in, std_ref),
                (col_index_in, col_index_ref),
                (col_weight_in, col_weight_ref),
            )
        )
    ]
    for copy in small_in + plane_in[0]:
        copy.start()
    load_half(1)
    for copy in plane_in[1]:
        copy.start()

    def planes(ref, number, side):
        return ref.at[number, side].reshape(lev_dev * own, 128)

    def widen(half):
        at = pl.ds(pl.multiple_of((other_y, y)[half] * half_rows, 16), half_rows)
        for k in range(members):
            pert_in[half * members + k].wait()

            def widen_level(level, carry):
                wide[k, level, at] = narrow[k, level, at].astype(F32)
                return carry

            lax.fori_loop(0, levels, widen_level, 0, unroll=8)

    def x_rows(ry, rx):
        return pl.ds(share(ry, rx), XROWS)

    def y_rows(ry, rx):
        return pl.ds(share(ry, rx) + XROWS, YROWS)

    def add(rows, *terms):
        total = sums[rows]
        for term in terms:
            total = total + term[...]
        sums[rows] = total

    amps = amp_out.reshape(members * modes * PITCH, 128)
    perts = wide.reshape(members * levels * PITCH, 128)
    lhs = lhs_ref[...]
    mode = lax.broadcasted_iota(jnp.int32, (modes, 128), 0)

    def contract(start):
        def row_pair(step, carry):
            first = start + step * 2
            keep = [mode < count_ref[pl.ds(first + h, 1), :] for h in range(2)]
            total = [jnp.zeros((levels, 128), F32) for _ in range(2)]
            for k in range(members):
                rhs = []
                for h in range(2):
                    amp = amps[pl.ds(k * modes * PITCH + first + h, modes, stride=PITCH), :]
                    rhs.append(stacked(jnp.where(keep[h], amp, 0.0)))
                level_amp = jnp.dot(lhs, jnp.concatenate(rhs, axis=1), preferred_element_type=F32)
                for h in range(2):
                    pert = perts[pl.ds(k * levels * PITCH + first + h, levels, stride=PITCH), :]
                    total[h] = total[h] + pert * level_amp[:, h * 128 : (h + 1) * 128]
            for h in range(2):
                tile[0, first + h] = total[h][: levels // 2]
                tile[1, first + h] = total[h][levels // 2 :]
            return carry

        lax.fori_loop(0, ROWS // 2, row_pair, 0, unroll=3)

    order = [(ry, rx) for ry in (other_y, y) for rx in (across, right, left, x)]
    ring = ((across, to_across), (right, to_right), (left, to_left))
    origins = (across, left, right)
    core_sends = []
    to_ring = [[], []]
    to_pair = []
    to_own = []

    def produce(number):
        contract(share(*order[number]))

    def send_core(number):
        rows = pl.ds(share(*order[number]), ROWS)
        core_sends.append(remote(tile.at[1 - lev, rows], core_in.at[rows], to_core))

    def settle(number):
        core_sends[number].wait_recv()
        rows = pl.ds(share(*order[number]), ROWS)
        add(rows, core_in.at[rows])
        half, place = number // 4, number % 4
        if place < 3:
            rx, device = ring[place]
            to_ring[half].append(
                remote(sums.at[x_rows(*order[number])], x_in.at[half, place], device)
            )
        if half == 0:
            rx = order[number][1]
            to_pair.append(remote(sums.at[y_rows(other_y, rx)], pair_y_in.at[place], to_y))

    def settle_pair(place):
        to_pair[place].wait_recv()
        rx = order[place][1]
        add(y_rows(y, rx), pair_y_in.at[place])
        if place < 3:
            to_own.append(remote(sums.at[y_rows(y, rx)], y_in.at[place], ring[place][1]))

    count_load.wait()
    widen(0)
    amp_in[0].wait()
    produce(0)
    pl.semaphore_wait(barrier, 7)
    send_core(0)
    amp_in[1].wait()
    produce(1)
    send_core(1)
    produce(2)
    send_core(2)
    settle(0)
    produce(3)
    send_core(3)
    settle(1)
    settle(2)

    for copy in small_in + plane_in[0]:
        copy.wait()

    def load_rows(i, carry):
        for side in range(2):
            field_a[EDGE + i, :, lanes[side]] = planes(planes_in, 0, side)[
                pl.ds(i, lev_dev, stride=own), :
            ]
        sub = lax.broadcasted_iota(jnp.int32, (8, 256), 0)
        weight = jnp.full((8, 256), row_weight_ref[i], F32)
        index = jnp.full((8, 256), row_index_ref[i], jnp.int32)
        upper = (index == (first_row + i) // 2).astype(F32)
        spread = jnp.broadcast_to(spread_ref[pl.ds(i, 1), :], (8, 256))
        land = jnp.broadcast_to(land_ref[pl.ds(i, 1), :], (8, 256)).astype(F32)
        cells[EDGE + i] = jnp.where(
            sub == 0, spread, jnp.where(sub == 1, land, jnp.where(sub == 2, weight, upper))
        )
        return carry

    lax.fori_loop(0, own, load_rows, 0, unroll=4)
    top, bottom = pl.ds(EDGE, HALO), pl.ds(EDGE + own - HALO, HALO)
    low, high = pl.ds(EDGE - HALO, HALO), pl.ds(EDGE + own, HALO)
    halo_sends = [
        remote(ref.at[src], ref.at[dst], device)
        for ref in (cells, field_a)
        for src, dst, device in ((top, high, to_before), (bottom, low, to_after))
    ]
    settle(3)

    widen(1)
    amp_in[2].wait()
    produce(4)
    send_core(4)
    amp_in[3].wait()
    produce(5)
    send_core(5)
    settle(4)
    settle_pair(0)
    produce(6)
    send_core(6)
    settle(5)
    produce(7)
    send_core(7)
    settle(6)
    settle_pair(1)
    for copy in to_ring[0]:
        copy.wait_recv()
    add(x_rows(other_y, x), x_in.at[0, 0], x_in.at[0, 1], x_in.at[0, 2])
    pair_x = remote(sums.at[x_rows(other_y, x)], pair_x_in, to_y)

    for ref in (cells, misfit):
        ref[0] = jnp.zeros(ref.shape[1:], F32)
        ref[GROWN - 1] = jnp.zeros(ref.shape[1:], F32)
    for row in (1, GROWN - 2):
        field_b[row] = jnp.zeros(field_b.shape[1:], F32)
    for lev_at in range(lev_dev):
        sigma[lev_at : lev_at + 1, :] = jnp.full((1, 256), std_ref[lev_at], F32)
    for copy in halo_sends[:2]:
        copy.wait_recv()

    def coefficients(e, carry):
        here, there = cells[e], cells[e + 1]
        line = first_row - EDGE + e
        inside = (line >= 0) & (line < rows_all) & (e >= 1) & (e <= GROWN - 2)
        facing = (line >= 0) & (line + 1 < rows_all)
        inside = jnp.where(inside, 1.0, 0.0).astype(F32)
        facing = jnp.where(facing, 1.0, 0.0).astype(F32)
        lane = lax.broadcasted_iota(jnp.int32, (8, 256), 1)
        spread, land = (jnp.broadcast_to(here[j : j + 1], (8, 256)) for j in (0, 1))
        spread_next, land_next = (jnp.broadcast_to(there[j : j + 1], (8, 256)) for j in (0, 1))
        row_faces[e] = (
            jnp.sqrt(spread * spread_next) * (1.0 - 0.5 * jnp.abs(land - land_next)) * facing
        )
        spread_right, land_right = (pltpu.roll(v, 255, 1) for v in (spread, land))
        col_faces[e] = jnp.where(
            lane < 255,
            jnp.sqrt(spread * spread_right) * (1.0 - 0.5 * jnp.abs(land - land_right)),
            0.0,
        )
        weight, upper = (jnp.broadcast_to(here[j : j + 1, :128], (8, 128)) for j in (2, 3))
        upper_on = upper > 0.5
        weights[0, e] = jnp.where(upper_on, 0.0, 1.0 - weight) * inside
        weights[1, e] = jnp.where(upper_on, 1.0 - weight, weight) * inside
        weights[2, e] = jnp.where(upper_on, weight, 0.0) * inside
        return carry

    lax.fori_loop(0, GROWN - 1, coefficients, 0, unroll=4)
    for j in range(3):
        weights[j, GROWN - 1] = jnp.zeros((8, 128), F32)
    col = lax.broadcasted_iota(jnp.int32, (128, 256), 0)
    col_at, col_w = col_index_ref[...], col_weight_ref[...]
    matrix = jnp.where(col == col_at, 1.0 - col_w, jnp.where(col == col_at + 1, col_w, 0.0))
    hi, lo = halves(matrix)
    col_mat[0], col_mat[1] = hi, lo

    def sweep(src, dst, first=0, last=7):
        def rows_of_four(step, carry):
            e = EDGE - 2 + 4 * step
            down = row_faces[pl.ds(e - 1, 5)]
            side = col_faces[pl.ds(e, 4)]
            for tile_at in range(lev_dev // 8):
                at = pl.ds(8 * tile_at, 8)
                v = src[pl.ds(e - 1, 6), at, :]
                mid = v[1:5]
                flux = down * (v[1:] - v[:-1])
                cross = side * (pltpu.roll(mid, 255, 2) - mid)
                dst[pl.ds(e, 4), at, :] = (
                    mid + (flux[1:] - flux[:-1]) + (cross - pltpu.roll(cross, 1, 2))
                )
            return carry

        lax.fori_loop(first, last, rows_of_four, 0)

    settle_pair(2)
    settle(7)
    for copy in halo_sends[2:]:
        copy.wait_recv()
        copy.wait_send()
    sweep(field_a, field_b)
    sweep(field_b, field_a)
    settle_pair(3)
    for copy in to_ring[1]:
        copy.wait_recv()
    add(x_rows(y, x), x_in.at[1, 0], x_in.at[1, 1], x_in.at[1, 2])
    sweep(field_a, field_b)

    for copy in to_own:
        copy.wait_recv()
    mine = share(y, x)
    window[pl.ds(HALO + XROWS, YROWS)] = sums[y_rows(y, x)] + y_in[0] + (y_in[1] + y_in[2])
    pair_x.wait_recv()
    window[pl.ds(HALO, XROWS)] = sums[x_rows(y, x)] + pair_x_in[...]
    halo_again = [
        remote(window.at[pl.ds(ROWS, HALO)], window.at[pl.ds(0, HALO)], to_after),
        remote(window.at[pl.ds(HALO, HALO)], window.at[pl.ds(HALO + ROWS, HALO)], to_before),
    ]

    def static_part(i, carry):
        for side in range(2):
            cols = lanes[side]
            misfit[EDGE + i, :, cols] = (
                sigma[:, cols] * field_b[EDGE + i, :, cols]
                - planes(planes_in, 1, side)[pl.ds(i, lev_dev, stride=own), :]
            )
        return carry

    for copy in plane_in[1]:
        copy.wait()
    lax.fori_loop(0, own, static_part, 0, unroll=4)
    halo_again += [
        remote(misfit.at[top], misfit.at[high], to_before),
        remote(misfit.at[bottom], misfit.at[low], to_after),
    ]

    def dot_split(lhs, which):
        hi, lo = halves(lhs)
        c_hi, c_lo = col_mat[0], col_mat[1]
        dims = (((1,), (which,)), ((), ()))
        dot = functools.partial(lax.dot_general, dimension_numbers=dims, preferred_element_type=F32)
        return dot(hi, c_hi) + (dot(lo, c_hi) + dot(hi, c_lo))

    span = 8

    def interpolate(step, carry):
        e0 = step * span
        lines = []
        for pair in range(span // 2):
            t = step * (span // 2) + pair + 1
            w = [window[t + d].reshape(lev_dev // 8, 8, 128) for d in (-1, 0, 1)]
            for h in range(2):
                e = e0 + 2 * pair + h
                line = weights[0, e] * w[0] + weights[1, e] * w[1] + weights[2, e] * w[2]
                lines.append(line.reshape(lev_dev, 128))
        fine_part = dot_split(jnp.concatenate(lines, axis=0), 0)
        at = pl.ds(e0, span)
        total = misfit[at] + fine_part.reshape(span, lev_dev, 256)
        misfit[at] = total
        field_a[at] = sigma[...] * total
        back[at] = dot_split(total.reshape(span * lev_dev, 256), 1).reshape(span, lev_dev, 128)
        return carry

    lax.fori_loop(1, 3, interpolate, 0)
    for copy in halo_again:
        copy.wait_recv()
    for copy in halo_again[2:]:
        copy.wait_send()
    interpolate(0, 0)
    interpolate(3, 0)

    def adjoint(r, carry):
        e = 2 * r + 2
        total = jnp.zeros((lev_dev // 8, 8, 128), F32)
        for j in range(6):
            total = total + weights[2 - j // 2, e + j] * back[e + j].reshape(lev_dev // 8, 8, 128)
        shares[lev, mine + r] = total.reshape(lev_dev, 128)
        return carry

    lax.fori_loop(0, ROWS, adjoint, 0, unroll=4)

    def to_all(rows, device):
        return remote(shares.at[lev, rows], shares.at[lev, rows], device)

    def to_ring_of(rows):
        return [to_all(rows, device) for _, device in ring]

    pair_first = to_all(x_rows(y, x), to_y)
    ring_y = to_ring_of(y_rows(y, x))
    pair_y = [to_all(y_rows(y, x), to_y)]
    ring_own = to_ring_of(x_rows(y, x))
    core = [to_all(pl.ds(mine, ROWS), to_core)]

    sweep(field_a, field_b)
    sweep(field_b, field_a, 0, 3)
    pair_first.wait_recv()
    ring_other = to_ring_of(x_rows(other_y, x))
    core.append(to_all(x_rows(other_y, x), to_core))
    for copy, rx in zip(ring_y, origins):
        copy.wait_recv()
        pair_y.append(to_all(y_rows(y, rx), to_y))
        core.append(to_all(y_rows(y, rx), to_core))
    sweep(field_b, field_a, 3, 7)
    sweep(field_a, field_b, 0, 3)
    for copy, rx in zip(ring_own, origins):
        copy.wait_recv()
        core.append(to_all(x_rows(y, rx), to_core))
    pair_y[0].wait_recv()
    core.append(to_all(y_rows(other_y, x), to_core))
    sweep(field_a, field_b, 3, 7)

    def finish(i, carry):
        at = pl.ds(i, lev_dev, stride=own)
        for side in range(2):
            for number, value in ((0, field_b), (1, misfit)):
                planes(planes_out, number, side)[at, :] = (
                    planes(planes_in, number, side)[at, :] + value[EDGE + i, :, lanes[side]]
                )
        return carry

    lax.fori_loop(0, own, finish, 0, unroll=4)
    for copy, rx in zip(pair_y[1:], origins):
        copy.wait_recv()
        core.append(to_all(y_rows(other_y, rx), to_core))
    for copy, rx in zip(ring_other, origins):
        copy.wait_recv()
        core.append(to_all(x_rows(other_y, rx), to_core))
    for copy in core:
        copy.wait_recv()
    waited = halo_sends[2:] + halo_again[2:]
    for copy in sent:
        if not any(copy is done for done in waited):
            copy.wait_send()


def exchange(sizes, lhs, count, amp, pert, control, innov, std, spread, land, row_index, row_weight, col_index, col_weight):
    members, modes, rows, cols = amp.shape
    levels = pert.shape[1]
    lev_dev, own, cols_fine = control.shape
    vmem = pl.BlockSpec(memory_space=pltpu.VMEM)
    anywhere = pl.BlockSpec(memory_space=pl.ANY)
    cell = (lev_dev, 128)
    row = (lev_dev, cols_fine)
    tile = (2, rows) + cell
    return pl.pallas_call(
        functools.partial(exchange_kernel, sizes),
        in_specs=[vmem] + [anywhere] * 12,
        out_specs=[vmem] * 5,
        out_shape=[
            pltpu.VMEM((members, modes, PITCH, cols), F32),
            pltpu.VMEM((members, levels, PITCH, cols), F32),
            pltpu.VMEM(tile, F32),
            pltpu.VMEM((2, 2, lev_dev, own, 128), F32),
            pltpu.VMEM(count.shape, jnp.int32),
        ],
        scratch_shapes=[
            pltpu.VMEM(tile, F32),
            pltpu.VMEM(pert.shape, BF16),
            pltpu.VMEM((rows,) + cell, F32),
            pltpu.VMEM((2, 3, XROWS) + cell, F32),
            pltpu.VMEM((XROWS,) + cell, F32),
            pltpu.VMEM((4, YROWS) + cell, F32),
            pltpu.VMEM((3, YROWS) + cell, F32),
            pltpu.VMEM((ROWS + 2 * HALO,) + cell, F32),
            pltpu.VMEM((GROWN,) + row, F32),
            pltpu.VMEM((GROWN,) + row, F32),
            pltpu.VMEM((GROWN,) + row, F32),
            pltpu.VMEM((GROWN, 8, cols_fine), F32),
            pltpu.VMEM((GROWN, 8, cols_fine), F32),
            pltpu.VMEM((GROWN, 8, cols_fine), F32),
            pltpu.VMEM((3, GROWN, 8, 128), F32),
            pltpu.VMEM(row, F32),
            pltpu.VMEM((2, 128, cols_fine), BF16),
            pltpu.VMEM((GROWN,) + cell, F32),
            pltpu.VMEM((2, 2, lev_dev, own, 128), F32),
            pltpu.SMEM(std.shape, F32),
            pltpu.VMEM(spread.shape, F32),
            pltpu.VMEM(land.shape, jnp.int32),
            pltpu.SMEM(row_index.shape, jnp.int32),
            pltpu.SMEM(row_weight.shape, F32),
            pltpu.VMEM((1, cols_fine), jnp.int32),
            pltpu.VMEM((1, cols_fine), F32),
            pltpu.SemaphoreType.DMA((80,)),
            pltpu.SemaphoreType.DMA((80,)),
            pltpu.SemaphoreType.DMA((2 * members + 4,)),
            pltpu.SemaphoreType.DMA((4,)),
            pltpu.SemaphoreType.DMA((8,)),
        ],
        compiler_params=pltpu.CompilerParams(
            collective_id=0, has_side_effects=True, vmem_limit_bytes=24 << 20
        ),
        name="exchange",
    )(
        lhs,
        *(
            pltpu.with_memory_space_constraint(operand, pltpu.HBM)
            for operand in (
                count,
                amp,
                pert,
                control,
                innov,
                std,
                spread,
                land,
                row_index,
                row_weight,
                col_index.reshape(1, cols_fine),
                col_weight.reshape(1, cols_fine),
            )
        ),
    )


def local(
    ens_pert,
    ens_control,
    eigen_modes,
    mode_count,
    row_index,
    row_weight,
    col_index,
    col_weight,
    static_control,
    static_std,
    diffusivity,
    land_mask,
    innovation,
):
    sizes = (
        lax.axis_size("coarse"),
        lax.axis_size("fine"),
        lax.axis_size("coarse") * lax.axis_size("fine") * row_index.shape[0],
    )
    scaled = eigen_modes * (1.0 / math.sqrt(MEMBERS - 1))
    tall, across = split_modes(scaled.T)
    amp, wide, coarse_grad, planes, count = exchange(
        sizes,
        tall,
        mode_count,
        ens_control,
        ens_pert,
        static_control,
        innovation,
        static_std,
        diffusivity,
        land_mask,
        row_index,
        row_weight,
        col_index,
        col_weight,
    )
    grad_ens, grad_static, increment = backward(
        across, count, amp, wide, coarse_grad, planes, mode_count.shape[0]
    )
    return increment, grad_static, grad_ens


def solution(mesh):
    in_specs = (
        P(("fine", "lev"), None, "coarse", None),
        P(("fine", "lev"), None, "coarse", None),
        P(),
        P("coarse", None),
        P(("coarse", "fine")),
        P(("coarse", "fine")),
        P(),
        P(),
        P("lev", ("coarse", "fine"), None),
        P("lev"),
        P(("coarse", "fine"), None),
        P(("coarse", "fine"), None),
        P("lev", ("coarse", "fine"), None),
    )
    out_specs = (
        P("lev", ("coarse", "fine"), None),
        P("lev", ("coarse", "fine"), None),
        P(("fine", "lev"), None, "coarse", None),
    )
    return jax.shard_map(local, mesh=mesh, in_specs=in_specs, out_specs=out_specs, check_vma=False)
```

```python
import functools
import math

import jax
import jax.numpy as jnp
from jax import lax
from jax.experimental import pallas as pl
from jax.experimental.pallas import tpu as pltpu
from jax.sharding import PartitionSpec as P

MEMBERS = 80
NSWEEP = 3
HALO = 3
EDGE = 4
GROWN = 32
ROWS = 12
XROWS = 5
YROWS = ROWS - XROWS
PITCH = 104
PIECE = 24
F32 = jnp.float32
BF16 = jnp.bfloat16


def halves(value):
    hi = value.astype(BF16)
    return hi, (value - hi.astype(F32)).astype(BF16)


def stacked(value):
    hi, lo = halves(value)
    return jnp.concatenate([hi, hi, lo], axis=0)


def split_modes(matrix):
    hi = lax.reduce_precision(matrix, 8, 7)
    lo = matrix - hi
    wide = jnp.concatenate([hi, lo, hi], axis=1).astype(BF16)
    tall = jnp.concatenate([hi, lo, hi], axis=0).astype(BF16)
    return tall.T, wide


def backward_kernel(
    lhs_ref,
    count_ref,
    amp_ref,
    wide_ref,
    grad_ref,
    planes_ref,
    out_ref,
    grad_static_ref,
    inc_ref,
    result,
    out_sem,
    plane_sem,
):
    members, modes = amp_ref.shape[:2]
    levels = wide_ref.shape[1]
    rows = out_ref.shape[2]
    plane_out = [
        pltpu.make_async_copy(
            planes_ref.at[number, side],
            ref.at[:, :, pl.ds(128 * side, 128)],
            plane_sem.at[2 * number + side],
        )
        for number, ref in enumerate((grad_static_ref, inc_ref))
        for side in range(2)
    ]
    for copy in plane_out:
        copy.start()
    amps = amp_ref.reshape(members * modes * PITCH, 128)
    perts = wide_ref.reshape(members * levels * PITCH, 128)
    outs = result.reshape(members * modes * PITCH, 128)
    lhs = lhs_ref[...]
    mode = lax.broadcasted_iota(jnp.int32, (modes, 128), 0)
    pieces = []
    for piece in range(rows // PIECE):

        def row_pair(step, carry):
            first = piece * PIECE + step * 2
            keep = [mode < count_ref[pl.ds(first + h, 1), :] for h in range(2)]
            grad = [
                jnp.concatenate([grad_ref[0, first + h], grad_ref[1, first + h]], axis=0)
                for h in range(2)
            ]
            for k in range(members):
                rhs = []
                for h in range(2):
                    pert = perts[pl.ds(k * levels * PITCH + first + h, levels, stride=PITCH), :]
                    rhs.append(stacked(pert * grad[h]))
                proj = jnp.dot(lhs, jnp.concatenate(rhs, axis=1), preferred_element_type=F32)
                for h in range(2):
                    at = pl.ds(k * modes * PITCH + first + h, modes, stride=PITCH)
                    outs[at, :] = amps[at, :] + jnp.where(
                        keep[h], proj[:, h * 128 : (h + 1) * 128], 0.0
                    )
            return carry

        lax.fori_loop(0, PIECE // 2, row_pair, 0, unroll=4)
        at = pl.ds(piece * PIECE, PIECE)
        copy = pltpu.make_async_copy(
            result.at[:, :, at, :], out_ref.at[:, :, at, :], out_sem.at[piece]
        )
        copy.start()
        pieces.append(copy)
    for copy in plane_out + pieces:
        copy.wait()


def backward(lhs, count, amp, wide, grad, planes, rows):
    members, modes, _, cols = amp.shape
    lev_dev, own = planes.shape[2:4]
    vmem = pl.BlockSpec(memory_space=pltpu.VMEM)
    anywhere = pl.BlockSpec(memory_space=pl.ANY)
    field = jax.ShapeDtypeStruct((lev_dev, own, 2 * cols), F32)
    return pl.pallas_call(
        backward_kernel,
        in_specs=[vmem] * 6,
        out_specs=[anywhere] * 3,
        out_shape=[jax.ShapeDtypeStruct((members, modes, rows, cols), F32), field, field],
        scratch_shapes=[
            pltpu.VMEM(amp.shape, F32),
            pltpu.SemaphoreType.DMA((rows // PIECE,)),
            pltpu.SemaphoreType.DMA((4,)),
        ],
        compiler_params=pltpu.CompilerParams(vmem_limit_bytes=12 << 20),
        name="backward_modes",
    )(lhs, count, amp, wide, grad, planes)


def exchange_kernel(
    sizes,
    lhs_ref,
    count_in,
    amp_ref,
    pert_ref,
    control_ref,
    innov_ref,
    std_in,
    spread_in,
    land_in,
    row_index_in,
    row_weight_in,
    col_index_in,
    col_weight_in,
    amp_out,
    wide,
    shares,
    planes_out,
    count_ref,
    tile,
    narrow,
    core_in,
    x_in,
    pair_x_in,
    pair_y_in,
    y_in,
    window,
    field_a,
    field_b,
    misfit,
    cells,
    row_faces,
    col_faces,
    centre,
    weights,
    sigma,
    col_mat,
    back,
    planes_in,
    std_ref,
    spread_ref,
    land_ref,
    row_index_ref,
    row_weight_ref,
    col_index_ref,
    col_weight_ref,
    send_sem,
    recv_sem,
    load_sem,
    plane_sem,
    small_sem,
):
    coarse_count, fine_count, rows_all = sizes
    xs = fine_count // 2
    coarse = lax.axis_index("coarse")
    fine = lax.axis_index("fine")
    lev = lax.axis_index("lev")
    x = lax.rem(fine, xs)
    y = fine // xs
    right, left, across = lax.rem(x + 1, xs), lax.rem(x + xs - 1, xs), lax.rem(x + 2, xs)
    other_y = 1 - y
    serial = coarse * fine_count + fine
    count = coarse_count * fine_count
    after, before = lax.rem(serial + 1, count), lax.rem(serial + count - 1, count)
    first_row = serial * 2 * ROWS
    members, modes = amp_ref.shape[:2]
    levels = pert_ref.shape[1]
    sums = tile.at[lev]

    to_core = (coarse, fine, 1 - lev)
    to_right = (coarse, y * xs + right, lev)
    to_left = (coarse, y * xs + left, lev)
    to_across = (coarse, y * xs + across, lev)
    to_y = (coarse, other_y * xs + x, lev)
    to_after = (after // fine_count, lax.rem(after, fine_count), lev)
    to_before = (before // fine_count, lax.rem(before, fine_count), lev)

    barrier = pltpu.get_barrier_semaphore()
    for device in (to_core, to_right, to_left, to_across, to_y, to_after, to_before):
        pl.semaphore_signal(barrier, inc=1, device_id=device, device_id_type=pl.DeviceIdType.MESH)

    numbers = iter(range(100))
    sent = []

    def remote(src, dst, device):
        number = next(numbers)
        copy = pltpu.make_async_remote_copy(
            src_ref=src,
            dst_ref=dst,
            send_sem=send_sem.at[number],
            recv_sem=recv_sem.at[number],
            device_id=device,
            device_id_type=pl.DeviceIdType.MESH,
        )
        copy.start()
        sent.append(copy)
        return copy

    def share(ry, rx):
        return (ry * xs + rx) * ROWS

    lev_dev = control_ref.shape[0]
    own = 2 * ROWS
    half_rows = xs * ROWS
    lanes = [pl.ds(0, 128), pl.ds(128, 128)]

    count_load = pltpu.make_async_copy(count_in, count_ref, small_sem.at[7])
    count_load.start()
    pert_in, amp_in = [], []

    def load_half(half):
        at = pl.ds(pl.multiple_of((other_y, y)[half] * half_rows, 16), half_rows)
        for k in range(members):
            copy = pltpu.make_async_copy(
                pert_ref.at[k, :, at, :], narrow.at[k, :, at, :], load_sem.at[half * members + k]
            )
            copy.start()
            pert_in.append(copy)
        for part in (0, 1):
            column = lax.rem(across // 2 + part, 2)
            start = (other_y, y)[half] * half_rows + column * PIECE
            at = pl.ds(pl.multiple_of(start, PIECE), PIECE)
            copy = pltpu.make_async_copy(
                amp_ref.at[:, :, at, :],
                amp_out.at[:, :, at, :],
                load_sem.at[2 * members + 2 * half + part],
            )
            copy.start()
            amp_in.append(copy)

    load_half(0)
    plane_in = [
        [
            pltpu.make_async_copy(
                ref.at[:, :, lanes[side]],
                planes_in.at[number, side],
                plane_sem.at[2 * number + side],
            )
            for side in range(2)
        ]
        for number, ref in enumerate((control_ref, innov_ref))
    ]
    small_in = [
        pltpu.make_async_copy(src, dst, small_sem.at[number])
        for number, (src, dst) in enumerate(
            (
                (spread_in, spread_ref),
                (land_in, land_ref),
                (row_index_in, row_index_ref),
                (row_weight_in, row_weight_ref),
                (std_in, std_ref),
                (col_index_in, col_index_ref),
                (col_weight_in, col_weight_ref),
            )
        )
    ]
    for copy in small_in + plane_in[0]:
        copy.start()
    load_half(1)
    for copy in plane_in[1]:
        copy.start()

    def planes(ref, number, side):
        return ref.at[number, side].reshape(lev_dev * own, 128)

    def widen(half):
        at = pl.ds(pl.multiple_of((other_y, y)[half] * half_rows, 16), half_rows)
        for k in range(members):
            pert_in[half * members + k].wait()

            def widen_level(level, carry):
                wide[k, level, at] = narrow[k, level, at].astype(F32)
                return carry

            lax.fori_loop(0, levels, widen_level, 0, unroll=8)

    def x_rows(ry, rx):
        return pl.ds(share(ry, rx), XROWS)

    def y_rows(ry, rx):
        return pl.ds(share(ry, rx) + XROWS, YROWS)

    def add(rows, *terms):
        total = sums[rows]
        for term in terms:
            total = total + term[...]
        sums[rows] = total

    amps = amp_out.reshape(members * modes * PITCH, 128)
    perts = wide.reshape(members * levels * PITCH, 128)
    lhs = lhs_ref[...]
    mode = lax.broadcasted_iota(jnp.int32, (modes, 128), 0)

    def contract(start):
        def row_pair(step, carry):
            first = start + step * 2
            keep = [mode < count_ref[pl.ds(first + h, 1), :] for h in range(2)]
            total = [jnp.zeros((levels, 128), F32) for _ in range(2)]
            for k in range(members):
                rhs = []
                for h in range(2):
                    amp = amps[pl.ds(k * modes * PITCH + first + h, modes, stride=PITCH), :]
                    rhs.append(stacked(jnp.where(keep[h], amp, 0.0)))
                level_amp = jnp.dot(lhs, jnp.concatenate(rhs, axis=1), preferred_element_type=F32)
                for h in range(2):
                    pert = perts[pl.ds(k * levels * PITCH + first + h, levels, stride=PITCH), :]
                    total[h] = total[h] + pert * level_amp[:, h * 128 : (h + 1) * 128]
            for h in range(2):
                tile[0, first + h] = total[h][: levels // 2]
                tile[1, first + h] = total[h][levels // 2 :]
            return carry

        lax.fori_loop(0, ROWS // 2, row_pair, 0, unroll=3)

    order = [(ry, rx) for ry in (other_y, y) for rx in (across, right, left, x)]
    ring = ((across, to_across), (right, to_right), (left, to_left))
    origins = (left, right, across)
    core_sends = []
    to_ring = [[], []]
    to_pair = []
    to_own = []

    def produce(number):
        contract(share(*order[number]))

    def send_core(number):
        rows = pl.ds(share(*order[number]), ROWS)
        core_sends.append(remote(tile.at[1 - lev, rows], core_in.at[rows], to_core))

    def settle(number):
        core_sends[number].wait_recv()
        rows = pl.ds(share(*order[number]), ROWS)
        add(rows, core_in.at[rows])
        half, place = number // 4, number % 4
        if place < 3:
            rx, device = ring[place]
            to_ring[half].append(
                remote(sums.at[x_rows(*order[number])], x_in.at[half, place], device)
            )
        if half == 0:
            rx = order[number][1]
            to_pair.append(remote(sums.at[y_rows(other_y, rx)], pair_y_in.at[place], to_y))

    def settle_pair(place):
        to_pair[place].wait_recv()
        rx = order[place][1]
        add(y_rows(y, rx), pair_y_in.at[place])
        if place < 3:
            to_own.append(remote(sums.at[y_rows(y, rx)], y_in.at[place], ring[place][1]))

    count_load.wait()
    widen(0)
    amp_in[0].wait()
    produce(0)
    pl.semaphore_wait(barrier, 7)
    send_core(0)
    amp_in[1].wait()
    produce(1)
    send_core(1)
    produce(2)
    send_core(2)
    settle(0)
    produce(3)
    send_core(3)
    settle(1)
    settle(2)

    for copy in small_in + plane_in[0]:
        copy.wait()

    def load_rows(i, carry):
        for side in range(2):
            field_a[EDGE + i, :, lanes[side]] = planes(planes_in, 0, side)[
                pl.ds(i, lev_dev, stride=own), :
            ]
        sub = lax.broadcasted_iota(jnp.int32, (8, 256), 0)
        weight = jnp.full((8, 256), row_weight_ref[i], F32)
        index = jnp.full((8, 256), row_index_ref[i], jnp.int32)
        upper = (index == (first_row + i) // 2).astype(F32)
        spread = jnp.broadcast_to(spread_ref[pl.ds(i, 1), :], (8, 256))
        land = jnp.broadcast_to(land_ref[pl.ds(i, 1), :], (8, 256)).astype(F32)
        cells[EDGE + i] = jnp.where(
            sub == 0, spread, jnp.where(sub == 1, land, jnp.where(sub == 2, weight, upper))
        )
        return carry

    lax.fori_loop(0, own, load_rows, 0, unroll=8)
    top, bottom = pl.ds(EDGE, HALO), pl.ds(EDGE + own - HALO, HALO)
    low, high = pl.ds(EDGE - HALO, HALO), pl.ds(EDGE + own, HALO)
    halo_sends = [
        remote(ref.at[src], ref.at[dst], device)
        for ref in (cells, field_a)
        for src, dst, device in ((top, high, to_before), (bottom, low, to_after))
    ]
    settle(3)

    widen(1)
    amp_in[2].wait()
    produce(4)
    send_core(4)
    amp_in[3].wait()
    produce(5)
    send_core(5)
    settle(4)
    settle_pair(0)
    produce(6)
    send_core(6)
    settle(5)
    produce(7)
    send_core(7)
    settle(6)
    settle_pair(1)
    for copy in to_ring[0]:
        copy.wait_recv()
    add(x_rows(other_y, x), x_in.at[0, 0], x_in.at[0, 1], x_in.at[0, 2])
    pair_x = remote(sums.at[x_rows(other_y, x)], pair_x_in, to_y)

    for ref in (cells, misfit):
        ref[0] = jnp.zeros(ref.shape[1:], F32)
        ref[GROWN - 1] = jnp.zeros(ref.shape[1:], F32)
    for row in (1, GROWN - 2):
        field_b[row] = jnp.zeros(field_b.shape[1:], F32)
    for lev_at in range(lev_dev):
        sigma[lev_at : lev_at + 1, :] = jnp.full((1, 256), std_ref[lev_at], F32)
    for copy in halo_sends[:2]:
        copy.wait_recv()

    def coefficients(e, carry):
        here, there = cells[e], cells[e + 1]
        line = first_row - EDGE + e
        inside = (line >= 0) & (line < rows_all) & (e >= 1) & (e <= GROWN - 2)
        facing = (line >= 0) & (line + 1 < rows_all)
        inside = jnp.where(inside, 1.0, 0.0).astype(F32)
        facing = jnp.where(facing, 1.0, 0.0).astype(F32)
        lane = lax.broadcasted_iota(jnp.int32, (8, 256), 1)
        spread, land = (jnp.broadcast_to(here[j : j + 1], (8, 256)) for j in (0, 1))
        spread_next, land_next = (jnp.broadcast_to(there[j : j + 1], (8, 256)) for j in (0, 1))
        row_face = (
            jnp.sqrt(spread * spread_next) * (1.0 - 0.5 * jnp.abs(land - land_next)) * facing
        )
        row_faces[e] = row_face
        spread_right, land_right = (pltpu.roll(v, 255, 1) for v in (spread, land))
        col_face = jnp.where(
            lane < 255,
            jnp.sqrt(spread * spread_right) * (1.0 - 0.5 * jnp.abs(land - land_right)),
            0.0,
        )
        col_before = pltpu.roll(col_face, 1, 1)
        col_faces[0, e] = col_face
        col_faces[1, e] = col_before
        centre[e] = 1.0 - (row_face + col_face + col_before)
        weight, upper = (jnp.broadcast_to(here[j : j + 1, :128], (8, 128)) for j in (2, 3))
        upper_on = upper > 0.5
        weights[0, e] = jnp.where(upper_on, 0.0, 1.0 - weight) * inside
        weights[1, e] = jnp.where(upper_on, 1.0 - weight, weight) * inside
        weights[2, e] = jnp.where(upper_on, weight, 0.0) * inside
        return carry

    lax.fori_loop(0, GROWN - 1, coefficients, 0, unroll=4)
    inner = pl.ds(1, GROWN - 2)
    centre[inner] = centre[inner] - row_faces[pl.ds(0, GROWN - 2)]
    for j in range(3):
        weights[j, GROWN - 1] = jnp.zeros((8, 128), F32)
    col = lax.broadcasted_iota(jnp.int32, (128, 256), 0)
    col_at, col_w = col_index_ref[...], col_weight_ref[...]
    matrix = jnp.where(col == col_at, 1.0 - col_w, jnp.where(col == col_at + 1, col_w, 0.0))
    hi, lo = halves(matrix)
    col_mat[0], col_mat[1] = hi, lo

    def sweep(src, dst, first=0, last=7):
        def rows_of_four(step, carry):
            e = EDGE - 2 + 4 * step
            at_four = pl.ds(e, 4)
            down = row_faces[pl.ds(e - 1, 5)]
            to_right_face, to_left_face = col_faces[0, at_four], col_faces[1, at_four]
            keep = centre[at_four]
            for tile_at in range(lev_dev // 8):
                at = pl.ds(8 * tile_at, 8)
                v = src[pl.ds(e - 1, 6), at, :]
                mid = v[1:5]
                dst[at_four, at, :] = (
                    keep * mid
                    + (down[1:] * v[2:] + down[:-1] * v[:-2])
                    + to_right_face * pltpu.roll(mid, 255, 2)
                    + to_left_face * pltpu.roll(mid, 1, 2)
                )
            return carry

        lax.fori_loop(first, last, rows_of_four, 0)

    settle_pair(2)
    settle(7)
    for copy in halo_sends[2:]:
        copy.wait_recv()
        copy.wait_send()
    sweep(field_a, field_b)
    sweep(field_b, field_a)
    settle_pair(3)
    for copy in to_ring[1]:
        copy.wait_recv()
    add(x_rows(y, x), x_in.at[1, 0], x_in.at[1, 1], x_in.at[1, 2])
    sweep(field_a, field_b)

    def static_part(i, carry):
        for side in range(2):
            cols = lanes[side]
            misfit[EDGE + i, :, cols] = (
                sigma[:, cols] * field_b[EDGE + i, :, cols]
                - planes(planes_in, 1, side)[pl.ds(i, lev_dev, stride=own), :]
            )
        return carry

    for copy in plane_in[1]:
        copy.wait()
    lax.fori_loop(0, own, static_part, 0, unroll=8)
    halo_again = [
        remote(misfit.at[top], misfit.at[high], to_before),
        remote(misfit.at[bottom], misfit.at[low], to_after),
    ]

    for copy in to_own:
        copy.wait_recv()
    mine = share(y, x)
    window[pl.ds(HALO + XROWS, YROWS)] = sums[y_rows(y, x)] + y_in[0] + (y_in[1] + y_in[2])
    pair_x.wait_recv()
    window[pl.ds(HALO, XROWS)] = sums[x_rows(y, x)] + pair_x_in[...]
    halo_again += [
        remote(window.at[pl.ds(ROWS, HALO)], window.at[pl.ds(0, HALO)], to_after),
        remote(window.at[pl.ds(HALO, HALO)], window.at[pl.ds(HALO + ROWS, HALO)], to_before),
    ]

    def dot_split(lhs, which):
        hi, lo = halves(lhs)
        c_hi, c_lo = col_mat[0], col_mat[1]
        dims = (((1,), (which,)), ((), ()))
        dot = functools.partial(lax.dot_general, dimension_numbers=dims, preferred_element_type=F32)
        return dot(hi, c_hi) + (dot(lo, c_hi) + dot(hi, c_lo))

    span = 8

    def interpolate(step, carry):
        e0 = step * span
        lines = []
        for pair in range(span // 2):
            t = step * (span // 2) + pair + 1
            w = [window[t + d].reshape(lev_dev // 8, 8, 128) for d in (-1, 0, 1)]
            for h in range(2):
                e = e0 + 2 * pair + h
                line = weights[0, e] * w[0] + weights[1, e] * w[1] + weights[2, e] * w[2]
                lines.append(line.reshape(lev_dev, 128))
        fine_part = dot_split(jnp.concatenate(lines, axis=0), 0)
        at = pl.ds(e0, span)
        total = misfit[at] + fine_part.reshape(span, lev_dev, 256)
        misfit[at] = total
        field_a[at] = sigma[...] * total
        back[at] = dot_split(total.reshape(span * lev_dev, 256), 1).reshape(span, lev_dev, 128)
        return carry

    lax.fori_loop(1, 3, interpolate, 0, unroll=2)
    for copy in halo_again:
        copy.wait_recv()
    for copy in halo_again[:2]:
        copy.wait_send()
    interpolate(0, 0)
    interpolate(3, 0)

    def adjoint(r, carry):
        e = 2 * r + 2
        total = jnp.zeros((lev_dev // 8, 8, 128), F32)
        for j in range(6):
            total = total + weights[2 - j // 2, e + j] * back[e + j].reshape(lev_dev // 8, 8, 128)
        shares[lev, mine + r] = total.reshape(lev_dev, 128)
        return carry

    lax.fori_loop(0, ROWS, adjoint, 0, unroll=12)

    def to_all(rows, device):
        return remote(shares.at[lev, rows], shares.at[lev, rows], device)

    def to_ring_of(rows):
        return [to_all(rows, device) for device in (to_right, to_left, to_across)]

    pair_first = to_all(x_rows(y, x), to_y)
    ring_y = to_ring_of(y_rows(y, x))
    pair_y = [to_all(y_rows(y, x), to_y)]
    ring_own = to_ring_of(x_rows(y, x))
    core = [to_all(pl.ds(mine, ROWS), to_core)]

    sweep(field_a, field_b)
    sweep(field_b, field_a, 0, 3)
    pair_first.wait_recv()
    ring_other = to_ring_of(x_rows(other_y, x))
    core.append(to_all(x_rows(other_y, x), to_core))
    for copy, rx in zip(ring_y, origins):
        copy.wait_recv()
        pair_y.append(to_all(y_rows(y, rx), to_y))
        core.append(to_all(y_rows(y, rx), to_core))
    sweep(field_b, field_a, 3, 7)
    sweep(field_a, field_b, 0, 3)
    for copy, rx in zip(ring_own, origins):
        copy.wait_recv()
        core.append(to_all(x_rows(y, rx), to_core))
    pair_y[0].wait_recv()
    core.append(to_all(y_rows(other_y, x), to_core))
    sweep(field_a, field_b, 3, 7)

    def finish(i, carry):
        at = pl.ds(i, lev_dev, stride=own)
        for side in range(2):
            for number, value in ((0, field_b), (1, misfit)):
                planes(planes_out, number, side)[at, :] = (
                    planes(planes_in, number, side)[at, :] + value[EDGE + i, :, lanes[side]]
                )
        return carry

    lax.fori_loop(0, own, finish, 0, unroll=8)
    for copy, rx in zip(pair_y[1:], origins):
        copy.wait_recv()
        core.append(to_all(y_rows(other_y, rx), to_core))
    for copy, rx in zip(ring_other, origins):
        copy.wait_recv()
        core.append(to_all(x_rows(other_y, rx), to_core))
    for copy in core:
        copy.wait_recv()
    waited = halo_sends[2:] + halo_again[:2]
    for copy in sent:
        if not any(copy is done for done in waited):
            copy.wait_send()


def exchange(sizes, lhs, count, amp, pert, control, innov, std, spread, land, row_index, row_weight, col_index, col_weight):
    members, modes, rows, cols = amp.shape
    levels = pert.shape[1]
    lev_dev, own, cols_fine = control.shape
    vmem = pl.BlockSpec(memory_space=pltpu.VMEM)
    anywhere = pl.BlockSpec(memory_space=pl.ANY)
    cell = (lev_dev, 128)
    row = (lev_dev, cols_fine)
    tile = (2, rows) + cell
    return pl.pallas_call(
        functools.partial(exchange_kernel, sizes),
        in_specs=[vmem] + [anywhere] * 12,
        out_specs=[vmem] * 5,
        out_shape=[
            pltpu.VMEM((members, modes, PITCH, cols), F32),
            pltpu.VMEM((members, levels, PITCH, cols), F32),
            pltpu.VMEM(tile, F32),
            pltpu.VMEM((2, 2, lev_dev, own, 128), F32),
            pltpu.VMEM(count.shape, jnp.int32),
        ],
        scratch_shapes=[
            pltpu.VMEM(tile, F32),
            pltpu.VMEM(pert.shape, BF16),
            pltpu.VMEM((rows,) + cell, F32),
            pltpu.VMEM((2, 3, XROWS) + cell, F32),
            pltpu.VMEM((XROWS,) + cell, F32),
            pltpu.VMEM((4, YROWS) + cell, F32),
            pltpu.VMEM((3, YROWS) + cell, F32),
            pltpu.VMEM((ROWS + 2 * HALO,) + cell, F32),
            pltpu.VMEM((GROWN,) + row, F32),
            pltpu.VMEM((GROWN,) + row, F32),
            pltpu.VMEM((GROWN,) + row, F32),
            pltpu.VMEM((GROWN, 8, cols_fine), F32),
            pltpu.VMEM((GROWN, 8, cols_fine), F32),
            pltpu.VMEM((2, GROWN, 8, cols_fine), F32),
            pltpu.VMEM((GROWN, 8, cols_fine), F32),
            pltpu.VMEM((3, GROWN, 8, 128), F32),
            pltpu.VMEM(row, F32),
            pltpu.VMEM((2, 128, cols_fine), BF16),
            pltpu.VMEM((GROWN,) + cell, F32),
            pltpu.VMEM((2, 2, lev_dev, own, 128), F32),
            pltpu.SMEM(std.shape, F32),
            pltpu.VMEM(spread.shape, F32),
            pltpu.VMEM(land.shape, jnp.int32),
            pltpu.SMEM(row_index.shape, jnp.int32),
            pltpu.SMEM(row_weight.shape, F32),
            pltpu.VMEM((1, cols_fine), jnp.int32),
            pltpu.VMEM((1, cols_fine), F32),
            pltpu.SemaphoreType.DMA((80,)),
            pltpu.SemaphoreType.DMA((80,)),
            pltpu.SemaphoreType.DMA((2 * members + 4,)),
            pltpu.SemaphoreType.DMA((4,)),
            pltpu.SemaphoreType.DMA((8,)),
        ],
        compiler_params=pltpu.CompilerParams(
            collective_id=0, has_side_effects=True, vmem_limit_bytes=24 << 20
        ),
        name="exchange",
    )(
        lhs,
        *(
            pltpu.with_memory_space_constraint(operand, pltpu.HBM)
            for operand in (
                count,
                amp,
                pert,
                control,
                innov,
                std,
                spread,
                land,
                row_index,
                row_weight,
                col_index.reshape(1, cols_fine),
                col_weight.reshape(1, cols_fine),
            )
        ),
    )


def local(
    ens_pert,
    ens_control,
    eigen_modes,
    mode_count,
    row_index,
    row_weight,
    col_index,
    col_weight,
    static_control,
    static_std,
    diffusivity,
    land_mask,
    innovation,
):
    sizes = (
        lax.axis_size("coarse"),
        lax.axis_size("fine"),
        lax.axis_size("coarse") * lax.axis_size("fine") * row_index.shape[0],
    )
    scaled = eigen_modes * (1.0 / math.sqrt(MEMBERS - 1))
    tall, across = split_modes(scaled.T)
    amp, wide, coarse_grad, planes, count = exchange(
        sizes,
        tall,
        mode_count,
        ens_control,
        ens_pert,
        static_control,
        innovation,
        static_std,
        diffusivity,
        land_mask,
        row_index,
        row_weight,
        col_index,
        col_weight,
    )
    grad_ens, grad_static, increment = backward(
        across, count, amp, wide, coarse_grad, planes, mode_count.shape[0]
    )
    return increment, grad_static, grad_ens


def solution(mesh):
    in_specs = (
        P(("fine", "lev"), None, "coarse", None),
        P(("fine", "lev"), None, "coarse", None),
        P(),
        P("coarse", None),
        P(("coarse", "fine")),
        P(("coarse", "fine")),
        P(),
        P(),
        P("lev", ("coarse", "fine"), None),
        P("lev"),
        P(("coarse", "fine"), None),
        P(("coarse", "fine"), None),
        P("lev", ("coarse", "fine"), None),
    )
    out_specs = (
        P("lev", ("coarse", "fine"), None),
        P("lev", ("coarse", "fine"), None),
        P(("fine", "lev"), None, "coarse", None),
    )
    return jax.shard_map(local, mesh=mesh, in_specs=in_specs, out_specs=out_specs, check_vma=False)
```

```python
import functools
import math

import jax
import jax.numpy as jnp
from jax import lax
from jax.experimental import pallas as pl
from jax.experimental.pallas import tpu as pltpu
from jax.sharding import PartitionSpec as P

MEMBERS = 80
NSWEEP = 3
HALO = 3
EDGE = 4
GROWN = 32
ROWS = 12
XROWS = 5
YROWS = ROWS - XROWS
PITCH = 104
HALF_PITCH = 56
PIECE = 24
F32 = jnp.float32
BF16 = jnp.bfloat16


def halves(value):
    hi = value.astype(BF16)
    return hi, (value - hi.astype(F32)).astype(BF16)


def stacked(value):
    hi, lo = halves(value)
    return jnp.concatenate([hi, hi, lo], axis=0)


def project_row_pair(lhs, keep_from, amps, perts, outs, grad_ref, sizes, first, out_first):
    members, modes, levels = sizes
    mode = lax.broadcasted_iota(jnp.int32, (modes, 128), 0)
    keep = [mode < keep_from[pl.ds(first + h, 1), :] for h in range(2)]
    grad = [
        jnp.concatenate([grad_ref[0, first + h], grad_ref[1, first + h]], axis=0) for h in range(2)
    ]
    for k in range(members):
        rhs = []
        for h in range(2):
            pert = perts[pl.ds(k * levels * PITCH + first + h, levels, stride=PITCH), :]
            rhs.append(stacked(pert * grad[h]))
        proj = jnp.dot(lhs, jnp.concatenate(rhs, axis=1), preferred_element_type=F32)
        for h in range(2):
            amp = amps[pl.ds(k * modes * PITCH + first + h, modes, stride=PITCH), :]
            at = pl.ds(k * modes * HALF_PITCH + out_first + h, modes, stride=HALF_PITCH)
            outs[at, :] = amp + jnp.where(keep[h], proj[:, h * 128 : (h + 1) * 128], 0.0)


def backward_kernel(
    lhs_ref,
    count_ref,
    amp_ref,
    wide_ref,
    grad_ref,
    planes_ref,
    done_ref,
    out_ref,
    grad_static_ref,
    inc_ref,
    result,
    out_sem,
    plane_sem,
):
    members, modes = amp_ref.shape[:2]
    levels = wide_ref.shape[1]
    half_rows = out_ref.shape[2] // 2
    y = lax.axis_index("fine") // (lax.axis_size("fine") // 2)
    at = pl.ds(pl.multiple_of(y * half_rows, 8), half_rows)
    copies = [
        pltpu.make_async_copy(
            done_ref.at[:, :, pl.ds(0, half_rows), :], out_ref.at[:, :, at, :], out_sem.at[0]
        )
    ]
    copies += [
        pltpu.make_async_copy(
            planes_ref.at[number, side],
            ref.at[:, :, pl.ds(128 * side, 128)],
            plane_sem.at[2 * number + side],
        )
        for number, ref in enumerate((grad_static_ref, inc_ref))
        for side in range(2)
    ]
    for copy in copies:
        copy.start()
    amps = amp_ref.reshape(members * modes * PITCH, 128)
    perts = wide_ref.reshape(members * levels * PITCH, 128)
    outs = result.reshape(members * modes * HALF_PITCH, 128)
    lhs = lhs_ref[...]
    base = (1 - y) * half_rows
    for piece in range(half_rows // PIECE):

        def row_pair(step, carry):
            row = piece * PIECE + step * 2
            project_row_pair(
                lhs, count_ref, amps, perts, outs, grad_ref, (members, modes, levels), base + row, row
            )
            return carry

        lax.fori_loop(0, PIECE // 2, row_pair, 0, unroll=4)
        copy = pltpu.make_async_copy(
            result.at[:, :, pl.ds(piece * PIECE, PIECE), :],
            out_ref.at[:, :, pl.ds(pl.multiple_of(base + piece * PIECE, 8), PIECE), :],
            out_sem.at[1 + piece],
        )
        copy.start()
        copies.append(copy)
    for copy in copies:
        copy.wait()


def backward(lhs, count, amp, wide, grad, planes, done, rows):
    members, modes, _, cols = amp.shape
    lev_dev, own = planes.shape[2:4]
    vmem = pl.BlockSpec(memory_space=pltpu.VMEM)
    anywhere = pl.BlockSpec(memory_space=pl.ANY)
    field = jax.ShapeDtypeStruct((lev_dev, own, 2 * cols), F32)
    return pl.pallas_call(
        backward_kernel,
        in_specs=[vmem] * 7,
        out_specs=[anywhere] * 3,
        out_shape=[jax.ShapeDtypeStruct((members, modes, rows, cols), F32), field, field],
        scratch_shapes=[
            pltpu.VMEM(done.shape, F32),
            pltpu.SemaphoreType.DMA((1 + rows // (2 * PIECE),)),
            pltpu.SemaphoreType.DMA((4,)),
        ],
        compiler_params=pltpu.CompilerParams(vmem_limit_bytes=6 << 20),
        name="backward_modes",
    )(lhs, count, amp, wide, grad, planes, done)


def exchange_kernel(
    sizes,
    modes_in,
    count_in,
    amp_ref,
    pert_ref,
    control_ref,
    innov_ref,
    std_in,
    spread_in,
    land_in,
    row_index_in,
    row_weight_in,
    col_index_in,
    col_weight_in,
    amp_out,
    wide,
    shares,
    planes_out,
    count_ref,
    back_lhs_ref,
    done,
    modes_ref,
    tile,
    narrow,
    core_in,
    x_in,
    pair_x_in,
    pair_y_in,
    y_in,
    window,
    field_a,
    field_b,
    misfit,
    cells,
    row_faces,
    col_faces,
    centre,
    weights,
    sigma,
    col_mat,
    back,
    planes_in,
    std_ref,
    spread_ref,
    land_ref,
    row_index_ref,
    row_weight_ref,
    col_index_ref,
    col_weight_ref,
    send_sem,
    recv_sem,
    load_sem,
    plane_sem,
    small_sem,
):
    coarse_count, fine_count, rows_all = sizes
    xs = fine_count // 2
    coarse = lax.axis_index("coarse")
    fine = lax.axis_index("fine")
    lev = lax.axis_index("lev")
    x = lax.rem(fine, xs)
    y = fine // xs
    right, left, across = lax.rem(x + 1, xs), lax.rem(x + xs - 1, xs), lax.rem(x + 2, xs)
    other_y = 1 - y
    serial = coarse * fine_count + fine
    count = coarse_count * fine_count
    after, before = lax.rem(serial + 1, count), lax.rem(serial + count - 1, count)
    first_row = serial * 2 * ROWS
    members, modes = amp_ref.shape[:2]
    levels = pert_ref.shape[1]
    sums = tile.at[lev]

    to_core = (coarse, fine, 1 - lev)
    to_right = (coarse, y * xs + right, lev)
    to_left = (coarse, y * xs + left, lev)
    to_across = (coarse, y * xs + across, lev)
    to_y = (coarse, other_y * xs + x, lev)
    to_after = (after // fine_count, lax.rem(after, fine_count), lev)
    to_before = (before // fine_count, lax.rem(before, fine_count), lev)

    barrier = pltpu.get_barrier_semaphore()
    for device in (to_core, to_right, to_left, to_across, to_y, to_after, to_before):
        pl.semaphore_signal(barrier, inc=1, device_id=device, device_id_type=pl.DeviceIdType.MESH)

    numbers = iter(range(100))
    sent = []

    def remote(src, dst, device):
        number = next(numbers)
        copy = pltpu.make_async_remote_copy(
            src_ref=src,
            dst_ref=dst,
            send_sem=send_sem.at[number],
            recv_sem=recv_sem.at[number],
            device_id=device,
            device_id_type=pl.DeviceIdType.MESH,
        )
        copy.start()
        sent.append(copy)
        return copy

    def share(ry, rx):
        return (ry * xs + rx) * ROWS

    lev_dev = control_ref.shape[0]
    own = 2 * ROWS
    half_rows = xs * ROWS
    lanes = [pl.ds(0, 128), pl.ds(128, 128)]

    count_load = pltpu.make_async_copy(count_in, count_ref, small_sem.at[7])
    count_load.start()
    modes_load = pltpu.make_async_copy(modes_in, modes_ref, small_sem.at[8])
    modes_load.start()
    pert_in, amp_in = [], []

    def load_half(half):
        at = pl.ds(pl.multiple_of((other_y, y)[half] * half_rows, 16), half_rows)
        for k in range(members):
            copy = pltpu.make_async_copy(
                pert_ref.at[k, :, at, :], narrow.at[k, :, at, :], load_sem.at[half * members + k]
            )
            copy.start()
            pert_in.append(copy)
        for part in (0, 1):
            column = lax.rem(across // 2 + part, 2)
            start = (other_y, y)[half] * half_rows + column * PIECE
            at = pl.ds(pl.multiple_of(start, PIECE), PIECE)
            copy = pltpu.make_async_copy(
                amp_ref.at[:, :, at, :],
                amp_out.at[:, :, at, :],
                load_sem.at[2 * members + 2 * half + part],
            )
            copy.start()
            amp_in.append(copy)

    load_half(0)
    plane_in = [
        [
            pltpu.make_async_copy(
                ref.at[:, :, lanes[side]],
                planes_in.at[number, side],
                plane_sem.at[2 * number + side],
            )
            for side in range(2)
        ]
        for number, ref in enumerate((control_ref, innov_ref))
    ]
    small_in = [
        pltpu.make_async_copy(src, dst, small_sem.at[number])
        for number, (src, dst) in enumerate(
            (
                (spread_in, spread_ref),
                (land_in, land_ref),
                (row_index_in, row_index_ref),
                (row_weight_in, row_weight_ref),
                (std_in, std_ref),
                (col_index_in, col_index_ref),
                (col_weight_in, col_weight_ref),
            )
        )
    ]
    for copy in small_in + plane_in[0]:
        copy.start()
    load_half(1)
    for copy in plane_in[1]:
        copy.start()

    def planes(ref, number, side):
        return ref.at[number, side].reshape(lev_dev * own, 128)

    def widen(half):
        at = pl.ds(pl.multiple_of((other_y, y)[half] * half_rows, 16), half_rows)
        for k in range(members):
            pert_in[half * members + k].wait()

            def widen_level(level, carry):
                wide[k, level, at] = narrow[k, level, at].astype(F32)
                return carry

            lax.fori_loop(0, levels, widen_level, 0, unroll=8)

    def x_rows(ry, rx):
        return pl.ds(share(ry, rx), XROWS)

    def y_rows(ry, rx):
        return pl.ds(share(ry, rx) + XROWS, YROWS)

    def add(rows, *terms):
        total = sums[rows]
        for term in terms:
            total = total + term[...]
        sums[rows] = total

    amps = amp_out.reshape(members * modes * PITCH, 128)
    perts = wide.reshape(members * levels * PITCH, 128)
    modes_load.wait()
    scaled = modes_ref[...] * (1.0 / math.sqrt(MEMBERS - 1))
    scaled_hi = scaled.astype(BF16).astype(F32)
    scaled_lo = scaled - scaled_hi
    lhs = jnp.concatenate([scaled_hi, scaled_lo, scaled_hi], axis=0).T.astype(BF16)
    back_lhs = jnp.concatenate([scaled_hi, scaled_lo, scaled_hi], axis=1).astype(BF16)
    back_lhs_ref[...] = back_lhs
    mode = lax.broadcasted_iota(jnp.int32, (modes, 128), 0)

    def contract(start):
        def row_pair(step, carry):
            first = start + step * 2
            keep = [mode < count_ref[pl.ds(first + h, 1), :] for h in range(2)]
            total = [jnp.zeros((levels, 128), F32) for _ in range(2)]
            for k in range(members):
                rhs = []
                for h in range(2):
                    amp = amps[pl.ds(k * modes * PITCH + first + h, modes, stride=PITCH), :]
                    rhs.append(stacked(jnp.where(keep[h], amp, 0.0)))
                level_amp = jnp.dot(lhs, jnp.concatenate(rhs, axis=1), preferred_element_type=F32)
                for h in range(2):
                    pert = perts[pl.ds(k * levels * PITCH + first + h, levels, stride=PITCH), :]
                    total[h] = total[h] + pert * level_amp[:, h * 128 : (h + 1) * 128]
            for h in range(2):
                tile[0, first + h] = total[h][: levels // 2]
                tile[1, first + h] = total[h][levels // 2 :]
            return carry

        lax.fori_loop(0, ROWS // 2, row_pair, 0, unroll=3)

    order = [(ry, rx) for ry in (other_y, y) for rx in (across, right, left, x)]
    ring = ((across, to_across), (right, to_right), (left, to_left))
    origins = (left, right, across)
    core_sends = []
    to_ring = [[], []]
    to_pair = []
    to_own = []

    def produce(number):
        contract(share(*order[number]))

    def send_core(number):
        rows = pl.ds(share(*order[number]), ROWS)
        core_sends.append(remote(tile.at[1 - lev, rows], core_in.at[rows], to_core))

    def settle(number):
        core_sends[number].wait_recv()
        rows = pl.ds(share(*order[number]), ROWS)
        add(rows, core_in.at[rows])
        half, place = number // 4, number % 4
        if place < 3:
            rx, device = ring[place]
            to_ring[half].append(
                remote(sums.at[x_rows(*order[number])], x_in.at[half, place], device)
            )
        if half == 0:
            rx = order[number][1]
            to_pair.append(remote(sums.at[y_rows(other_y, rx)], pair_y_in.at[place], to_y))

    def settle_pair(place):
        to_pair[place].wait_recv()
        rx = order[place][1]
        add(y_rows(y, rx), pair_y_in.at[place])
        if place < 3:
            to_own.append(remote(sums.at[y_rows(y, rx)], y_in.at[place], ring[place][1]))

    count_load.wait()
    widen(0)
    amp_in[0].wait()
    produce(0)
    pl.semaphore_wait(barrier, 7)
    send_core(0)
    amp_in[1].wait()
    produce(1)
    send_core(1)
    produce(2)
    send_core(2)
    settle(0)
    produce(3)
    send_core(3)
    settle(1)
    settle(2)

    for copy in small_in + plane_in[0]:
        copy.wait()

    def load_rows(i, carry):
        for side in range(2):
            field_a[EDGE + i, :, lanes[side]] = planes(planes_in, 0, side)[
                pl.ds(i, lev_dev, stride=own), :
            ]
        sub = lax.broadcasted_iota(jnp.int32, (8, 256), 0)
        weight = jnp.full((8, 256), row_weight_ref[i], F32)
        index = jnp.full((8, 256), row_index_ref[i], jnp.int32)
        upper = (index == (first_row + i) // 2).astype(F32)
        spread = jnp.broadcast_to(spread_ref[pl.ds(i, 1), :], (8, 256))
        land = jnp.broadcast_to(land_ref[pl.ds(i, 1), :], (8, 256)).astype(F32)
        cells[EDGE + i] = jnp.where(
            sub == 0, spread, jnp.where(sub == 1, land, jnp.where(sub == 2, weight, upper))
        )
        return carry

    lax.fori_loop(0, own, load_rows, 0, unroll=8)
    top, bottom = pl.ds(EDGE, HALO), pl.ds(EDGE + own - HALO, HALO)
    low, high = pl.ds(EDGE - HALO, HALO), pl.ds(EDGE + own, HALO)
    halo_sends = [
        remote(ref.at[src], ref.at[dst], device)
        for ref in (cells, field_a)
        for src, dst, device in ((top, high, to_before), (bottom, low, to_after))
    ]
    settle(3)

    widen(1)
    amp_in[2].wait()
    produce(4)
    send_core(4)
    amp_in[3].wait()
    produce(5)
    send_core(5)
    settle(4)
    settle_pair(0)
    produce(6)
    send_core(6)
    settle(5)
    produce(7)
    send_core(7)
    settle(6)
    settle_pair(1)
    for copy in to_ring[0]:
        copy.wait_recv()
    add(x_rows(other_y, x), x_in.at[0, 0], x_in.at[0, 1], x_in.at[0, 2])
    pair_x = remote(sums.at[x_rows(other_y, x)], pair_x_in, to_y)

    for ref in (cells, misfit):
        ref[0] = jnp.zeros(ref.shape[1:], F32)
        ref[GROWN - 1] = jnp.zeros(ref.shape[1:], F32)
    for row in (1, GROWN - 2):
        field_b[row] = jnp.zeros(field_b.shape[1:], F32)
    for lev_at in range(lev_dev):
        sigma[lev_at : lev_at + 1, :] = jnp.full((1, 256), std_ref[lev_at], F32)
    for copy in halo_sends[:2]:
        copy.wait_recv()

    def coefficients(e, carry):
        here, there = cells[e], cells[e + 1]
        line = first_row - EDGE + e
        inside = (line >= 0) & (line < rows_all) & (e >= 1) & (e <= GROWN - 2)
        facing = (line >= 0) & (line + 1 < rows_all)
        inside = jnp.where(inside, 1.0, 0.0).astype(F32)
        facing = jnp.where(facing, 1.0, 0.0).astype(F32)
        lane = lax.broadcasted_iota(jnp.int32, (8, 256), 1)
        spread, land = (jnp.broadcast_to(here[j : j + 1], (8, 256)) for j in (0, 1))
        spread_next, land_next = (jnp.broadcast_to(there[j : j + 1], (8, 256)) for j in (0, 1))
        row_face = (
            jnp.sqrt(spread * spread_next) * (1.0 - 0.5 * jnp.abs(land - land_next)) * facing
        )
        row_faces[e] = row_face
        spread_right, land_right = (pltpu.roll(v, 255, 1) for v in (spread, land))
        col_face = jnp.where(
            lane < 255,
            jnp.sqrt(spread * spread_right) * (1.0 - 0.5 * jnp.abs(land - land_right)),
            0.0,
        )
        col_before = pltpu.roll(col_face, 1, 1)
        col_faces[0, e] = col_face
        col_faces[1, e] = col_before
        centre[e] = 1.0 - (row_face + col_face + col_before)
        weight, upper = (jnp.broadcast_to(here[j : j + 1, :128], (8, 128)) for j in (2, 3))
        upper_on = upper > 0.5
        weights[0, e] = jnp.where(upper_on, 0.0, 1.0 - weight) * inside
        weights[1, e] = jnp.where(upper_on, 1.0 - weight, weight) * inside
        weights[2, e] = jnp.where(upper_on, weight, 0.0) * inside
        return carry

    lax.fori_loop(0, GROWN - 1, coefficients, 0, unroll=4)
    inner = pl.ds(1, GROWN - 2)
    centre[inner] = centre[inner] - row_faces[pl.ds(0, GROWN - 2)]
    for j in range(3):
        weights[j, GROWN - 1] = jnp.zeros((8, 128), F32)
    col = lax.broadcasted_iota(jnp.int32, (128, 256), 0)
    col_at, col_w = col_index_ref[...], col_weight_ref[...]
    matrix = jnp.where(col == col_at, 1.0 - col_w, jnp.where(col == col_at + 1, col_w, 0.0))
    hi, lo = halves(matrix)
    col_mat[0], col_mat[1] = hi, lo

    def sweep(src, dst, first=0, last=7):
        def rows_of_four(step, carry):
            e = EDGE - 2 + 4 * step
            at_four = pl.ds(e, 4)
            down = row_faces[pl.ds(e - 1, 5)]
            to_right_face, to_left_face = col_faces[0, at_four], col_faces[1, at_four]
            keep = centre[at_four]
            for tile_at in range(lev_dev // 8):
                at = pl.ds(8 * tile_at, 8)
                v = src[pl.ds(e - 1, 6), at, :]
                mid = v[1:5]
                dst[at_four, at, :] = (
                    keep * mid
                    + (down[1:] * v[2:] + down[:-1] * v[:-2])
                    + to_right_face * pltpu.roll(mid, 255, 2)
                    + to_left_face * pltpu.roll(mid, 1, 2)
                )
            return carry

        lax.fori_loop(first, last, rows_of_four, 0)

    settle_pair(2)
    settle(7)
    for copy in halo_sends[2:]:
        copy.wait_recv()
        copy.wait_send()
    sweep(field_a, field_b)
    sweep(field_b, field_a)
    settle_pair(3)
    for copy in to_ring[1]:
        copy.wait_recv()
    add(x_rows(y, x), x_in.at[1, 0], x_in.at[1, 1], x_in.at[1, 2])
    sweep(field_a, field_b)

    def static_part(i, carry):
        for side in range(2):
            cols = lanes[side]
            misfit[EDGE + i, :, cols] = (
                sigma[:, cols] * field_b[EDGE + i, :, cols]
                - planes(planes_in, 1, side)[pl.ds(i, lev_dev, stride=own), :]
            )
        return carry

    for copy in plane_in[1]:
        copy.wait()
    lax.fori_loop(0, own, static_part, 0, unroll=8)
    halo_again = [
        remote(misfit.at[top], misfit.at[high], to_before),
        remote(misfit.at[bottom], misfit.at[low], to_after),
    ]

    for copy in to_own:
        copy.wait_recv()
    mine = share(y, x)
    window[pl.ds(HALO + XROWS, YROWS)] = sums[y_rows(y, x)] + y_in[0] + (y_in[1] + y_in[2])
    pair_x.wait_recv()
    window[pl.ds(HALO, XROWS)] = sums[x_rows(y, x)] + pair_x_in[...]
    halo_again += [
        remote(window.at[pl.ds(ROWS, HALO)], window.at[pl.ds(0, HALO)], to_after),
        remote(window.at[pl.ds(HALO, HALO)], window.at[pl.ds(HALO + ROWS, HALO)], to_before),
    ]

    def dot_split(lhs, which):
        hi, lo = halves(lhs)
        c_hi, c_lo = col_mat[0], col_mat[1]
        dims = (((1,), (which,)), ((), ()))
        dot = functools.partial(lax.dot_general, dimension_numbers=dims, preferred_element_type=F32)
        return dot(hi, c_hi) + (dot(lo, c_hi) + dot(hi, c_lo))

    span = 8

    def interpolate(step, carry):
        e0 = step * span
        lines = []
        for pair in range(span // 2):
            t = step * (span // 2) + pair + 1
            w = [window[t + d].reshape(lev_dev // 8, 8, 128) for d in (-1, 0, 1)]
            for h in range(2):
                e = e0 + 2 * pair + h
                line = weights[0, e] * w[0] + weights[1, e] * w[1] + weights[2, e] * w[2]
                lines.append(line.reshape(lev_dev, 128))
        fine_part = dot_split(jnp.concatenate(lines, axis=0), 0)
        at = pl.ds(e0, span)
        total = misfit[at] + fine_part.reshape(span, lev_dev, 256)
        misfit[at] = total
        field_a[at] = sigma[...] * total
        back[at] = dot_split(total.reshape(span * lev_dev, 256), 1).reshape(span, lev_dev, 128)
        return carry

    lax.fori_loop(1, 3, interpolate, 0, unroll=2)
    for copy in halo_again:
        copy.wait_recv()
    for copy in halo_again[:2]:
        copy.wait_send()
    interpolate(0, 0)
    interpolate(3, 0)

    def adjoint(r, carry):
        e = 2 * r + 2
        total = jnp.zeros((lev_dev // 8, 8, 128), F32)
        for j in range(6):
            total = total + weights[2 - j // 2, e + j] * back[e + j].reshape(lev_dev // 8, 8, 128)
        shares[lev, mine + r] = total.reshape(lev_dev, 128)
        return carry

    lax.fori_loop(0, ROWS, adjoint, 0, unroll=12)

    def to_all(rows, device):
        return remote(shares.at[lev, rows], shares.at[lev, rows], device)

    def to_ring_of(rows):
        return [to_all(rows, device) for device in (to_right, to_left, to_across)]

    pair_first = to_all(x_rows(y, x), to_y)
    ring_y = to_ring_of(y_rows(y, x))
    pair_y = [to_all(y_rows(y, x), to_y)]
    ring_own = to_ring_of(x_rows(y, x))
    core = [to_all(pl.ds(mine, ROWS), to_core)]

    dones = done.reshape(members * modes * HALF_PITCH, 128)

    def project(rx):
        def row_pair(step, carry):
            row = rx * ROWS + step * 2
            project_row_pair(
                back_lhs,
                count_ref,
                amps,
                perts,
                dones,
                shares,
                (members, modes, levels),
                y * half_rows + row,
                row,
            )
            return carry

        lax.fori_loop(0, ROWS // 2, row_pair, 0, unroll=3)

    sweep(field_a, field_b)
    core[0].wait_recv()
    project(x)
    sweep(field_b, field_a, 0, 3)
    pair_first.wait_recv()
    ring_other = to_ring_of(x_rows(other_y, x))
    core.append(to_all(x_rows(other_y, x), to_core))
    core_y, core_x = [], []
    for copy, rx in zip(ring_y, origins):
        copy.wait_recv()
        pair_y.append(to_all(y_rows(y, rx), to_y))
        core_y.append(to_all(y_rows(y, rx), to_core))
    sweep(field_b, field_a, 3, 7)
    sweep(field_a, field_b, 0, 3)
    for copy, rx in zip(ring_own, origins):
        copy.wait_recv()
        core_x.append(to_all(x_rows(y, rx), to_core))
    pair_y[0].wait_recv()
    core.append(to_all(y_rows(other_y, x), to_core))
    sweep(field_a, field_b, 3, 7)

    def project_origin(number):
        core_x[number].wait_recv()
        core_y[number].wait_recv()
        project(origins[number])

    def pass_on(number):
        pair_y[1 + number].wait_recv()
        core.append(to_all(y_rows(other_y, origins[number]), to_core))

    project_origin(0)
    pass_on(0)

    def finish(i, carry):
        at = pl.ds(i, lev_dev, stride=own)
        for side in range(2):
            for number, value in ((0, field_b), (1, misfit)):
                planes(planes_out, number, side)[at, :] = (
                    planes(planes_in, number, side)[at, :] + value[EDGE + i, :, lanes[side]]
                )
        return carry

    lax.fori_loop(0, own, finish, 0, unroll=8)
    project_origin(1)
    pass_on(1)
    project_origin(2)
    pass_on(2)
    for copy, rx in zip(ring_other, origins):
        copy.wait_recv()
        core.append(to_all(x_rows(other_y, rx), to_core))
    for copy in core[1:]:
        copy.wait_recv()
    waited = halo_sends[2:] + halo_again[:2]
    for copy in sent:
        if not any(copy is done for done in waited):
            copy.wait_send()


def exchange(sizes, modes_t, count, amp, pert, control, innov, std, spread, land, row_index, row_weight, col_index, col_weight):
    members, modes, rows, cols = amp.shape
    levels = pert.shape[1]
    lev_dev, own, cols_fine = control.shape
    vmem = pl.BlockSpec(memory_space=pltpu.VMEM)
    anywhere = pl.BlockSpec(memory_space=pl.ANY)
    cell = (lev_dev, 128)
    row = (lev_dev, cols_fine)
    tile = (2, rows) + cell
    return pl.pallas_call(
        functools.partial(exchange_kernel, sizes),
        in_specs=[anywhere] * 13,
        out_specs=[vmem] * 7,
        out_shape=[
            pltpu.VMEM((members, modes, PITCH, cols), F32),
            pltpu.VMEM((members, levels, PITCH, cols), F32),
            pltpu.VMEM(tile, F32),
            pltpu.VMEM((2, 2, lev_dev, own, 128), F32),
            pltpu.VMEM(count.shape, jnp.int32),
            pltpu.VMEM((modes, 3 * levels), BF16),
            pltpu.VMEM((members, modes, HALF_PITCH, cols), F32),
        ],
        scratch_shapes=[
            pltpu.VMEM(modes_t.shape, F32),
            pltpu.VMEM(tile, F32),
            pltpu.VMEM(pert.shape, BF16),
            pltpu.VMEM((rows,) + cell, F32),
            pltpu.VMEM((2, 3, XROWS) + cell, F32),
            pltpu.VMEM((XROWS,) + cell, F32),
            pltpu.VMEM((4, YROWS) + cell, F32),
            pltpu.VMEM((3, YROWS) + cell, F32),
            pltpu.VMEM((ROWS + 2 * HALO,) + cell, F32),
            pltpu.VMEM((GROWN,) + row, F32),
            pltpu.VMEM((GROWN,) + row, F32),
            pltpu.VMEM((GROWN,) + row, F32),
            pltpu.VMEM((GROWN, 8, cols_fine), F32),
            pltpu.VMEM((GROWN, 8, cols_fine), F32),
            pltpu.VMEM((2, GROWN, 8, cols_fine), F32),
            pltpu.VMEM((GROWN, 8, cols_fine), F32),
            pltpu.VMEM((3, GROWN, 8, 128), F32),
            pltpu.VMEM(row, F32),
            pltpu.VMEM((2, 128, cols_fine), BF16),
            pltpu.VMEM((GROWN,) + cell, F32),
            pltpu.VMEM((2, 2, lev_dev, own, 128), F32),
            pltpu.SMEM(std.shape, F32),
            pltpu.VMEM(spread.shape, F32),
            pltpu.VMEM(land.shape, jnp.int32),
            pltpu.SMEM(row_index.shape, jnp.int32),
            pltpu.SMEM(row_weight.shape, F32),
            pltpu.VMEM((1, cols_fine), jnp.int32),
            pltpu.VMEM((1, cols_fine), F32),
            pltpu.SemaphoreType.DMA((80,)),
            pltpu.SemaphoreType.DMA((80,)),
            pltpu.SemaphoreType.DMA((2 * members + 4,)),
            pltpu.SemaphoreType.DMA((4,)),
            pltpu.SemaphoreType.DMA((9,)),
        ],
        compiler_params=pltpu.CompilerParams(
            collective_id=0, has_side_effects=True, vmem_limit_bytes=18 << 20
        ),
        name="exchange",
    )(
        *(
            pltpu.with_memory_space_constraint(operand, pltpu.HBM)
            for operand in (
                modes_t,
                count,
                amp,
                pert,
                control,
                innov,
                std,
                spread,
                land,
                row_index,
                row_weight,
                col_index.reshape(1, cols_fine),
                col_weight.reshape(1, cols_fine),
            )
        ),
    )


def local(
    ens_pert,
    ens_control,
    eigen_modes,
    mode_count,
    row_index,
    row_weight,
    col_index,
    col_weight,
    static_control,
    static_std,
    diffusivity,
    land_mask,
    innovation,
):
    sizes = (
        lax.axis_size("coarse"),
        lax.axis_size("fine"),
        lax.axis_size("coarse") * lax.axis_size("fine") * row_index.shape[0],
    )
    amp, wide, coarse_grad, planes, count, back_lhs, done = exchange(
        sizes,
        eigen_modes.T,
        mode_count,
        ens_control,
        ens_pert,
        static_control,
        innovation,
        static_std,
        diffusivity,
        land_mask,
        row_index,
        row_weight,
        col_index,
        col_weight,
    )
    grad_ens, grad_static, increment = backward(
        back_lhs, count, amp, wide, coarse_grad, planes, done, mode_count.shape[0]
    )
    return increment, grad_static, grad_ens


def solution(mesh):
    in_specs = (
        P(("fine", "lev"), None, "coarse", None),
        P(("fine", "lev"), None, "coarse", None),
        P(),
        P("coarse", None),
        P(("coarse", "fine")),
        P(("coarse", "fine")),
        P(),
        P(),
        P("lev", ("coarse", "fine"), None),
        P("lev"),
        P(("coarse", "fine"), None),
        P(("coarse", "fine"), None),
        P("lev", ("coarse", "fine"), None),
    )
    out_specs = (
        P("lev", ("coarse", "fine"), None),
        P("lev", ("coarse", "fine"), None),
        P(("fine", "lev"), None, "coarse", None),
    )
    return jax.shard_map(local, mesh=mesh, in_specs=in_specs, out_specs=out_specs, check_vma=False)
```

```python
import functools
import math

import jax
import jax.numpy as jnp
from jax import lax
from jax.experimental import pallas as pl
from jax.experimental.pallas import tpu as pltpu
from jax.sharding import PartitionSpec as P

MEMBERS = 80
NSWEEP = 3
HALO = 3
EDGE = 4
GROWN = 32
ROWS = 12
XROWS = 5
YROWS = ROWS - XROWS
PITCH = 104
HALF_PITCH = 56
PIECE = 24
F32 = jnp.float32
BF16 = jnp.bfloat16


def halves(value):
    hi = value.astype(BF16)
    return hi, (value - hi.astype(F32)).astype(BF16)


def stacked(value):
    hi, lo = halves(value)
    return jnp.concatenate([hi, hi, lo], axis=0)


def project_row_pair(lhs, keep_from, amps, perts, outs, grad_ref, sizes, first, out_first):
    members, modes, levels = sizes
    mode = lax.broadcasted_iota(jnp.int32, (modes, 128), 0)
    keep = [mode < keep_from[pl.ds(first + h, 1), :] for h in range(2)]
    grad = [
        jnp.concatenate([grad_ref[0, first + h], grad_ref[1, first + h]], axis=0) for h in range(2)
    ]
    for k in range(members):
        rhs = []
        for h in range(2):
            pert = perts[pl.ds(k * levels * PITCH + first + h, levels, stride=PITCH), :]
            rhs.append(stacked(pert * grad[h]))
        proj = jnp.dot(lhs, jnp.concatenate(rhs, axis=1), preferred_element_type=F32)
        for h in range(2):
            amp = amps[pl.ds(k * modes * PITCH + first + h, modes, stride=PITCH), :]
            at = pl.ds(k * modes * HALF_PITCH + out_first + h, modes, stride=HALF_PITCH)
            outs[at, :] = amp + jnp.where(keep[h], proj[:, h * 128 : (h + 1) * 128], 0.0)


def backward_kernel(
    lhs_ref,
    count_ref,
    amp_ref,
    wide_ref,
    grad_ref,
    planes_ref,
    done_ref,
    out_ref,
    grad_static_ref,
    inc_ref,
    result,
    out_sem,
    plane_sem,
):
    members, modes = amp_ref.shape[:2]
    levels = wide_ref.shape[1]
    half_rows = out_ref.shape[2] // 2
    y = lax.axis_index("fine") // (lax.axis_size("fine") // 2)
    at = pl.ds(pl.multiple_of(y * half_rows, 8), half_rows)
    copies = [
        pltpu.make_async_copy(
            done_ref.at[:, :, pl.ds(0, half_rows), :], out_ref.at[:, :, at, :], out_sem.at[0]
        )
    ]
    copies += [
        pltpu.make_async_copy(
            planes_ref.at[number, side],
            ref.at[:, :, pl.ds(128 * side, 128)],
            plane_sem.at[2 * number + side],
        )
        for number, ref in enumerate((grad_static_ref, inc_ref))
        for side in range(2)
    ]
    for copy in copies:
        copy.start()
    amps = amp_ref.reshape(members * modes * PITCH, 128)
    perts = wide_ref.reshape(members * levels * PITCH, 128)
    outs = result.reshape(members * modes * HALF_PITCH, 128)
    lhs = lhs_ref[...]
    base = (1 - y) * half_rows
    for piece in range(half_rows // PIECE):

        def row_pair(step, carry):
            row = piece * PIECE + step * 2
            project_row_pair(
                lhs, count_ref, amps, perts, outs, grad_ref, (members, modes, levels), base + row, row
            )
            return carry

        lax.fori_loop(0, PIECE // 2, row_pair, 0, unroll=4)
        copy = pltpu.make_async_copy(
            result.at[:, :, pl.ds(piece * PIECE, PIECE), :],
            out_ref.at[:, :, pl.ds(pl.multiple_of(base + piece * PIECE, 8), PIECE), :],
            out_sem.at[1 + piece],
        )
        copy.start()
        copies.append(copy)
    for copy in copies:
        copy.wait()


def backward(lhs, count, amp, wide, grad, planes, done, rows):
    members, modes, _, cols = amp.shape
    lev_dev, own = planes.shape[2:4]
    vmem = pl.BlockSpec(memory_space=pltpu.VMEM)
    anywhere = pl.BlockSpec(memory_space=pl.ANY)
    field = jax.ShapeDtypeStruct((lev_dev, own, 2 * cols), F32)
    return pl.pallas_call(
        backward_kernel,
        in_specs=[vmem] * 7,
        out_specs=[anywhere] * 3,
        out_shape=[jax.ShapeDtypeStruct((members, modes, rows, cols), F32), field, field],
        scratch_shapes=[
            pltpu.VMEM(done.shape, F32),
            pltpu.SemaphoreType.DMA((1 + rows // (2 * PIECE),)),
            pltpu.SemaphoreType.DMA((4,)),
        ],
        compiler_params=pltpu.CompilerParams(vmem_limit_bytes=6 << 20),
        name="backward_modes",
    )(lhs, count, amp, wide, grad, planes, done)


def exchange_kernel(
    sizes,
    modes_in,
    count_in,
    amp_ref,
    pert_ref,
    control_ref,
    innov_ref,
    std_in,
    spread_in,
    land_in,
    row_index_in,
    row_weight_in,
    col_index_in,
    col_weight_in,
    amp_out,
    wide,
    shares,
    planes_out,
    count_ref,
    back_lhs_ref,
    done,
    modes_ref,
    tile,
    narrow,
    core_in,
    x_in,
    pair_x_in,
    pair_y_in,
    y_in,
    window,
    field_a,
    field_b,
    misfit,
    cells,
    row_faces,
    col_faces,
    centre,
    weights,
    sigma,
    col_mat,
    back,
    planes_in,
    std_ref,
    spread_ref,
    land_ref,
    row_index_ref,
    row_weight_ref,
    col_index_ref,
    col_weight_ref,
    send_sem,
    recv_sem,
    load_sem,
    plane_sem,
    small_sem,
):
    coarse_count, fine_count, rows_all = sizes
    xs = fine_count // 2
    coarse = lax.axis_index("coarse")
    fine = lax.axis_index("fine")
    lev = lax.axis_index("lev")
    x = lax.rem(fine, xs)
    y = fine // xs
    right, left, across = lax.rem(x + 1, xs), lax.rem(x + xs - 1, xs), lax.rem(x + 2, xs)
    other_y = 1 - y
    serial = coarse * fine_count + fine
    count = coarse_count * fine_count
    after, before = lax.rem(serial + 1, count), lax.rem(serial + count - 1, count)
    first_row = serial * 2 * ROWS
    members, modes = amp_ref.shape[:2]
    levels = pert_ref.shape[1]
    sums = tile.at[lev]

    to_core = (coarse, fine, 1 - lev)
    to_right = (coarse, y * xs + right, lev)
    to_left = (coarse, y * xs + left, lev)
    to_across = (coarse, y * xs + across, lev)
    to_y = (coarse, other_y * xs + x, lev)
    to_after = (after // fine_count, lax.rem(after, fine_count), lev)
    to_before = (before // fine_count, lax.rem(before, fine_count), lev)

    barrier = pltpu.get_barrier_semaphore()
    for device in (to_core, to_right, to_left, to_across, to_y, to_after, to_before):
        pl.semaphore_signal(barrier, inc=1, device_id=device, device_id_type=pl.DeviceIdType.MESH)

    numbers = iter(range(100))
    sent = []

    def remote(src, dst, device):
        number = next(numbers)
        copy = pltpu.make_async_remote_copy(
            src_ref=src,
            dst_ref=dst,
            send_sem=send_sem.at[number],
            recv_sem=recv_sem.at[number],
            device_id=device,
            device_id_type=pl.DeviceIdType.MESH,
        )
        copy.start()
        sent.append(copy)
        return copy

    def share(ry, rx):
        return (ry * xs + rx) * ROWS

    lev_dev = control_ref.shape[0]
    own = 2 * ROWS
    half_rows = xs * ROWS
    lanes = [pl.ds(0, 128), pl.ds(128, 128)]

    count_load = pltpu.make_async_copy(count_in, count_ref, small_sem.at[7])
    count_load.start()
    modes_load = pltpu.make_async_copy(modes_in, modes_ref, small_sem.at[8])
    modes_load.start()
    pert_in, amp_in = [], []

    def load_half(half):
        at = pl.ds(pl.multiple_of((other_y, y)[half] * half_rows, 16), half_rows)
        for k in range(members):
            copy = pltpu.make_async_copy(
                pert_ref.at[k, :, at, :], narrow.at[k, :, at, :], load_sem.at[half * members + k]
            )
            copy.start()
            pert_in.append(copy)
        for part in (0, 1):
            column = lax.rem(across // 2 + part, 2)
            start = (other_y, y)[half] * half_rows + column * PIECE
            at = pl.ds(pl.multiple_of(start, PIECE), PIECE)
            copy = pltpu.make_async_copy(
                amp_ref.at[:, :, at, :],
                amp_out.at[:, :, at, :],
                load_sem.at[2 * members + 2 * half + part],
            )
            copy.start()
            amp_in.append(copy)

    load_half(0)
    plane_in = [
        [
            pltpu.make_async_copy(
                ref.at[:, :, lanes[side]],
                planes_in.at[number, side],
                plane_sem.at[2 * number + side],
            )
            for side in range(2)
        ]
        for number, ref in enumerate((control_ref, innov_ref))
    ]
    small_in = [
        pltpu.make_async_copy(src, dst, small_sem.at[number])
        for number, (src, dst) in enumerate(
            (
                (spread_in, spread_ref),
                (land_in, land_ref),
                (row_index_in, row_index_ref),
                (row_weight_in, row_weight_ref),
                (std_in, std_ref),
                (col_index_in, col_index_ref),
                (col_weight_in, col_weight_ref),
            )
        )
    ]
    for copy in small_in + plane_in[0]:
        copy.start()
    load_half(1)
    for copy in plane_in[1]:
        copy.start()

    def planes(ref, number, side):
        return ref.at[number, side].reshape(lev_dev * own, 128)

    def widen(half):
        at = pl.ds(pl.multiple_of((other_y, y)[half] * half_rows, 16), half_rows)
        for k in range(members):
            pert_in[half * members + k].wait()

            def widen_level(level, carry):
                wide[k, level, at] = narrow[k, level, at].astype(F32)
                return carry

            lax.fori_loop(0, levels, widen_level, 0, unroll=8)

    def x_rows(ry, rx):
        return pl.ds(share(ry, rx), XROWS)

    def y_rows(ry, rx):
        return pl.ds(share(ry, rx) + XROWS, YROWS)

    def add(rows, *terms):
        total = sums[rows]
        for term in terms:
            total = total + term[...]
        sums[rows] = total

    amps = amp_out.reshape(members * modes * PITCH, 128)
    perts = wide.reshape(members * levels * PITCH, 128)
    modes_load.wait()
    scaled = modes_ref[...] * (1.0 / math.sqrt(MEMBERS - 1))
    scaled_hi = scaled.astype(BF16).astype(F32)
    scaled_lo = scaled - scaled_hi
    lhs = jnp.concatenate([scaled_hi, scaled_lo, scaled_hi], axis=0).T.astype(BF16)
    back_lhs = jnp.concatenate([scaled_hi, scaled_lo, scaled_hi], axis=1).astype(BF16)
    back_lhs_ref[...] = back_lhs
    mode = lax.broadcasted_iota(jnp.int32, (modes, 128), 0)

    def contract(start):
        def row_pair(step, carry):
            first = start + step * 2
            keep = [mode < count_ref[pl.ds(first + h, 1), :] for h in range(2)]
            total = [jnp.zeros((levels, 128), F32) for _ in range(2)]
            for k in range(members):
                rhs = []
                for h in range(2):
                    amp = amps[pl.ds(k * modes * PITCH + first + h, modes, stride=PITCH), :]
                    rhs.append(stacked(jnp.where(keep[h], amp, 0.0)))
                level_amp = jnp.dot(lhs, jnp.concatenate(rhs, axis=1), preferred_element_type=F32)
                for h in range(2):
                    pert = perts[pl.ds(k * levels * PITCH + first + h, levels, stride=PITCH), :]
                    total[h] = total[h] + pert * level_amp[:, h * 128 : (h + 1) * 128]
            for h in range(2):
                tile[0, first + h] = total[h][: levels // 2]
                tile[1, first + h] = total[h][levels // 2 :]
            return carry

        lax.fori_loop(0, ROWS // 2, row_pair, 0, unroll=3)

    order = [(ry, rx) for ry in (other_y, y) for rx in (across, right, left, x)]
    ring = ((across, to_across), (right, to_right), (left, to_left))
    origins = (left, right, across)
    core_sends = []
    to_ring = [[], []]
    to_pair = []
    to_own = []

    def produce(number):
        contract(share(*order[number]))

    def send_core(number):
        rows = pl.ds(share(*order[number]), ROWS)
        core_sends.append(remote(tile.at[1 - lev, rows], core_in.at[rows], to_core))

    def settle(number):
        core_sends[number].wait_recv()
        rows = pl.ds(share(*order[number]), ROWS)
        add(rows, core_in.at[rows])
        half, place = number // 4, number % 4
        if place < 3:
            rx, device = ring[place]
            to_ring[half].append(
                remote(sums.at[x_rows(*order[number])], x_in.at[half, place], device)
            )
        if half == 0:
            rx = order[number][1]
            to_pair.append(remote(sums.at[y_rows(other_y, rx)], pair_y_in.at[place], to_y))

    def settle_pair(place):
        to_pair[place].wait_recv()
        rx = order[place][1]
        add(y_rows(y, rx), pair_y_in.at[place])
        if place < 3:
            to_own.append(remote(sums.at[y_rows(y, rx)], y_in.at[place], ring[place][1]))

    count_load.wait()
    widen(0)
    amp_in[0].wait()
    produce(0)
    pl.semaphore_wait(barrier, 7)
    send_core(0)
    amp_in[1].wait()
    produce(1)
    send_core(1)
    produce(2)
    send_core(2)
    settle(0)
    produce(3)
    send_core(3)
    settle(1)
    settle(2)

    for copy in small_in + plane_in[0]:
        copy.wait()

    def load_rows(i, carry):
        for side in range(2):
            field_a[EDGE + i, :, lanes[side]] = planes(planes_in, 0, side)[
                pl.ds(i, lev_dev, stride=own), :
            ]
        sub = lax.broadcasted_iota(jnp.int32, (8, 256), 0)
        weight = jnp.full((8, 256), row_weight_ref[i], F32)
        index = jnp.full((8, 256), row_index_ref[i], jnp.int32)
        upper = (index == (first_row + i) // 2).astype(F32)
        spread = jnp.broadcast_to(spread_ref[pl.ds(i, 1), :], (8, 256))
        land = jnp.broadcast_to(land_ref[pl.ds(i, 1), :], (8, 256)).astype(F32)
        cells[EDGE + i] = jnp.where(
            sub == 0, spread, jnp.where(sub == 1, land, jnp.where(sub == 2, weight, upper))
        )
        return carry

    lax.fori_loop(0, own, load_rows, 0, unroll=8)
    top, bottom = pl.ds(EDGE, HALO), pl.ds(EDGE + own - HALO, HALO)
    low, high = pl.ds(EDGE - HALO, HALO), pl.ds(EDGE + own, HALO)
    halo_sends = [
        remote(ref.at[src], ref.at[dst], device)
        for ref in (cells, field_a)
        for src, dst, device in ((top, high, to_before), (bottom, low, to_after))
    ]
    settle(3)

    widen(1)
    amp_in[2].wait()
    produce(4)
    send_core(4)
    amp_in[3].wait()
    produce(5)
    send_core(5)
    settle(4)
    settle_pair(0)
    produce(6)
    send_core(6)
    settle(5)
    produce(7)
    send_core(7)
    settle(6)
    settle_pair(1)
    for copy in to_ring[0]:
        copy.wait_recv()
    add(x_rows(other_y, x), x_in.at[0, 0], x_in.at[0, 1], x_in.at[0, 2])
    pair_x = remote(sums.at[x_rows(other_y, x)], pair_x_in, to_y)

    for ref in (cells, misfit):
        ref[0] = jnp.zeros(ref.shape[1:], F32)
        ref[GROWN - 1] = jnp.zeros(ref.shape[1:], F32)
    for row in (1, GROWN - 2):
        field_b[row] = jnp.zeros(field_b.shape[1:], F32)
    for lev_at in range(lev_dev):
        sigma[lev_at : lev_at + 1, :] = jnp.full((1, 256), std_ref[lev_at], F32)
    for copy in halo_sends[:2]:
        copy.wait_recv()

    def coefficients(e, carry):
        here, there = cells[e], cells[e + 1]
        line = first_row - EDGE + e
        inside = (line >= 0) & (line < rows_all) & (e >= 1) & (e <= GROWN - 2)
        facing = (line >= 0) & (line + 1 < rows_all)
        inside = jnp.where(inside, 1.0, 0.0).astype(F32)
        facing = jnp.where(facing, 1.0, 0.0).astype(F32)
        lane = lax.broadcasted_iota(jnp.int32, (8, 256), 1)
        spread, land = (jnp.broadcast_to(here[j : j + 1], (8, 256)) for j in (0, 1))
        spread_next, land_next = (jnp.broadcast_to(there[j : j + 1], (8, 256)) for j in (0, 1))
        row_face = (
            jnp.sqrt(spread * spread_next) * (1.0 - 0.5 * jnp.abs(land - land_next)) * facing
        )
        row_faces[e] = row_face
        spread_right, land_right = (pltpu.roll(v, 255, 1) for v in (spread, land))
        col_face = jnp.where(
            lane < 255,
            jnp.sqrt(spread * spread_right) * (1.0 - 0.5 * jnp.abs(land - land_right)),
            0.0,
        )
        col_before = pltpu.roll(col_face, 1, 1)
        col_faces[0, e] = col_face
        col_faces[1, e] = col_before
        centre[e] = 1.0 - (row_face + col_face + col_before)
        weight, upper = (jnp.broadcast_to(here[j : j + 1, :128], (8, 128)) for j in (2, 3))
        upper_on = upper > 0.5
        weights[0, e] = jnp.where(upper_on, 0.0, 1.0 - weight) * inside
        weights[1, e] = jnp.where(upper_on, 1.0 - weight, weight) * inside
        weights[2, e] = jnp.where(upper_on, weight, 0.0) * inside
        return carry

    lax.fori_loop(0, 15, coefficients, 0, unroll=5)
    settle_pair(2)
    lax.fori_loop(15, GROWN - 1, coefficients, 0, unroll=4)
    inner = pl.ds(1, GROWN - 2)
    centre[inner] = centre[inner] - row_faces[pl.ds(0, GROWN - 2)]
    for j in range(3):
        weights[j, GROWN - 1] = jnp.zeros((8, 128), F32)
    col = lax.broadcasted_iota(jnp.int32, (128, 256), 0)
    col_at, col_w = col_index_ref[...], col_weight_ref[...]
    matrix = jnp.where(col == col_at, 1.0 - col_w, jnp.where(col == col_at + 1, col_w, 0.0))
    hi, lo = halves(matrix)
    col_mat[0], col_mat[1] = hi, lo

    def sweep(src, dst, first=0, last=7):
        def rows_of_four(step, carry):
            e = EDGE - 2 + 4 * step
            at_four = pl.ds(e, 4)
            down = row_faces[pl.ds(e - 1, 5)]
            to_right_face, to_left_face = col_faces[0, at_four], col_faces[1, at_four]
            keep = centre[at_four]
            for tile_at in range(lev_dev // 8):
                at = pl.ds(8 * tile_at, 8)
                v = src[pl.ds(e - 1, 6), at, :]
                mid = v[1:5]
                dst[at_four, at, :] = (
                    keep * mid
                    + (down[1:] * v[2:] + down[:-1] * v[:-2])
                    + to_right_face * pltpu.roll(mid, 255, 2)
                    + to_left_face * pltpu.roll(mid, 1, 2)
                )
            return carry

        lax.fori_loop(first, last, rows_of_four, 0)

    settle(7)
    for copy in halo_sends[2:]:
        copy.wait_recv()
        copy.wait_send()
    sweep(field_a, field_b)
    sweep(field_b, field_a)
    settle_pair(3)
    for copy in to_ring[1]:
        copy.wait_recv()
    add(x_rows(y, x), x_in.at[1, 0], x_in.at[1, 1], x_in.at[1, 2])
    sweep(field_a, field_b)

    def static_part(i, carry):
        for side in range(2):
            cols = lanes[side]
            misfit[EDGE + i, :, cols] = (
                sigma[:, cols] * field_b[EDGE + i, :, cols]
                - planes(planes_in, 1, side)[pl.ds(i, lev_dev, stride=own), :]
            )
        return carry

    for copy in plane_in[1]:
        copy.wait()
    lax.fori_loop(0, own, static_part, 0, unroll=8)
    halo_again = [
        remote(misfit.at[top], misfit.at[high], to_before),
        remote(misfit.at[bottom], misfit.at[low], to_after),
    ]

    for copy in to_own:
        copy.wait_recv()
    mine = share(y, x)
    window[pl.ds(HALO + XROWS, YROWS)] = sums[y_rows(y, x)] + y_in[0] + (y_in[1] + y_in[2])
    pair_x.wait_recv()
    window[pl.ds(HALO, XROWS)] = sums[x_rows(y, x)] + pair_x_in[...]
    halo_again += [
        remote(window.at[pl.ds(ROWS, HALO)], window.at[pl.ds(0, HALO)], to_after),
        remote(window.at[pl.ds(HALO, HALO)], window.at[pl.ds(HALO + ROWS, HALO)], to_before),
    ]

    def dot_split(lhs, which):
        hi, lo = halves(lhs)
        c_hi, c_lo = col_mat[0], col_mat[1]
        dims = (((1,), (which,)), ((), ()))
        dot = functools.partial(lax.dot_general, dimension_numbers=dims, preferred_element_type=F32)
        return dot(hi, c_hi) + (dot(lo, c_hi) + dot(hi, c_lo))

    span = 8

    def interpolate(step, carry):
        e0 = step * span
        lines = []
        for pair in range(span // 2):
            t = step * (span // 2) + pair + 1
            w = [window[t + d].reshape(lev_dev // 8, 8, 128) for d in (-1, 0, 1)]
            for h in range(2):
                e = e0 + 2 * pair + h
                line = weights[0, e] * w[0] + weights[1, e] * w[1] + weights[2, e] * w[2]
                lines.append(line.reshape(lev_dev, 128))
        fine_part = dot_split(jnp.concatenate(lines, axis=0), 0)
        at = pl.ds(e0, span)
        total = misfit[at] + fine_part.reshape(span, lev_dev, 256)
        misfit[at] = total
        field_a[at] = sigma[...] * total
        back[at] = dot_split(total.reshape(span * lev_dev, 256), 1).reshape(span, lev_dev, 128)
        return carry

    lax.fori_loop(1, 3, interpolate, 0, unroll=2)
    for copy in halo_again:
        copy.wait_recv()
    for copy in halo_again[:2]:
        copy.wait_send()
    interpolate(0, 0)
    interpolate(3, 0)

    def adjoint(r, carry):
        e = 2 * r + 2
        total = jnp.zeros((lev_dev // 8, 8, 128), F32)
        for j in range(6):
            total = total + weights[2 - j // 2, e + j] * back[e + j].reshape(lev_dev // 8, 8, 128)
        shares[lev, mine + r] = total.reshape(lev_dev, 128)
        return carry

    lax.fori_loop(0, ROWS, adjoint, 0, unroll=12)

    def to_all(rows, device):
        return remote(shares.at[lev, rows], shares.at[lev, rows], device)

    def to_ring_of(rows):
        return [to_all(rows, device) for device in (to_right, to_left, to_across)]

    pair_first = to_all(x_rows(y, x), to_y)
    ring_y = to_ring_of(y_rows(y, x))
    pair_y = [to_all(y_rows(y, x), to_y)]
    ring_own = to_ring_of(x_rows(y, x))
    core = [to_all(pl.ds(mine, ROWS), to_core)]

    dones = done.reshape(members * modes * HALF_PITCH, 128)

    def project(rx):
        def row_pair(step, carry):
            row = rx * ROWS + step * 2
            project_row_pair(
                back_lhs,
                count_ref,
                amps,
                perts,
                dones,
                shares,
                (members, modes, levels),
                y * half_rows + row,
                row,
            )
            return carry

        lax.fori_loop(0, ROWS // 2, row_pair, 0, unroll=3)

    core_y, core_x = [], []

    def share_y(number):
        ring_y[number].wait_recv()
        rows = y_rows(y, origins[number])
        pair_y.append(to_all(rows, to_y))
        core_y.append(to_all(rows, to_core))

    def share_x(number):
        ring_own[number].wait_recv()
        core_x.append(to_all(x_rows(y, origins[number]), to_core))

    def pass_on(number):
        pair_y[number].wait_recv()
        core.append(to_all(y_rows(other_y, (x, *origins)[number]), to_core))

    def project_origin(number):
        core_x[number].wait_recv()
        core_y[number].wait_recv()
        project(origins[number])

    sweep(field_a, field_b)
    core[0].wait_recv()
    project(x)
    sweep(field_b, field_a)
    pair_first.wait_recv()
    ring_other = to_ring_of(x_rows(other_y, x))
    core.append(to_all(x_rows(other_y, x), to_core))
    share_y(0)
    share_y(1)
    sweep(field_a, field_b)

    def finish(i, carry):
        at = pl.ds(i, lev_dev, stride=own)
        for side in range(2):
            for number, value in ((0, field_b), (1, misfit)):
                planes(planes_out, number, side)[at, :] = (
                    planes(planes_in, number, side)[at, :] + value[EDGE + i, :, lanes[side]]
                )
        return carry

    lax.fori_loop(0, own, finish, 0, unroll=8)
    share_y(2)
    share_x(0)
    share_x(1)
    pass_on(0)
    project_origin(0)
    share_x(2)
    pass_on(1)
    project_origin(1)
    pass_on(2)
    pass_on(3)
    for copy, rx in zip(ring_other, origins):
        copy.wait_recv()
        core.append(to_all(x_rows(other_y, rx), to_core))
    project_origin(2)
    for copy in core[1:]:
        copy.wait_recv()
    waited = halo_sends[2:] + halo_again[:2]
    for copy in sent:
        if not any(copy is done for done in waited):
            copy.wait_send()


def exchange(sizes, modes_t, count, amp, pert, control, innov, std, spread, land, row_index, row_weight, col_index, col_weight):
    members, modes, rows, cols = amp.shape
    levels = pert.shape[1]
    lev_dev, own, cols_fine = control.shape
    vmem = pl.BlockSpec(memory_space=pltpu.VMEM)
    anywhere = pl.BlockSpec(memory_space=pl.ANY)
    cell = (lev_dev, 128)
    row = (lev_dev, cols_fine)
    tile = (2, rows) + cell
    return pl.pallas_call(
        functools.partial(exchange_kernel, sizes),
        in_specs=[anywhere] * 13,
        out_specs=[vmem] * 7,
        out_shape=[
            pltpu.VMEM((members, modes, PITCH, cols), F32),
            pltpu.VMEM((members, levels, PITCH, cols), F32),
            pltpu.VMEM(tile, F32),
            pltpu.VMEM((2, 2, lev_dev, own, 128), F32),
            pltpu.VMEM(count.shape, jnp.int32),
            pltpu.VMEM((modes, 3 * levels), BF16),
            pltpu.VMEM((members, modes, HALF_PITCH, cols), F32),
        ],
        scratch_shapes=[
            pltpu.VMEM(modes_t.shape, F32),
            pltpu.VMEM(tile, F32),
            pltpu.VMEM(pert.shape, BF16),
            pltpu.VMEM((rows,) + cell, F32),
            pltpu.VMEM((2, 3, XROWS) + cell, F32),
            pltpu.VMEM((XROWS,) + cell, F32),
            pltpu.VMEM((4, YROWS) + cell, F32),
            pltpu.VMEM((3, YROWS) + cell, F32),
            pltpu.VMEM((ROWS + 2 * HALO,) + cell, F32),
            pltpu.VMEM((GROWN,) + row, F32),
            pltpu.VMEM((GROWN,) + row, F32),
            pltpu.VMEM((GROWN,) + row, F32),
            pltpu.VMEM((GROWN, 8, cols_fine), F32),
            pltpu.VMEM((GROWN, 8, cols_fine), F32),
            pltpu.VMEM((2, GROWN, 8, cols_fine), F32),
            pltpu.VMEM((GROWN, 8, cols_fine), F32),
            pltpu.VMEM((3, GROWN, 8, 128), F32),
            pltpu.VMEM(row, F32),
            pltpu.VMEM((2, 128, cols_fine), BF16),
            pltpu.VMEM((GROWN,) + cell, F32),
            pltpu.VMEM((2, 2, lev_dev, own, 128), F32),
            pltpu.SMEM(std.shape, F32),
            pltpu.VMEM(spread.shape, F32),
            pltpu.VMEM(land.shape, jnp.int32),
            pltpu.SMEM(row_index.shape, jnp.int32),
            pltpu.SMEM(row_weight.shape, F32),
            pltpu.VMEM((1, cols_fine), jnp.int32),
            pltpu.VMEM((1, cols_fine), F32),
            pltpu.SemaphoreType.DMA((80,)),
            pltpu.SemaphoreType.DMA((80,)),
            pltpu.SemaphoreType.DMA((2 * members + 4,)),
            pltpu.SemaphoreType.DMA((4,)),
            pltpu.SemaphoreType.DMA((9,)),
        ],
        compiler_params=pltpu.CompilerParams(
            collective_id=0, has_side_effects=True, vmem_limit_bytes=18 << 20
        ),
        name="exchange",
    )(
        *(
            pltpu.with_memory_space_constraint(operand, pltpu.HBM)
            for operand in (
                modes_t,
                count,
                amp,
                pert,
                control,
                innov,
                std,
                spread,
                land,
                row_index,
                row_weight,
                col_index.reshape(1, cols_fine),
                col_weight.reshape(1, cols_fine),
            )
        ),
    )


def local(
    ens_pert,
    ens_control,
    eigen_modes,
    mode_count,
    row_index,
    row_weight,
    col_index,
    col_weight,
    static_control,
    static_std,
    diffusivity,
    land_mask,
    innovation,
):
    sizes = (
        lax.axis_size("coarse"),
        lax.axis_size("fine"),
        lax.axis_size("coarse") * lax.axis_size("fine") * row_index.shape[0],
    )
    amp, wide, coarse_grad, planes, count, back_lhs, done = exchange(
        sizes,
        eigen_modes.T,
        mode_count,
        ens_control,
        ens_pert,
        static_control,
        innovation,
        static_std,
        diffusivity,
        land_mask,
        row_index,
        row_weight,
        col_index,
        col_weight,
    )
    grad_ens, grad_static, increment = backward(
        back_lhs, count, amp, wide, coarse_grad, planes, done, mode_count.shape[0]
    )
    return increment, grad_static, grad_ens


def solution(mesh):
    in_specs = (
        P(("fine", "lev"), None, "coarse", None),
        P(("fine", "lev"), None, "coarse", None),
        P(),
        P("coarse", None),
        P(("coarse", "fine")),
        P(("coarse", "fine")),
        P(),
        P(),
        P("lev", ("coarse", "fine"), None),
        P("lev"),
        P(("coarse", "fine"), None),
        P(("coarse", "fine"), None),
        P("lev", ("coarse", "fine"), None),
    )
    out_specs = (
        P("lev", ("coarse", "fine"), None),
        P("lev", ("coarse", "fine"), None),
        P(("fine", "lev"), None, "coarse", None),
    )
    return jax.shard_map(local, mesh=mesh, in_specs=in_specs, out_specs=out_specs, check_vma=False)
```

```python
import functools
import math

import jax
import jax.numpy as jnp
from jax import lax
from jax.experimental import pallas as pl
from jax.experimental.pallas import tpu as pltpu
from jax.sharding import PartitionSpec as P

MEMBERS = 80
NSWEEP = 3
HALO = 3
EDGE = 4
GROWN = 32
ROWS = 12
XROWS = 5
YROWS = ROWS - XROWS
PITCH = 104
HALF_PITCH = 56
PIECE = 24
F32 = jnp.float32
BF16 = jnp.bfloat16


def halves(value):
    hi = value.astype(BF16)
    return hi, (value - hi.astype(F32)).astype(BF16)


def stacked(value):
    hi, lo = halves(value)
    return jnp.concatenate([hi, hi, lo], axis=0)


def project_row_pair(lhs, keep_from, amps, perts, outs, grad_ref, sizes, first, out_first):
    members, modes, levels = sizes
    mode = lax.broadcasted_iota(jnp.int32, (modes, 128), 0)
    keep = [mode < keep_from[pl.ds(first + h, 1), :] for h in range(2)]
    grad = [
        jnp.concatenate([grad_ref[0, first + h], grad_ref[1, first + h]], axis=0) for h in range(2)
    ]
    for k in range(members):
        rhs = []
        for h in range(2):
            pert = perts[pl.ds(k * levels * PITCH + first + h, levels, stride=PITCH), :]
            rhs.append(stacked(pert * grad[h]))
        proj = jnp.dot(lhs, jnp.concatenate(rhs, axis=1), preferred_element_type=F32)
        for h in range(2):
            amp = amps[pl.ds(k * modes * PITCH + first + h, modes, stride=PITCH), :]
            at = pl.ds(k * modes * HALF_PITCH + out_first + h, modes, stride=HALF_PITCH)
            outs[at, :] = amp + jnp.where(keep[h], proj[:, h * 128 : (h + 1) * 128], 0.0)


def backward_kernel(
    lhs_ref,
    count_ref,
    amp_ref,
    wide_ref,
    grad_ref,
    planes_ref,
    done_ref,
    out_ref,
    grad_static_ref,
    inc_ref,
    result,
    out_sem,
    plane_sem,
):
    members, modes = amp_ref.shape[:2]
    levels = wide_ref.shape[1]
    half_rows = out_ref.shape[2] // 2
    y = lax.axis_index("fine") // (lax.axis_size("fine") // 2)
    at = pl.ds(pl.multiple_of(y * half_rows, 8), half_rows)
    copies = [
        pltpu.make_async_copy(
            done_ref.at[:, :, pl.ds(0, half_rows), :], out_ref.at[:, :, at, :], out_sem.at[0]
        )
    ]
    copies += [
        pltpu.make_async_copy(
            planes_ref.at[number, side],
            ref.at[:, :, pl.ds(128 * side, 128)],
            plane_sem.at[2 * number + side],
        )
        for number, ref in enumerate((grad_static_ref, inc_ref))
        for side in range(2)
    ]
    for copy in copies:
        copy.start()
    amps = amp_ref.reshape(members * modes * PITCH, 128)
    perts = wide_ref.reshape(members * levels * PITCH, 128)
    outs = result.reshape(members * modes * HALF_PITCH, 128)
    lhs = lhs_ref[...]
    base = (1 - y) * half_rows
    for piece in range(half_rows // PIECE):

        def row_pair(step, carry):
            row = piece * PIECE + step * 2
            project_row_pair(
                lhs, count_ref, amps, perts, outs, grad_ref, (members, modes, levels), base + row, row
            )
            return carry

        lax.fori_loop(0, PIECE // 2, row_pair, 0, unroll=4)
        copy = pltpu.make_async_copy(
            result.at[:, :, pl.ds(piece * PIECE, PIECE), :],
            out_ref.at[:, :, pl.ds(pl.multiple_of(base + piece * PIECE, 8), PIECE), :],
            out_sem.at[1 + piece],
        )
        copy.start()
        copies.append(copy)
    for copy in copies:
        copy.wait()


def backward(lhs, count, amp, wide, grad, planes, done, rows):
    members, modes, _, cols = amp.shape
    lev_dev, own = planes.shape[2:4]
    vmem = pl.BlockSpec(memory_space=pltpu.VMEM)
    anywhere = pl.BlockSpec(memory_space=pl.ANY)
    field = jax.ShapeDtypeStruct((lev_dev, own, 2 * cols), F32)
    return pl.pallas_call(
        backward_kernel,
        in_specs=[vmem] * 7,
        out_specs=[anywhere] * 3,
        out_shape=[jax.ShapeDtypeStruct((members, modes, rows, cols), F32), field, field],
        scratch_shapes=[
            pltpu.VMEM(done.shape, F32),
            pltpu.SemaphoreType.DMA((1 + rows // (2 * PIECE),)),
            pltpu.SemaphoreType.DMA((4,)),
        ],
        compiler_params=pltpu.CompilerParams(vmem_limit_bytes=6 << 20),
        name="backward_modes",
    )(lhs, count, amp, wide, grad, planes, done)


def exchange_kernel(
    sizes,
    modes_in,
    count_in,
    amp_ref,
    pert_ref,
    control_ref,
    innov_ref,
    std_in,
    spread_in,
    land_in,
    row_index_in,
    row_weight_in,
    col_index_in,
    col_weight_in,
    amp_out,
    wide,
    shares,
    planes_out,
    count_ref,
    back_lhs_ref,
    done,
    modes_ref,
    tile,
    narrow,
    core_in,
    x_in,
    pair_x_in,
    pair_y_in,
    y_in,
    window,
    field_a,
    field_b,
    misfit,
    cells,
    row_faces,
    col_faces,
    centre,
    weights,
    sigma,
    col_mat,
    back,
    planes_in,
    std_ref,
    spread_ref,
    land_ref,
    row_index_ref,
    row_weight_ref,
    col_index_ref,
    col_weight_ref,
    send_sem,
    recv_sem,
    load_sem,
    plane_sem,
    small_sem,
):
    coarse_count, fine_count, rows_all = sizes
    xs = fine_count // 2
    coarse = lax.axis_index("coarse")
    fine = lax.axis_index("fine")
    lev = lax.axis_index("lev")
    x = lax.rem(fine, xs)
    y = fine // xs
    right, left, across = lax.rem(x + 1, xs), lax.rem(x + xs - 1, xs), lax.rem(x + 2, xs)
    other_y = 1 - y
    serial = coarse * fine_count + fine
    count = coarse_count * fine_count
    after, before = lax.rem(serial + 1, count), lax.rem(serial + count - 1, count)
    first_row = serial * 2 * ROWS
    members, modes = amp_ref.shape[:2]
    levels = pert_ref.shape[1]
    sums = tile.at[lev]

    to_core = (coarse, fine, 1 - lev)
    to_right = (coarse, y * xs + right, lev)
    to_left = (coarse, y * xs + left, lev)
    to_across = (coarse, y * xs + across, lev)
    to_y = (coarse, other_y * xs + x, lev)
    to_after = (after // fine_count, lax.rem(after, fine_count), lev)
    to_before = (before // fine_count, lax.rem(before, fine_count), lev)

    barrier = pltpu.get_barrier_semaphore()
    for device in (to_core, to_right, to_left, to_across, to_y, to_after, to_before):
        pl.semaphore_signal(barrier, inc=1, device_id=device, device_id_type=pl.DeviceIdType.MESH)

    numbers = iter(range(100))
    sent = []

    def remote(src, dst, device):
        number = next(numbers)
        copy = pltpu.make_async_remote_copy(
            src_ref=src,
            dst_ref=dst,
            send_sem=send_sem.at[number],
            recv_sem=recv_sem.at[number],
            device_id=device,
            device_id_type=pl.DeviceIdType.MESH,
        )
        copy.start()
        sent.append(copy)
        return copy

    def share(ry, rx):
        return (ry * xs + rx) * ROWS

    lev_dev = control_ref.shape[0]
    own = 2 * ROWS
    half_rows = xs * ROWS
    lanes = [pl.ds(0, 128), pl.ds(128, 128)]

    count_load = pltpu.make_async_copy(count_in, count_ref, small_sem.at[7])
    count_load.start()
    modes_load = pltpu.make_async_copy(modes_in, modes_ref, small_sem.at[8])
    modes_load.start()
    pert_in, amp_in = [], []

    def load_half(half):
        at = pl.ds(pl.multiple_of((other_y, y)[half] * half_rows, 16), half_rows)
        for k in range(members):
            copy = pltpu.make_async_copy(
                pert_ref.at[k, :, at, :], narrow.at[k, :, at, :], load_sem.at[half * members + k]
            )
            copy.start()
            pert_in.append(copy)
        for part in (0, 1):
            column = lax.rem(across // 2 + part, 2)
            start = (other_y, y)[half] * half_rows + column * PIECE
            at = pl.ds(pl.multiple_of(start, PIECE), PIECE)
            copy = pltpu.make_async_copy(
                amp_ref.at[:, :, at, :],
                amp_out.at[:, :, at, :],
                load_sem.at[2 * members + 2 * half + part],
            )
            copy.start()
            amp_in.append(copy)

    small_in = [
        pltpu.make_async_copy(src, dst, small_sem.at[number])
        for number, (src, dst) in enumerate(
            (
                (spread_in, spread_ref),
                (land_in, land_ref),
                (row_index_in, row_index_ref),
                (row_weight_in, row_weight_ref),
                (std_in, std_ref),
                (col_index_in, col_index_ref),
                (col_weight_in, col_weight_ref),
            )
        )
    ]
    for copy in small_in:
        copy.start()
    load_half(0)
    plane_in = [
        [
            pltpu.make_async_copy(
                ref.at[:, :, lanes[side]],
                planes_in.at[number, side],
                plane_sem.at[2 * number + side],
            )
            for side in range(2)
        ]
        for number, ref in enumerate((control_ref, innov_ref))
    ]
    for copy in plane_in[0]:
        copy.start()
    load_half(1)
    for copy in plane_in[1]:
        copy.start()

    def planes(ref, number, side):
        return ref.at[number, side].reshape(lev_dev * own, 128)

    def widen(half):
        at = pl.ds(pl.multiple_of((other_y, y)[half] * half_rows, 16), half_rows)
        for k in range(members):
            pert_in[half * members + k].wait()

            def widen_level(level, carry):
                wide[k, level, at] = narrow[k, level, at].astype(F32)
                return carry

            lax.fori_loop(0, levels, widen_level, 0, unroll=8)

    def x_rows(ry, rx):
        return pl.ds(share(ry, rx), XROWS)

    def y_rows(ry, rx):
        return pl.ds(share(ry, rx) + XROWS, YROWS)

    def add(rows, *terms):
        total = sums[rows]
        for term in terms:
            total = total + term[...]
        sums[rows] = total

    amps = amp_out.reshape(members * modes * PITCH, 128)
    perts = wide.reshape(members * levels * PITCH, 128)
    modes_load.wait()
    scaled = modes_ref[...] * (1.0 / math.sqrt(MEMBERS - 1))
    scaled_hi = scaled.astype(BF16).astype(F32)
    scaled_lo = scaled - scaled_hi
    lhs = jnp.concatenate([scaled_hi, scaled_lo, scaled_hi], axis=0).T.astype(BF16)
    back_lhs = jnp.concatenate([scaled_hi, scaled_lo, scaled_hi], axis=1).astype(BF16)
    back_lhs_ref[...] = back_lhs
    mode = lax.broadcasted_iota(jnp.int32, (modes, 128), 0)

    def contract(start):
        def row_pair(step, carry):
            first = start + step * 2
            keep = [mode < count_ref[pl.ds(first + h, 1), :] for h in range(2)]
            total = [jnp.zeros((levels, 128), F32) for _ in range(2)]
            for k in range(members):
                rhs = []
                for h in range(2):
                    amp = amps[pl.ds(k * modes * PITCH + first + h, modes, stride=PITCH), :]
                    rhs.append(stacked(jnp.where(keep[h], amp, 0.0)))
                level_amp = jnp.dot(lhs, jnp.concatenate(rhs, axis=1), preferred_element_type=F32)
                for h in range(2):
                    pert = perts[pl.ds(k * levels * PITCH + first + h, levels, stride=PITCH), :]
                    total[h] = total[h] + pert * level_amp[:, h * 128 : (h + 1) * 128]
            for h in range(2):
                tile[0, first + h] = total[h][: levels // 2]
                tile[1, first + h] = total[h][levels // 2 :]
            return carry

        lax.fori_loop(0, ROWS // 2, row_pair, 0, unroll=3)

    order = [(ry, rx) for ry in (other_y, y) for rx in (across, right, left, x)]
    ring = ((across, to_across), (right, to_right), (left, to_left))
    origins = (left, right, across)
    core_sends = []
    to_ring = [[], []]
    to_pair = []
    to_own = []

    def produce(number):
        contract(share(*order[number]))

    def send_core(number):
        rows = pl.ds(share(*order[number]), ROWS)
        core_sends.append(remote(tile.at[1 - lev, rows], core_in.at[rows], to_core))

    def settle(number):
        core_sends[number].wait_recv()
        rows = pl.ds(share(*order[number]), ROWS)
        add(rows, core_in.at[rows])
        half, place = number // 4, number % 4
        if place < 3:
            rx, device = ring[place]
            to_ring[half].append(
                remote(sums.at[x_rows(*order[number])], x_in.at[half, place], device)
            )
        if half == 0:
            rx = order[number][1]
            to_pair.append(remote(sums.at[y_rows(other_y, rx)], pair_y_in.at[place], to_y))

    def settle_pair(place):
        to_pair[place].wait_recv()
        rx = order[place][1]
        add(y_rows(y, rx), pair_y_in.at[place])
        if place < 3:
            to_own.append(remote(sums.at[y_rows(y, rx)], y_in.at[place], ring[place][1]))

    for copy in small_in:
        copy.wait()
    for ref in (cells, misfit):
        ref[0] = jnp.zeros(ref.shape[1:], F32)
        ref[GROWN - 1] = jnp.zeros(ref.shape[1:], F32)
    for row in (1, GROWN - 2):
        field_b[row] = jnp.zeros(field_b.shape[1:], F32)
    for lev_at in range(lev_dev):
        sigma[lev_at : lev_at + 1, :] = jnp.full((1, 256), std_ref[lev_at], F32)
    for j in range(3):
        weights[j, GROWN - 1] = jnp.zeros((8, 128), F32)
    col = lax.broadcasted_iota(jnp.int32, (128, 256), 0)
    col_at, col_w = col_index_ref[...], col_weight_ref[...]
    matrix = jnp.where(col == col_at, 1.0 - col_w, jnp.where(col == col_at + 1, col_w, 0.0))
    hi, lo = halves(matrix)
    col_mat[0], col_mat[1] = hi, lo

    count_load.wait()
    widen(0)
    amp_in[0].wait()
    produce(0)
    pl.semaphore_wait(barrier, 7)
    send_core(0)
    amp_in[1].wait()
    produce(1)
    send_core(1)
    produce(2)
    send_core(2)
    settle(0)
    produce(3)
    send_core(3)
    settle(1)
    settle(2)

    for copy in plane_in[0]:
        copy.wait()

    def load_rows(i, carry):
        for side in range(2):
            field_a[EDGE + i, :, lanes[side]] = planes(planes_in, 0, side)[
                pl.ds(i, lev_dev, stride=own), :
            ]
        sub = lax.broadcasted_iota(jnp.int32, (8, 256), 0)
        weight = jnp.full((8, 256), row_weight_ref[i], F32)
        index = jnp.full((8, 256), row_index_ref[i], jnp.int32)
        upper = (index == (first_row + i) // 2).astype(F32)
        spread = jnp.broadcast_to(spread_ref[pl.ds(i, 1), :], (8, 256))
        land = jnp.broadcast_to(land_ref[pl.ds(i, 1), :], (8, 256)).astype(F32)
        cells[EDGE + i] = jnp.where(
            sub == 0, spread, jnp.where(sub == 1, land, jnp.where(sub == 2, weight, upper))
        )
        return carry

    lax.fori_loop(0, own, load_rows, 0, unroll=8)
    top, bottom = pl.ds(EDGE, HALO), pl.ds(EDGE + own - HALO, HALO)
    low, high = pl.ds(EDGE - HALO, HALO), pl.ds(EDGE + own, HALO)
    halo_sends = [
        remote(ref.at[src], ref.at[dst], device)
        for ref in (cells, field_a)
        for src, dst, device in ((top, high, to_before), (bottom, low, to_after))
    ]
    settle(3)

    widen(1)
    amp_in[2].wait()
    produce(4)
    send_core(4)
    amp_in[3].wait()
    produce(5)
    send_core(5)
    settle(4)
    settle_pair(0)
    produce(6)
    send_core(6)
    settle(5)
    produce(7)
    send_core(7)
    settle(6)
    settle_pair(1)
    for copy in to_ring[0]:
        copy.wait_recv()
    add(x_rows(other_y, x), x_in.at[0, 0], x_in.at[0, 1], x_in.at[0, 2])
    pair_x = remote(sums.at[x_rows(other_y, x)], pair_x_in, to_y)

    for copy in halo_sends[:2]:
        copy.wait_recv()

    def coefficients(e, carry):
        here, there = cells[e], cells[e + 1]
        line = first_row - EDGE + e
        inside = (line >= 0) & (line < rows_all) & (e >= 1) & (e <= GROWN - 2)
        facing = (line >= 0) & (line + 1 < rows_all)
        inside = jnp.where(inside, 1.0, 0.0).astype(F32)
        facing = jnp.where(facing, 1.0, 0.0).astype(F32)
        lane = lax.broadcasted_iota(jnp.int32, (8, 256), 1)
        spread, land = (jnp.broadcast_to(here[j : j + 1], (8, 256)) for j in (0, 1))
        spread_next, land_next = (jnp.broadcast_to(there[j : j + 1], (8, 256)) for j in (0, 1))
        row_face = (
            jnp.sqrt(spread * spread_next) * (1.0 - 0.5 * jnp.abs(land - land_next)) * facing
        )
        row_faces[e] = row_face
        spread_right, land_right = (pltpu.roll(v, 255, 1) for v in (spread, land))
        col_face = jnp.where(
            lane < 255,
            jnp.sqrt(spread * spread_right) * (1.0 - 0.5 * jnp.abs(land - land_right)),
            0.0,
        )
        col_before = pltpu.roll(col_face, 1, 1)
        col_faces[0, e] = col_face
        col_faces[1, e] = col_before
        centre[e] = 1.0 - (row_face + col_face + col_before)
        weight, upper = (jnp.broadcast_to(here[j : j + 1, :128], (8, 128)) for j in (2, 3))
        upper_on = upper > 0.5
        weights[0, e] = jnp.where(upper_on, 0.0, 1.0 - weight) * inside
        weights[1, e] = jnp.where(upper_on, 1.0 - weight, weight) * inside
        weights[2, e] = jnp.where(upper_on, weight, 0.0) * inside
        return carry

    lax.fori_loop(0, 15, coefficients, 0, unroll=5)
    settle_pair(2)
    lax.fori_loop(15, GROWN - 1, coefficients, 0, unroll=4)
    inner = pl.ds(1, GROWN - 2)
    centre[inner] = centre[inner] - row_faces[pl.ds(0, GROWN - 2)]
    def sweep(src, dst, first=0, last=7):
        def rows_of_four(step, carry):
            e = EDGE - 2 + 4 * step
            at_four = pl.ds(e, 4)
            down = row_faces[pl.ds(e - 1, 5)]
            to_right_face, to_left_face = col_faces[0, at_four], col_faces[1, at_four]
            keep = centre[at_four]
            for tile_at in range(lev_dev // 8):
                at = pl.ds(8 * tile_at, 8)
                v = src[pl.ds(e - 1, 6), at, :]
                mid = v[1:5]
                dst[at_four, at, :] = (
                    keep * mid
                    + (down[1:] * v[2:] + down[:-1] * v[:-2])
                    + to_right_face * pltpu.roll(mid, 255, 2)
                    + to_left_face * pltpu.roll(mid, 1, 2)
                )
            return carry

        lax.fori_loop(first, last, rows_of_four, 0)

    settle(7)
    for copy in halo_sends[2:]:
        copy.wait_recv()
        copy.wait_send()
    sweep(field_a, field_b)
    sweep(field_b, field_a)
    settle_pair(3)
    for copy in to_ring[1]:
        copy.wait_recv()
    add(x_rows(y, x), x_in.at[1, 0], x_in.at[1, 1], x_in.at[1, 2])
    sweep(field_a, field_b)

    def static_part(i, carry):
        for side in range(2):
            cols = lanes[side]
            misfit[EDGE + i, :, cols] = (
                sigma[:, cols] * field_b[EDGE + i, :, cols]
                - planes(planes_in, 1, side)[pl.ds(i, lev_dev, stride=own), :]
            )
        return carry

    for copy in plane_in[1]:
        copy.wait()
    lax.fori_loop(0, own, static_part, 0, unroll=8)
    halo_again = [
        remote(misfit.at[top], misfit.at[high], to_before),
        remote(misfit.at[bottom], misfit.at[low], to_after),
    ]

    for copy in to_own:
        copy.wait_recv()
    mine = share(y, x)
    window[pl.ds(HALO + XROWS, YROWS)] = sums[y_rows(y, x)] + y_in[0] + (y_in[1] + y_in[2])
    pair_x.wait_recv()
    window[pl.ds(HALO, XROWS)] = sums[x_rows(y, x)] + pair_x_in[...]
    halo_again += [
        remote(window.at[pl.ds(ROWS, HALO)], window.at[pl.ds(0, HALO)], to_after),
        remote(window.at[pl.ds(HALO, HALO)], window.at[pl.ds(HALO + ROWS, HALO)], to_before),
    ]

    def dot_split(lhs, which):
        hi, lo = halves(lhs)
        c_hi, c_lo = col_mat[0], col_mat[1]
        dims = (((1,), (which,)), ((), ()))
        dot = functools.partial(lax.dot_general, dimension_numbers=dims, preferred_element_type=F32)
        return dot(hi, c_hi) + (dot(lo, c_hi) + dot(hi, c_lo))

    span = 8

    def interpolate(step, carry):
        e0 = step * span
        lines = []
        for pair in range(span // 2):
            t = step * (span // 2) + pair + 1
            w = [window[t + d].reshape(lev_dev // 8, 8, 128) for d in (-1, 0, 1)]
            for h in range(2):
                e = e0 + 2 * pair + h
                line = weights[0, e] * w[0] + weights[1, e] * w[1] + weights[2, e] * w[2]
                lines.append(line.reshape(lev_dev, 128))
        fine_part = dot_split(jnp.concatenate(lines, axis=0), 0)
        at = pl.ds(e0, span)
        total = misfit[at] + fine_part.reshape(span, lev_dev, 256)
        misfit[at] = total
        field_a[at] = sigma[...] * total
        back[at] = dot_split(total.reshape(span * lev_dev, 256), 1).reshape(span, lev_dev, 128)
        return carry

    lax.fori_loop(1, 3, interpolate, 0, unroll=2)
    for copy in halo_again:
        copy.wait_recv()
    for copy in halo_again[:2]:
        copy.wait_send()
    interpolate(0, 0)
    interpolate(3, 0)

    def adjoint(r, carry):
        e = 2 * r + 2
        total = jnp.zeros((lev_dev // 8, 8, 128), F32)
        for j in range(6):
            total = total + weights[2 - j // 2, e + j] * back[e + j].reshape(lev_dev // 8, 8, 128)
        shares[lev, mine + r] = total.reshape(lev_dev, 128)
        return carry

    lax.fori_loop(0, ROWS, adjoint, 0, unroll=12)

    def to_all(rows, device):
        return remote(shares.at[lev, rows], shares.at[lev, rows], device)

    def to_ring_of(rows):
        return [to_all(rows, device) for device in (to_right, to_left, to_across)]

    pair_first = to_all(x_rows(y, x), to_y)
    ring_y = to_ring_of(y_rows(y, x))
    pair_y = [to_all(y_rows(y, x), to_y)]
    ring_own = to_ring_of(x_rows(y, x))
    core = [to_all(pl.ds(mine, ROWS), to_core)]

    dones = done.reshape(members * modes * HALF_PITCH, 128)

    def project(rx):
        def row_pair(step, carry):
            row = rx * ROWS + step * 2
            project_row_pair(
                back_lhs,
                count_ref,
                amps,
                perts,
                dones,
                shares,
                (members, modes, levels),
                y * half_rows + row,
                row,
            )
            return carry

        lax.fori_loop(0, ROWS // 2, row_pair, 0, unroll=3)

    core_y, core_x = [], []

    def share_y(number):
        ring_y[number].wait_recv()
        rows = y_rows(y, origins[number])
        pair_y.append(to_all(rows, to_y))
        core_y.append(to_all(rows, to_core))

    def share_x(number):
        ring_own[number].wait_recv()
        core_x.append(to_all(x_rows(y, origins[number]), to_core))

    def pass_on(number):
        pair_y[number].wait_recv()
        core.append(to_all(y_rows(other_y, (x, *origins)[number]), to_core))

    def project_origin(number):
        core_x[number].wait_recv()
        core_y[number].wait_recv()
        project(origins[number])

    sweep(field_a, field_b)
    core[0].wait_recv()
    project(x)
    sweep(field_b, field_a)
    pair_first.wait_recv()
    ring_other = to_ring_of(x_rows(other_y, x))
    core.append(to_all(x_rows(other_y, x), to_core))
    share_y(0)
    share_y(1)
    sweep(field_a, field_b)

    def finish(i, carry):
        at = pl.ds(i, lev_dev, stride=own)
        for side in range(2):
            for number, value in ((0, field_b), (1, misfit)):
                planes(planes_out, number, side)[at, :] = (
                    planes(planes_in, number, side)[at, :] + value[EDGE + i, :, lanes[side]]
                )
        return carry

    lax.fori_loop(0, own, finish, 0, unroll=8)
    share_y(2)
    share_x(0)
    share_x(1)
    pass_on(0)
    project_origin(0)
    share_x(2)
    pass_on(1)
    project_origin(1)
    pass_on(2)
    pass_on(3)
    for copy, rx in zip(ring_other, origins):
        copy.wait_recv()
        core.append(to_all(x_rows(other_y, rx), to_core))
    project_origin(2)
    for copy in core[1:]:
        copy.wait_recv()
    waited = halo_sends[2:] + halo_again[:2]
    for copy in sent:
        if not any(copy is done for done in waited):
            copy.wait_send()


def exchange(sizes, modes_t, count, amp, pert, control, innov, std, spread, land, row_index, row_weight, col_index, col_weight):
    members, modes, rows, cols = amp.shape
    levels = pert.shape[1]
    lev_dev, own, cols_fine = control.shape
    vmem = pl.BlockSpec(memory_space=pltpu.VMEM)
    anywhere = pl.BlockSpec(memory_space=pl.ANY)
    cell = (lev_dev, 128)
    row = (lev_dev, cols_fine)
    tile = (2, rows) + cell
    return pl.pallas_call(
        functools.partial(exchange_kernel, sizes),
        in_specs=[anywhere] * 13,
        out_specs=[vmem] * 7,
        out_shape=[
            pltpu.VMEM((members, modes, PITCH, cols), F32),
            pltpu.VMEM((members, levels, PITCH, cols), F32),
            pltpu.VMEM(tile, F32),
            pltpu.VMEM((2, 2, lev_dev, own, 128), F32),
            pltpu.VMEM(count.shape, jnp.int32),
            pltpu.VMEM((modes, 3 * levels), BF16),
            pltpu.VMEM((members, modes, HALF_PITCH, cols), F32),
        ],
        scratch_shapes=[
            pltpu.VMEM(modes_t.shape, F32),
            pltpu.VMEM(tile, F32),
            pltpu.VMEM(pert.shape, BF16),
            pltpu.VMEM((rows,) + cell, F32),
            pltpu.VMEM((2, 3, XROWS) + cell, F32),
            pltpu.VMEM((XROWS,) + cell, F32),
            pltpu.VMEM((4, YROWS) + cell, F32),
            pltpu.VMEM((3, YROWS) + cell, F32),
            pltpu.VMEM((ROWS + 2 * HALO,) + cell, F32),
            pltpu.VMEM((GROWN,) + row, F32),
            pltpu.VMEM((GROWN,) + row, F32),
            pltpu.VMEM((GROWN,) + row, F32),
            pltpu.VMEM((GROWN, 8, cols_fine), F32),
            pltpu.VMEM((GROWN, 8, cols_fine), F32),
            pltpu.VMEM((2, GROWN, 8, cols_fine), F32),
            pltpu.VMEM((GROWN, 8, cols_fine), F32),
            pltpu.VMEM((3, GROWN, 8, 128), F32),
            pltpu.VMEM(row, F32),
            pltpu.VMEM((2, 128, cols_fine), BF16),
            pltpu.VMEM((GROWN,) + cell, F32),
            pltpu.VMEM((2, 2, lev_dev, own, 128), F32),
            pltpu.SMEM(std.shape, F32),
            pltpu.VMEM(spread.shape, F32),
            pltpu.VMEM(land.shape, jnp.int32),
            pltpu.SMEM(row_index.shape, jnp.int32),
            pltpu.SMEM(row_weight.shape, F32),
            pltpu.VMEM((1, cols_fine), jnp.int32),
            pltpu.VMEM((1, cols_fine), F32),
            pltpu.SemaphoreType.DMA((80,)),
            pltpu.SemaphoreType.DMA((80,)),
            pltpu.SemaphoreType.DMA((2 * members + 4,)),
            pltpu.SemaphoreType.DMA((4,)),
            pltpu.SemaphoreType.DMA((9,)),
        ],
        compiler_params=pltpu.CompilerParams(
            collective_id=0, has_side_effects=True, vmem_limit_bytes=18 << 20
        ),
        name="exchange",
    )(
        *(
            pltpu.with_memory_space_constraint(operand, pltpu.HBM)
            for operand in (
                modes_t,
                count,
                amp,
                pert,
                control,
                innov,
                std,
                spread,
                land,
                row_index,
                row_weight,
                col_index.reshape(1, cols_fine),
                col_weight.reshape(1, cols_fine),
            )
        ),
    )


def local(
    ens_pert,
    ens_control,
    eigen_modes,
    mode_count,
    row_index,
    row_weight,
    col_index,
    col_weight,
    static_control,
    static_std,
    diffusivity,
    land_mask,
    innovation,
):
    sizes = (
        lax.axis_size("coarse"),
        lax.axis_size("fine"),
        lax.axis_size("coarse") * lax.axis_size("fine") * row_index.shape[0],
    )
    amp, wide, coarse_grad, planes, count, back_lhs, done = exchange(
        sizes,
        eigen_modes.T,
        mode_count,
        ens_control,
        ens_pert,
        static_control,
        innovation,
        static_std,
        diffusivity,
        land_mask,
        row_index,
        row_weight,
        col_index,
        col_weight,
    )
    grad_ens, grad_static, increment = backward(
        back_lhs, count, amp, wide, coarse_grad, planes, done, mode_count.shape[0]
    )
    return increment, grad_static, grad_ens


def solution(mesh):
    in_specs = (
        P(("fine", "lev"), None, "coarse", None),
        P(("fine", "lev"), None, "coarse", None),
        P(),
        P("coarse", None),
        P(("coarse", "fine")),
        P(("coarse", "fine")),
        P(),
        P(),
        P("lev", ("coarse", "fine"), None),
        P("lev"),
        P(("coarse", "fine"), None),
        P(("coarse", "fine"), None),
        P("lev", ("coarse", "fine"), None),
    )
    out_specs = (
        P("lev", ("coarse", "fine"), None),
        P("lev", ("coarse", "fine"), None),
        P(("fine", "lev"), None, "coarse", None),
    )
    return jax.shard_map(local, mesh=mesh, in_specs=in_specs, out_specs=out_specs, check_vma=False)
```
